32 devices in a mesh: wide: 4 (over x, core), narrow: 8 (over z, y).
Axes of the slice: x: 2, y: 2, z: 4, core: 2. Of those that a mesh axis runs over, the one named last changes fastest.
Arguments:
- tokens: bfloat16 [8192, 1280], P(('wide', 'narrow')), may hold values from -6 to 6
- routes: int32 [8192, 7], P(('wide', 'narrow')), may hold values from 0 to 15, all different within a row; in each aligned block of 256 rows (0 to 255, 256 to 511, ...) at most 168 rows name the same one
- gates: float32 [8192, 7], P(('wide', 'narrow')), may hold values from 0.06 to 0.24
- attn_gain: bfloat16 [1280], replicated, may hold values from 0.5 to 1.5
- query_weight: bfloat16 [1280, 1280], replicated, may hold values from -0.15625 to 0.15625
- key_weight: bfloat16 [1280, 1280], replicated, may hold values from -0.15625 to 0.15625
- value_weight: bfloat16 [1280, 1280], replicated, may hold values from -0.15625 to 0.15625
- output_weight: bfloat16 [1280, 1280], replicated, may hold values from -1.25 to 1.25
- ffn_gain: bfloat16 [1280], replicated, may hold values from 0.5 to 1.5
- shared_gate: bfloat16 [1280, 896], replicated, may hold values from -0.15625 to 0.15625
- shared_up: bfloat16 [1280, 896], replicated, may hold values from -0.15625 to 0.15625
- shared_down: bfloat16 [896, 1280], replicated, may hold values from -0.1875 to 0.1875
- expert_gate: bfloat16 [16, 1280, 896], P('narrow'), may hold values from -0.15625 to 0.15625
- expert_up: bfloat16 [16, 1280, 896], P('narrow'), may hold values from -0.15625 to 0.15625
- expert_down: bfloat16 [16, 896, 1280], P('narrow'), may hold values from -0.1875 to 0.1875
- cotangent: bfloat16 [8192, 1280], P(('wide', 'narrow')), may hold values from -6 to 6
Outputs:
- mixed: bfloat16 [8192, 1280], P(('wide', 'narrow'))
- tokens_grad: float32 [8192, 1280], P(('wide', 'narrow'))
- attn_gain_grad: float32 [1280], P(('wide', 'narrow'))
- query_weight_grad: float32 [1280, 1280], P(('wide', 'narrow'))
- key_weight_grad: float32 [1280, 1280], P(('wide', 'narrow'))
- value_weight_grad: float32 [1280, 1280], P(('wide', 'narrow'))
- output_weight_grad: float32 [1280, 1280], P(('wide', 'narrow'))
- ffn_gain_grad: float32 [1280], P(('wide', 'narrow'))
- shared_gate_grad: float32 [1280, 896], P(('wide', 'narrow'))
- shared_up_grad: float32 [1280, 896], P(('wide', 'narrow'))
- shared_down_grad: float32 [896, 1280], P(('wide', 'narrow'))
- expert_gate_grad: float32 [16, 1280, 896], P('narrow', 'wide')
- expert_up_grad: float32 [16, 1280, 896], P('narrow', 'wide')
- expert_down_grad: float32 [16, 896, 1280], P('narrow', 'wide')
The draws below stay inside these ranges and needn't reach their ends.
Inputs may be any that keep to these rules, and one draw needn't show every extreme that they name: `routes`: each row names 7 different experts. Within each aligned block of 256 rows no expert is named by more than 168 rows, and in some block one expert is named by exactly 168.
All inputs are finite; a program needn't handle non-finite values.
Results may differ from the reference program's by a relative error of at most 0.017.
Values may be sent and summed in bfloat16 or wider, within the bound.
No kernel may reach another device: no remote copies, remote signals or barrier semaphores. Data moves between devices by JAX's collectives and lax.ppermute only.
A program may use at most 320 MiB of HBM per device.

```python
import math
import jax
import jax.numpy as jnp
import numpy as np
from jax import lax

D = 1280
HEADS = 10
HEAD_DIM = 128
FF = 896
TOP = 7
TOK_DEV = 256
SEQ = 2048
EXPERTS = 16
TOKENS = 8192
CAP = 168


def block_levels(key, dims, shards, smallest, top_value):
    def one(position, parts):
        draws = jax.random.uniform(jax.random.fold_in(jax.random.fold_in(key, 6), position), (parts,), jnp.float32, smallest / len(shards), top_value / len(shards))
        return jnp.repeat(jnp.exp(draws), dims[position] // parts).reshape((-1,) + (1,) * (len(dims) - position - 1))

    loudness = one(*shards[0])
    for cut in shards[1:]:
        loudness = loudness * one(*cut)
    return loudness


def assign_block(stream_key, own, number, rows, count, top, limit, lean):
    order = jax.random.permutation(stream_key, count)
    crowded, usual = shares(count, rows * top, limit, lean, True), shares(count, rows * top, limit, lean, False)
    places = jnp.arange(count)

    def named(lengths, offset_by):
        used = int((lengths > 0).sum())
        fixed = max(1, used // 4)
        shifted = fixed + (places - fixed + offset_by * (used - fixed)) % max(1, count - fixed)
        return jnp.zeros((count,), jnp.int32).at[order[jnp.where(places < fixed, places, shifted)]].set(jnp.asarray(lengths, jnp.int32))

    lengths = jnp.where(number % 4 == 0, named(crowded, number // 4), named(usual, number - number // 4 - 1))
    mixed = jax.random.permutation(jax.random.fold_in(own, 3), count)
    giver, taker = mixed[0:count // 2 * 2:2], mixed[1:count // 2 * 2:2]
    room = jnp.minimum(lengths[giver] - 1, limit - lengths[taker]) // 2
    room = jnp.where((giver == order[0]) | (taker == order[0]) | (lengths[taker] == 0), 0, jnp.maximum(room, 0))
    shifted = jax.random.randint(jax.random.fold_in(own, 4), (count // 2,), 0, 1 << 20) % (room + 1)
    lengths = lengths.at[giver].add(-shifted).at[taker].add(shifted)
    labels = jnp.searchsorted(jnp.cumsum(lengths), jnp.arange(rows * top), side="right").astype(jnp.int32)
    table = labels.reshape(top, rows).T
    table = table[jax.random.permutation(jax.random.fold_in(own, 1), rows)]
    offset_by = jax.random.randint(jax.random.fold_in(own, 2), (rows, 1), 0, top)
    return jnp.take_along_axis(table, (jnp.arange(top)[None, :] + offset_by) % top, axis=1)


def shares(count, total, reach, lean, full):
    portions = [(1 << 20) // math.isqrt(grade ** lean) + 1 for grade in range(1, count + 1)]
    largest = reach if full else min(reach, max(-(-total // count), total * portions[0] // sum(portions)))
    least = 1 if total - largest >= count - 1 else 0
    counts, surplus = [largest] + [least] * (count - 1), total - largest - least * (count - 1)
    while surplus > 0:
        free = [i for i in range(1, count) if counts[i] < largest] or [i for i in range(1, count) if counts[i] < reach]
        mass, remaining = sum([portions[i] for i in free]), surplus
        for i in free:
            addition = min(reach - counts[i], max(1, remaining * portions[i] // mass), surplus)
            counts[i] = counts[i] + addition
            surplus = surplus - addition
    return np.array(counts)


def scatter_about(stream_key, shape, scale, reach, cuts=(), kind=jnp.bfloat16):
    drawn = jax.random.normal(stream_key, shape, jnp.float32) * scale
    if len(cuts) > 0:
        drawn = block_levels(stream_key, shape, cuts, -0.22, 0.18) * drawn
    return jnp.clip(drawn, min=-reach, max=reach).astype(kind)


def setup_inputs(seed: int = 0) -> dict:
    seeds = jax.random.split(jax.random.key(seed), 17)
    tokens = scatter_about(seeds[0], (TOKENS, D), 1.0, 6.0, ((0, 32),))
    routes_keys = jax.random.split(jax.random.fold_in(seeds[1], 1), TOKENS // TOK_DEV)
    routes_turns = jax.random.permutation(jax.random.fold_in(seeds[1], 3), TOKENS // TOK_DEV)
    routes = jax.vmap(lambda own, number: assign_block(jax.random.fold_in(seeds[1], 2), own, number, TOK_DEV, EXPERTS, TOP, CAP, 1))(routes_keys, routes_turns).reshape((TOKENS, TOP))
    gates = jnp.clip(0.06 + 0.179999996 * jax.random.uniform(seeds[2], (TOKENS, TOP), jnp.float32) ** block_levels(seeds[2], (TOKENS, TOP), ((0, 32),), -0.2, 0.2), 0.06, 0.24)
    attn_gain = jnp.clip(1.0 + 0.1 * jax.random.normal(seeds[3], (D,), jnp.float32), 0.5, 1.5).astype(jnp.bfloat16)
    query_weight = scatter_about(seeds[4], (D, D), D ** -0.5, 0.15625)
    key_weight = scatter_about(seeds[5], (D, D), D ** -0.5, 0.15625)
    value_weight = scatter_about(seeds[6], (D, D), D ** -0.5, 0.15625)
    output_weight = scatter_about(seeds[7], (D, D), (D // 64) ** -0.5, 1.25)
    ffn_gain = jnp.clip(1.0 + 0.1 * jax.random.normal(seeds[8], (D,), jnp.float32), 0.5, 1.5).astype(jnp.bfloat16)
    shared_gate = scatter_about(seeds[9], (D, FF), D ** -0.5, 0.15625)
    shared_up = scatter_about(seeds[10], (D, FF), D ** -0.5, 0.15625)
    shared_down = scatter_about(seeds[11], (FF, D), FF ** -0.5, 0.1875)
    expert_gate = scatter_about(seeds[12], (EXPERTS, D, FF), D ** -0.5, 0.15625, ((0, 8),))
    expert_up = scatter_about(seeds[13], (EXPERTS, D, FF), D ** -0.5, 0.15625, ((0, 8),))
    expert_down = scatter_about(seeds[14], (EXPERTS, FF, D), FF ** -0.5, 0.1875, ((0, 8),))
    cotangent = scatter_about(seeds[15], (TOKENS, D), 1.0, 6.0, ((0, 32),))
    return dict(tokens=tokens, routes=routes, gates=gates, attn_gain=attn_gain, query_weight=query_weight, key_weight=key_weight, value_weight=value_weight, output_weight=output_weight, ffn_gain=ffn_gain, shared_gate=shared_gate, shared_up=shared_up, shared_down=shared_down, expert_gate=expert_gate, expert_up=expert_up, expert_down=expert_down, cotangent=cotangent)


EPS = 1e-06
HIGH = lax.Precision.HIGHEST

@jax.custom_vjp
def low(v):
    return lax.optimization_barrier(v.astype(jnp.bfloat16)).astype(jnp.float32)

@jax.custom_vjp
def low_back(v):
    return v

def low_keep(v):
    return (low(v), None)

def low_pass(kept, grad):
    return (grad,)

def back_keep(v):
    return (v, None)

def back_low(kept, grad):
    return (low(grad),)
low.defvjp(low_keep, low_pass)
low_back.defvjp(back_keep, back_low)

def norm_rows(values, gain):
    return values * lax.rsqrt(lax.optimization_barrier(jnp.mean(values * values, axis=-1, keepdims=True)) + EPS) * gain

def rope_tables(length, width):
    half = width // 2
    freq = 10000.0 ** (-(jnp.arange(half, dtype=jnp.float32) * 2.0) / width)
    angles = jnp.arange(length, dtype=jnp.float32)[:, None] * freq[None, :]
    return (jnp.cos(angles)[:, None, :], jnp.sin(angles)[:, None, :])

def rotate(values, cosine_table, sine_table):
    half = values.shape[-1] // 2
    first = values[..., :half]
    second = values[..., half:]
    return jnp.concatenate([first * cosine_table - second * sine_table, second * cosine_table + first * sine_table], axis=-1)

def swiglu(rows, gate_w, up_w, down_w, form_in, form_out):
    gate_pre = low_back(jnp.einsum(form_in, rows, gate_w, precision=HIGH))
    up_pre = low_back(jnp.einsum(form_in, rows, up_w, precision=HIGH))
    inner_act = low(jax.nn.silu(gate_pre) * up_pre)
    return jnp.einsum(form_out, inner_act, down_w, precision=HIGH)

def moe_block(ffn_block, route_rows, gate_rows, expert_gate, expert_up, expert_down):
    picked = route_rows[:, :, None] == jnp.arange(EXPERTS, dtype=jnp.int32)[None, None, :]
    member = lax.optimization_barrier(jnp.sum(picked.astype(jnp.int32), axis=1))
    token_gate = lax.optimization_barrier(jnp.sum(jnp.where(picked, gate_rows[:, :, None], 0.0), axis=1))
    rank = jnp.cumsum(member, axis=0) - 1
    slot_ids = jnp.arange(CAP, dtype=jnp.int32)
    hit = (member.T[:, None, :] == 1) & (rank.T[:, None, :] == slot_ids[None, :, None])
    positions = jnp.arange(TOK_DEV, dtype=jnp.int32)
    slot_token = lax.optimization_barrier(jnp.sum(jnp.where(hit, positions[None, None, :], 0), axis=2)).astype(jnp.int32)
    slot_gate = lax.optimization_barrier(jnp.sum(jnp.where(hit, token_gate.T[:, None, :], 0.0), axis=2))
    slot_rows = low_back(jnp.take(ffn_block, slot_token.reshape(-1), axis=0).reshape(EXPERTS, CAP, D))
    routed_out = low(low_back(swiglu(slot_rows, expert_gate, expert_up, expert_down, 'ecd,edf->ecf', 'ecf,efd->ecd')))
    return jnp.zeros((TOK_DEV, D), ffn_block.dtype).at[slot_token.reshape(-1)].add((slot_gate[:, :, None] * routed_out).reshape(-1, D))

def block_forward(weights, rows, route_rows, gate_rows):
    attn_gain, query_weight, key_weight, value_weight, output_weight, ffn_gain, shared_gate, shared_up, shared_down, expert_gate, expert_up, expert_down = weights
    attn_in = low(norm_rows(rows, attn_gain))
    cosine_table, sine_table = rope_tables(SEQ, HEAD_DIM)
    query_lin = low_back(jnp.dot(attn_in, query_weight, precision=HIGH)).reshape(SEQ, HEADS, HEAD_DIM)
    key_lin = low_back(jnp.dot(attn_in, key_weight, precision=HIGH)).reshape(SEQ, HEADS, HEAD_DIM)
    values = low(low_back(jnp.dot(attn_in, value_weight, precision=HIGH))).reshape(SEQ, HEADS, HEAD_DIM)
    queries = low(rotate(query_lin, cosine_table, sine_table))
    key_rot = low(rotate(key_lin, cosine_table, sine_table))
    causal = jnp.arange(SEQ, dtype=jnp.int32)[:, None] >= jnp.arange(SEQ, dtype=jnp.int32)[None, :]
    scores = low_back(jnp.einsum('qhd,khd->hqk', queries, key_rot, precision=HIGH) * HEAD_DIM ** (-0.5))
    scores = jnp.where(causal[None], scores, -1e+30)
    prob_low = low(jax.nn.softmax(scores, axis=-1))
    attended = low(low_back(jnp.einsum('hqk,khd->qhd', prob_low, values, precision=HIGH))).reshape(SEQ, D)
    hidden = rows + low_back(jnp.dot(attended, output_weight, precision=HIGH))
    ffn_in = low(norm_rows(hidden, ffn_gain))
    shared_out = low_back(swiglu(ffn_in, shared_gate, shared_up, shared_down, 'td,df->tf', 'tf,fd->td'))
    pieces = SEQ // TOK_DEV
    routed = jax.vmap(moe_block, in_axes=(0, 0, 0, None, None, None))(ffn_in.reshape(pieces, TOK_DEV, D), route_rows.reshape(pieces, TOK_DEV, TOP), gate_rows.reshape(pieces, TOK_DEV, TOP), expert_gate, expert_up, expert_down).reshape(SEQ, D)
    return hidden + shared_out + routed

def reference(tokens, routes, gates, attn_gain, query_weight, key_weight, value_weight, output_weight, ffn_gain, shared_gate, shared_up, shared_down, expert_gate, expert_up, expert_down, cotangent):
    weights = tuple((weight.astype(jnp.float32) for weight in (attn_gain, query_weight, key_weight, value_weight, output_weight, ffn_gain, shared_gate, shared_up, shared_down, expert_gate, expert_up, expert_down)))
    blocks = TOKENS // SEQ
    checked = jax.checkpoint(block_forward)

    def forward(inputs, params):

        def one_block(carry, pieces):
            return (carry, checked(params, pieces[0], pieces[1], pieces[2]))
        _, outputs = lax.scan(one_block, None, (inputs.reshape(blocks, SEQ, D), routes.reshape(blocks, SEQ, TOP), gates.astype(jnp.float32).reshape(blocks, SEQ, TOP)))
        return outputs.reshape(TOKENS, D)
    mixed, pullback = jax.vjp(forward, tokens.astype(jnp.float32), weights)
    tokens_grad, weight_grads = pullback(cotangent.astype(jnp.float32))
    return (mixed.astype(jnp.bfloat16), tokens_grad, weight_grads[0], weight_grads[1], weight_grads[2], weight_grads[3], weight_grads[4], weight_grads[5], weight_grads[6], weight_grads[7], weight_grads[8], weight_grads[9], weight_grads[10], weight_grads[11])
```

```python
import jax
import jax.numpy as jnp
from jax import lax
from jax.sharding import PartitionSpec as P

HEAD_DIM = 128
EPS = 1e-06
FLOAT = jnp.float32
HALF = jnp.bfloat16


def matmul(a, b, contract):
    return lax.dot_general(a, b, ((contract[:1], contract[1:]), ((), ())), preferred_element_type=FLOAT)


def rotate(values, cosine, sine):
    half = values.shape[-1] // 2
    first = values[..., :half]
    second = values[..., half:]
    return jnp.concatenate(
        [first * cosine - second * sine, second * cosine + first * sine], axis=-1
    )


def ring_order(count):
    return list(range(0, count, 2)) + list(range(count - 1, 0, -2))


def ring_steps(count):
    order = ring_order(count)
    ahead = [(order[i], order[(i + 1) % count]) for i in range(count)]
    back = [(b, a) for a, b in ahead]
    return ahead, back


def ring_gather(block):
    count = lax.axis_size("narrow")
    ahead, back = ring_steps(count)
    slots = [None] * count
    slots[0] = block
    forward = backward = block
    for step in range(1, count // 2 + 1):
        forward = lax.ppermute(forward, "narrow", ahead)
        slots[count - step] = forward
        if step < count // 2:
            backward = lax.ppermute(backward, "narrow", back)
            slots[step] = backward
    return slots


def ring_scatter(parts):
    count = lax.axis_size("narrow")
    ahead, back = ring_steps(count)
    half = count // 2
    forward = parts[half].astype(HALF)
    backward = parts[half + 1].astype(HALF)
    for step in range(1, half + 1):
        forward = lax.ppermute(forward, "narrow", ahead).astype(FLOAT)
        if step < half:
            forward = (forward + parts[half - step].astype(FLOAT)).astype(HALF)
            backward = lax.ppermute(backward, "narrow", back).astype(FLOAT)
            if step < half - 1:
                backward = (backward + parts[half + 1 + step].astype(FLOAT)).astype(HALF)
    return parts[0].astype(FLOAT) + forward + backward


def wide_scatter(chunks):
    count = lax.axis_size("wide")
    place = lax.axis_index("wide")
    bit = 1
    while bit < count:
        pairs = chunks.reshape((chunks.shape[0] // 2, 2) + chunks.shape[1:])
        mine = (place // bit) % 2
        kept = lax.dynamic_index_in_dim(pairs, mine, axis=1, keepdims=False)
        sent = lax.dynamic_index_in_dim(pairs, 1 - mine, axis=1, keepdims=False)
        got = lax.ppermute(sent, "wide", [(i, i ^ bit) for i in range(count)])
        chunks = (kept.astype(FLOAT) + got.astype(FLOAT)).astype(HALF)
        bit *= 2
    return chunks[0]


def norm_back(grad_out, normed, inv_scale, gain):
    scaled = grad_out * gain
    return inv_scale * (scaled - normed * jnp.mean(scaled * normed, axis=1, keepdims=True))


def causal_attention(queries, keys, values, query_pos, key_pos):
    scores = jnp.einsum("qd,kd->qk", queries, keys, preferred_element_type=FLOAT)
    scores = jnp.where(
        query_pos[:, None] >= key_pos[None, :], scores * HEAD_DIM**-0.5, -1e30
    )
    peak = jnp.max(scores, axis=1, keepdims=True)
    shifted = jnp.exp(scores - peak)
    total = jnp.sum(shifted, axis=1, keepdims=True)
    low = (shifted / total).astype(HALF)
    out = matmul(low, values, (1, 0)).astype(HALF)
    return out, peak + jnp.log(total)


def causal_back(queries, keys, values, query_pos, key_pos, log_total, out_grad):
    scores = jnp.einsum("qd,kd->qk", queries, keys, preferred_element_type=FLOAT)
    scores = jnp.where(
        query_pos[:, None] >= key_pos[None, :], scores * HEAD_DIM**-0.5, -1e30
    )
    probs = jnp.exp(scores - log_total)
    prob_grad = matmul(out_grad, values, (1, 1))
    score_grad = (
        probs * (prob_grad - jnp.sum(prob_grad * probs, axis=1, keepdims=True))
    ).astype(HALF)
    value_grad = matmul(probs.astype(HALF), out_grad, (0, 0))
    query_grad = matmul(score_grad, keys, (1, 0)) * HEAD_DIM**-0.5
    key_grad = matmul(score_grad, queries, (0, 0)) * HEAD_DIM**-0.5
    return query_grad, key_grad, value_grad


def on_device(
    tokens,
    routes,
    gates,
    attn_gain,
    query_weight,
    key_weight,
    value_weight,
    output_weight,
    ffn_gain,
    shared_gate,
    shared_up,
    shared_down,
    expert_gate,
    expert_up,
    expert_down,
    cotangent,
):
    length, width = tokens.shape
    hidden_units = expert_gate.shape[2]
    local_experts = expert_gate.shape[0]
    group = lax.axis_size("narrow")
    copies = lax.axis_size("wide")
    place = lax.axis_index("narrow")
    experts = group * local_experts
    seq_len = length * group
    own_heads = group * HEAD_DIM
    spare_heads = width // HEAD_DIM - group

    order = jnp.asarray(ring_order(group), dtype=jnp.int32)
    ring_place = jnp.where(place % 2 == 0, place // 2, group - 1 - place // 2)
    slot_block = order[(ring_place + jnp.arange(group, dtype=jnp.int32)) % group]
    blocks = jnp.arange(group, dtype=jnp.int32)
    block_ring = jnp.where(blocks % 2 == 0, blocks // 2, group - 1 - blocks // 2)
    block_slot = (block_ring - ring_place) % group

    def by_slot(array):
        return jnp.take(array, slot_block, axis=0)

    def by_block(array):
        return jnp.take(array, block_slot, axis=0)

    inputs = tokens.astype(FLOAT)
    inv_one = lax.rsqrt(jnp.mean(inputs * inputs, axis=1, keepdims=True) + EPS)
    normed_one = inputs * inv_one
    attn_in = (normed_one * attn_gain).astype(HALF)
    attn_slots = ring_gather(attn_in)
    cot_slots = ring_gather(cotangent)

    expert_ids = jnp.arange(experts, dtype=jnp.int32)
    picked = routes[:, :, None] == expert_ids[None, None, :]
    token_gate = jnp.sum(jnp.where(picked, gates[:, :, None], 0.0), axis=1)
    all_gates = lax.all_gather(token_gate.T, "narrow", axis=0)
    own_gates = lax.dynamic_slice_in_dim(all_gates, place * local_experts, local_experts, axis=1)
    own_gates = by_slot(own_gates)

    def head_columns(weight):
        return lax.dynamic_slice_in_dim(weight, place * HEAD_DIM, HEAD_DIM, axis=1)

    own_weights = jnp.concatenate(
        [head_columns(query_weight), head_columns(key_weight), head_columns(value_weight)], axis=1
    )
    spare_weights = jnp.concatenate([key_weight[:, own_heads:], value_weight[:, own_heads:]], axis=1)
    spare_query_weight = query_weight[:, own_heads:]
    attn_all = jnp.concatenate(attn_slots, axis=0)
    positions = (
        slot_block[:, None] * length + jnp.arange(length, dtype=jnp.int32)[None, :]
    ).reshape(seq_len)
    half = HEAD_DIM // 2
    freq = 10000.0 ** (-(jnp.arange(half, dtype=FLOAT) * 2.0) / HEAD_DIM)
    angles = positions.astype(FLOAT)[:, None] * freq[None, :]
    cosine, sine = jnp.cos(angles), jnp.sin(angles)
    own_lin = matmul(attn_all, own_weights, (1, 0))
    spare_lin = matmul(attn_all, spare_weights, (1, 0))
    spare_query_lin = matmul(attn_in, spare_query_weight, (1, 0))

    heads = []
    own_q = rotate(own_lin[:, :HEAD_DIM], cosine, sine).astype(HALF)
    own_k = rotate(own_lin[:, HEAD_DIM : 2 * HEAD_DIM], cosine, sine).astype(HALF)
    own_v = own_lin[:, 2 * HEAD_DIM :].astype(HALF)
    heads.append((own_q, own_k, own_v, positions))
    for head in range(spare_heads):
        columns = slice(head * HEAD_DIM, (head + 1) * HEAD_DIM)
        value_columns = slice(
            (spare_heads + head) * HEAD_DIM, (spare_heads + head + 1) * HEAD_DIM
        )
        q = rotate(spare_query_lin[:, columns], cosine[:length], sine[:length]).astype(HALF)
        k = rotate(spare_lin[:, columns], cosine, sine).astype(HALF)
        v = spare_lin[:, value_columns].astype(HALF)
        heads.append((q, k, v, positions[:length]))
    outs = [causal_attention(q, k, v, pos, positions) for q, k, v, pos in heads]

    own_out = by_block(outs[0][0].reshape(group, length, HEAD_DIM))
    returned = lax.all_to_all(own_out, "narrow", split_axis=0, concat_axis=0, tiled=True)
    attended = jnp.concatenate(
        [returned.transpose(1, 0, 2).reshape(length, own_heads)] + [out for out, _ in outs[1:]],
        axis=1,
    )
    hidden = inputs + matmul(attended, output_weight, (1, 0))
    inv_two = lax.rsqrt(jnp.mean(hidden * hidden, axis=1, keepdims=True) + EPS)
    normed_two = hidden * inv_two
    ffn_in = (normed_two * ffn_gain).astype(HALF)

    share = hidden_units // (copies * group)
    taken = copies * share
    padded = -(-taken // 128) * 128
    column = jnp.arange(padded, dtype=jnp.int32)
    unit = jnp.where(
        column < taken, ((column // share) * group + place) * share + column % share, -1
    )
    choice = (jnp.arange(hidden_units, dtype=jnp.int32)[:, None] == unit[None, :]).astype(HALF)
    share_gate = matmul(shared_gate, choice, (1, 0)).astype(HALF)
    share_up = matmul(shared_up, choice, (1, 0)).astype(HALF)
    share_down = matmul(choice, shared_down, (0, 0)).astype(HALF)
    gate_weight = jnp.concatenate([expert_gate[e] for e in range(local_experts)] + [share_gate], axis=1)
    up_weight = jnp.concatenate([expert_up[e] for e in range(local_experts)] + [share_up], axis=1)
    down_weight = jnp.concatenate([expert_down[e] for e in range(local_experts)] + [share_down], axis=0)

    ffn_slots = ring_gather(ffn_in)
    rows = jnp.concatenate(ffn_slots, axis=0)
    cots = jnp.concatenate(cot_slots, axis=0)
    gate_columns = own_gates.transpose(0, 2, 1).reshape(seq_len, local_experts)
    scale = jnp.concatenate(
        [
            jnp.broadcast_to(gate_columns[:, e : e + 1], (seq_len, hidden_units))
            for e in range(local_experts)
        ]
        + [jnp.ones((seq_len, padded), FLOAT)],
        axis=1,
    )
    gate_pre = matmul(rows, gate_weight, (1, 0))
    up_pre = matmul(rows, up_weight, (1, 0))
    sigma = jax.nn.sigmoid(gate_pre)
    active = gate_pre * sigma
    slope = sigma * (1.0 + gate_pre * (1.0 - sigma))
    gated_inner = (scale * active * up_pre).astype(HALF)
    out_part = matmul(gated_inner, down_weight, (1, 0)).astype(HALF)
    inner_grad = matmul(cots, down_weight, (1, 1)) * scale
    gate_grad = (inner_grad * up_pre * slope).astype(HALF)
    up_grad = (inner_grad * active).astype(HALF)
    row_part = (
        matmul(gate_grad, gate_weight, (1, 1)) + matmul(up_grad, up_weight, (1, 1))
    ).astype(HALF)
    row_part = row_part.reshape(group, length, width)
    ffn_in_grad = ring_scatter([row_part[j] for j in range(group)])
    out_part = out_part.reshape(group, length, width)

    down_wgrad = matmul(gated_inner, cots, (0, 0)).astype(HALF)
    gate_wgrad = matmul(rows, gate_grad, (0, 0)).astype(HALF)
    up_wgrad = matmul(rows, up_grad, (0, 0)).astype(HALF)
    routed = local_experts * hidden_units

    def expert_sum(grad):
        return wide_scatter(
            grad.reshape(copies, width // copies, grad.shape[1])[:, :, :routed]
        ).reshape(width // copies, local_experts, hidden_units)

    expert_gate_grad = expert_sum(gate_wgrad).transpose(1, 0, 2).astype(FLOAT)
    expert_up_grad = expert_sum(up_wgrad).transpose(1, 0, 2).astype(FLOAT)
    expert_down_grad = wide_scatter(
        down_wgrad[:routed]
        .reshape(local_experts, copies, hidden_units // copies, width)
        .transpose(1, 0, 2, 3)
    ).astype(FLOAT)
    shared_down_grad = wide_scatter(
        down_wgrad[routed : routed + taken].reshape(copies, share, width)
    ).astype(FLOAT)

    hidden_grad = cotangent.astype(FLOAT) + norm_back(ffn_in_grad, normed_two, inv_two, ffn_gain)
    branch_grad = hidden_grad.astype(HALF)
    attended_grad = matmul(branch_grad, output_weight, (1, 1)).astype(HALF)
    own_out_grad = lax.all_to_all(
        attended_grad[:, :own_heads].reshape(length, group, HEAD_DIM).transpose(1, 0, 2),
        "narrow",
        split_axis=0,
        concat_axis=0,
        tiled=True,
    )
    own_out_grad = by_slot(own_out_grad).reshape(seq_len, HEAD_DIM)
    out_grads = [own_out_grad] + [
        attended_grad[:, own_heads + h * HEAD_DIM : own_heads + (h + 1) * HEAD_DIM]
        for h in range(spare_heads)
    ]
    mixed = (hidden + ring_scatter([out_part[j] for j in range(group)])).astype(HALF)
    grads = [
        causal_back(q, k, v, pos, positions, log_total, out_grad)
        for (q, k, v, pos), (_, log_total), out_grad in zip(heads, outs, out_grads)
    ]
    own_grad = jnp.concatenate(
        [
            rotate(grads[0][0], cosine, -sine).astype(HALF),
            rotate(grads[0][1], cosine, -sine).astype(HALF),
            grads[0][2].astype(HALF),
        ],
        axis=1,
    )
    spare_grad = jnp.concatenate(
        [rotate(g[1], cosine, -sine).astype(HALF) for g in grads[1:]]
        + [g[2].astype(HALF) for g in grads[1:]],
        axis=1,
    )
    spare_query_grad = jnp.concatenate(
        [rotate(g[0], cosine[:length], -sine[:length]).astype(HALF) for g in grads[1:]], axis=1
    )
    attn_part = (
        matmul(own_grad, own_weights, (1, 1)) + matmul(spare_grad, spare_weights, (1, 1))
    ).astype(HALF)
    attn_part = attn_part.reshape(group, length, width)
    attn_in_grad = ring_scatter([attn_part[j] for j in range(group)]) + matmul(
        spare_query_grad, spare_query_weight, (1, 1)
    )
    tokens_grad = hidden_grad + norm_back(attn_in_grad, normed_one, inv_one, attn_gain)

    def spread(grad):
        return wide_scatter(grad.astype(HALF).reshape(copies, width // copies, grad.shape[1]))

    def exchange(part):
        return lax.all_to_all(
            part.reshape(group, part.shape[0] // group, part.shape[1]),
            "narrow",
            split_axis=0,
            concat_axis=0,
            tiled=True,
        ).astype(FLOAT)

    gain_terms = (ffn_in_grad * normed_two).astype(HALF)
    gain_column = matmul(gain_terms, jnp.ones((length, 128), HALF), (0, 0))
    out_wgrad = matmul(attended, branch_grad, (0, 0))
    first = exchange(
        jnp.concatenate(
            [
                spread(jnp.concatenate([out_wgrad, gain_column], axis=1)),
                spread(
                    jnp.concatenate(
                        [
                            gate_wgrad[:, routed : routed + taken],
                            up_wgrad[:, routed : routed + taken],
                        ],
                        axis=1,
                    )
                ),
            ],
            axis=1,
        )
    )
    summed = jnp.sum(first[:, :, : width + 128], axis=0)
    output_weight_grad = summed[:, :width]
    ffn_gain_grad = summed[:, width]

    def shared_columns(part):
        own = part.shape[1]
        return part.reshape(group, own, copies, share).transpose(1, 2, 0, 3).reshape(own, hidden_units)

    shared_gate_grad = shared_columns(first[:, :, width + 128 : width + 128 + taken])
    shared_up_grad = shared_columns(first[:, :, width + 128 + taken :])

    own_wgrad = matmul(attn_all, own_grad, (0, 0))
    spare_wgrad = jnp.concatenate(
        [matmul(attn_in, spare_query_grad, (0, 0)), matmul(attn_all, spare_grad, (0, 0))], axis=1
    )
    second = exchange(spread(jnp.concatenate([own_wgrad, spare_wgrad], axis=1)))
    spare_sum = jnp.sum(second[:, :, 3 * HEAD_DIM :], axis=0)
    spare_width = spare_heads * HEAD_DIM

    def head_grad(index):
        own = second[:, :, index * HEAD_DIM : (index + 1) * HEAD_DIM]
        own = own.transpose(1, 0, 2).reshape(own.shape[1], own_heads)
        return jnp.concatenate(
            [own, spare_sum[:, index * spare_width : (index + 1) * spare_width]], axis=1
        )

    query_weight_grad = head_grad(0)
    key_weight_grad = head_grad(1)
    value_weight_grad = head_grad(2)
    own_rows = width // (copies * group)
    first_row = (lax.axis_index("wide") * group + place) * own_rows

    def own_part(array):
        return lax.dynamic_slice_in_dim(array, first_row, own_rows, axis=0).astype(FLOAT)

    attn_gain_grad = (
        jnp.sum(
            query_weight_grad * own_part(query_weight)
            + key_weight_grad * own_part(key_weight)
            + value_weight_grad * own_part(value_weight),
            axis=1,
        )
        / own_part(attn_gain)
    )
    return (
        mixed,
        tokens_grad,
        attn_gain_grad,
        query_weight_grad,
        key_weight_grad,
        value_weight_grad,
        output_weight_grad,
        ffn_gain_grad,
        shared_gate_grad,
        shared_up_grad,
        shared_down_grad,
        expert_gate_grad,
        expert_up_grad,
        expert_down_grad,
    )


def solution(mesh):
    rows = P(("wide", "narrow"), None)
    vector = P(("wide", "narrow"))
    held = P("narrow", None, None)
    in_specs = (rows, rows, rows) + (P(),) * 9 + (held, held, held, rows)
    out_specs = (rows, rows, vector) + (rows,) * 4 + (vector,) + (rows,) * 3 + (P("narrow", "wide", None),) * 3
    return jax.shard_map(
        on_device, mesh=mesh, in_specs=in_specs, out_specs=out_specs, check_vma=False
    )
```

```python
import functools

import jax
import jax.numpy as jnp
from jax import lax
from jax.experimental import pallas as pl
from jax.experimental.pallas import tpu as pltpu
from jax.sharding import PartitionSpec as P

HEAD_DIM = 128
EPS = 1e-06
FLOAT = jnp.float32
HALF = jnp.bfloat16


def matmul(a, b, contract):
    return lax.dot_general(a, b, ((contract[:1], contract[1:]), ((), ())), preferred_element_type=FLOAT)


def rotate(values, cosine, sine):
    half = values.shape[-1] // 2
    first = values[..., :half]
    second = values[..., half:]
    return jnp.concatenate(
        [first * cosine - second * sine, second * cosine + first * sine], axis=-1
    )


def ring_order(count):
    return list(range(0, count, 2)) + list(range(count - 1, 0, -2))


def ring_steps(count):
    order = ring_order(count)
    ahead = [(order[i], order[(i + 1) % count]) for i in range(count)]
    back = [(b, a) for a, b in ahead]
    return ahead, back


def ring_gather(block):
    count = lax.axis_size("narrow")
    ahead, back = ring_steps(count)
    slots = [None] * count
    slots[0] = block
    forward = backward = block
    for step in range(1, count // 2 + 1):
        forward = lax.ppermute(forward, "narrow", ahead)
        slots[count - step] = forward
        if step < count // 2:
            backward = lax.ppermute(backward, "narrow", back)
            slots[step] = backward
    return slots


def ring_scatter(parts):
    count = lax.axis_size("narrow")
    ahead, back = ring_steps(count)
    half = count // 2
    forward = parts[half].astype(HALF)
    backward = parts[half + 1].astype(HALF)
    for step in range(1, half + 1):
        forward = lax.ppermute(forward, "narrow", ahead).astype(FLOAT)
        if step < half:
            forward = (forward + parts[half - step].astype(FLOAT)).astype(HALF)
            backward = lax.ppermute(backward, "narrow", back).astype(FLOAT)
            if step < half - 1:
                backward = (backward + parts[half + 1 + step].astype(FLOAT)).astype(HALF)
    return parts[0].astype(FLOAT) + forward + backward


def wide_scatter(chunks):
    count = lax.axis_size("wide")
    place = lax.axis_index("wide")
    bit = 1
    while bit < count:
        pairs = chunks.reshape((chunks.shape[0] // 2, 2) + chunks.shape[1:])
        mine = (place // bit) % 2
        kept = lax.dynamic_index_in_dim(pairs, mine, axis=1, keepdims=False)
        sent = lax.dynamic_index_in_dim(pairs, 1 - mine, axis=1, keepdims=False)
        got = lax.ppermute(sent, "wide", [(i, i ^ bit) for i in range(count)])
        chunks = (kept.astype(FLOAT) + got.astype(FLOAT)).astype(HALF)
        bit *= 2
    return chunks[0]


def wide_finish(kept, sent):
    count = lax.axis_size("wide")
    place = lax.axis_index("wide")
    got = lax.ppermute(sent, "wide", [(i, i ^ 1) for i in range(count)])
    bit = 2
    while bit < count:
        mine = (place // bit) % 2

        def half(array, index):
            pairs = array.reshape((array.shape[0] // 2, 2) + array.shape[1:])
            return lax.dynamic_index_in_dim(pairs, index, axis=1, keepdims=False)

        def added(index):
            return (half(kept, index).astype(FLOAT) + half(got, index).astype(FLOAT)).astype(HALF)

        kept, got = added(mine), lax.ppermute(
            added(1 - mine), "wide", [(i, i ^ bit) for i in range(count)]
        )
        bit *= 2
    return kept[0].astype(FLOAT) + got[0].astype(FLOAT)


def norm_back(grad_out, normed, inv_scale, gain):
    scaled = grad_out * gain
    return inv_scale * (scaled - normed * jnp.mean(scaled * normed, axis=1, keepdims=True))


def causal_attention(queries, keys, values, query_pos, key_pos):
    scores = jnp.einsum("qd,kd->qk", queries, keys, preferred_element_type=FLOAT)
    scores = jnp.where(
        query_pos[:, None] >= key_pos[None, :], scores * HEAD_DIM**-0.5, -1e30
    )
    peak = jnp.max(scores, axis=1, keepdims=True)
    shifted = jnp.exp(scores - peak)
    total = jnp.sum(shifted, axis=1, keepdims=True)
    low = (shifted / total).astype(HALF)
    out = matmul(low, values, (1, 0)).astype(HALF)
    return out, peak + jnp.log(total)


def causal_back(queries, keys, values, query_pos, key_pos, log_total, out_grad):
    scores = jnp.einsum("qd,kd->qk", queries, keys, preferred_element_type=FLOAT)
    scores = jnp.where(
        query_pos[:, None] >= key_pos[None, :], scores * HEAD_DIM**-0.5, -1e30
    )
    probs = jnp.exp(scores - log_total)
    prob_grad = matmul(out_grad, values, (1, 1))
    score_grad = (
        probs * (prob_grad - jnp.sum(prob_grad * probs, axis=1, keepdims=True))
    ).astype(HALF)
    value_grad = matmul(probs.astype(HALF), out_grad, (0, 0))
    query_grad = matmul(score_grad, keys, (1, 0)) * HEAD_DIM**-0.5
    key_grad = matmul(score_grad, queries, (0, 0)) * HEAD_DIM**-0.5
    return query_grad, key_grad, value_grad


VMEM_LIMIT = 60 * 2**20
CHUNK = 512


def whole_block(shape):
    return pl.BlockSpec(shape, lambda *_: (0,) * len(shape))


def rows_kernel(count, units, chained, *refs):
    xs, cs, gates = refs[:count], refs[count : 2 * count], refs[2 * count : 3 * count]
    gate_w, up_w, down_w = refs[3 * count : 3 * count + 3]
    outs = refs[3 * count + 3 + (3 if chained else 0) :]
    inner, gate_g, up_g = outs[:3]
    ys, ds = outs[3 : 3 + count], outs[3 + count : 3 + 2 * count]
    y_sum, d_sum, x_rows, c_rows = outs[3 + 2 * count :]
    step = pl.program_id(0)
    length = xs[0].shape[0]
    chunk = gate_w.shape[1]
    per_expert = pl.num_programs(0) // gates[0].shape[1]

    @pl.when(step == 0)
    def _():
        for i in range(count):
            x_rows[i * length : (i + 1) * length] = xs[i][...]
            c_rows[i * length : (i + 1) * length] = cs[i][...]
        y_sum[...] = jnp.zeros_like(y_sum)
        d_sum[...] = jnp.zeros_like(d_sum)

    x, c = x_rows[...], c_rows[...]
    expert = step // per_expert
    column = (step % per_expert) * chunk + lax.broadcasted_iota(
        jnp.int32, (count * length, chunk), 1
    )
    picked = []
    for gate in gates:
        own = gate[:, 0:1]
        for e in range(1, gate.shape[1]):
            own = jnp.where(expert == e, gate[:, e : e + 1], own)
        picked.append(own)
    scale = jnp.where(column < units, jnp.concatenate(picked, axis=0), 1.0)
    gate_pre = matmul(x, gate_w[...], (1, 0))
    up_pre = matmul(x, up_w[...], (1, 0))
    inner_grad = matmul(c, down_w[...], (1, 1)) * scale
    sigma = 0.5 * jnp.tanh(0.5 * gate_pre) + 0.5
    active = gate_pre * sigma
    inner[...] = (active * up_pre * scale).astype(HALF)
    gate_g[...] = (inner_grad * up_pre * (sigma + active * (1.0 - sigma))).astype(HALF)
    up_g[...] = (inner_grad * active).astype(HALF)
    y_sum[...] += matmul(inner[...], down_w[...], (1, 0))
    d_sum[...] += matmul(gate_g[...], gate_w[...], (1, 1)) + matmul(up_g[...], up_w[...], (1, 1))

    @pl.when(step == pl.num_programs(0) - 1)
    def _():
        for i in range(count):
            ys[i][...] = y_sum[i * length : (i + 1) * length].astype(HALF)
            ds[i][...] = d_sum[i * length : (i + 1) * length].astype(HALF)


def expert_rows(units, place, total, kept, xs, cs, gates, gate_w, up_w, down_w):
    count = len(xs)
    length, width = xs[0].shape
    padded = gate_w.shape[1]
    rows = count * length
    column_block = pl.BlockSpec((width, CHUNK), lambda f: (0, f))
    row_block = pl.BlockSpec((CHUNK, width), lambda f: (f, 0))
    kept_block = pl.BlockSpec((rows, CHUNK), lambda f: (place // rows, f))
    chained = kept is not None
    first_kept = 3 * count + 3
    return pl.pallas_call(
        functools.partial(rows_kernel, count, units, chained),
        grid=(padded // CHUNK,),
        in_specs=[whole_block(xs[0].shape)] * (2 * count)
        + [whole_block(gates[0].shape)] * count
        + [column_block, column_block, row_block]
        + [pl.BlockSpec(memory_space=pl.ANY)] * (3 if chained else 0),
        out_specs=[kept_block] * 3 + [whole_block(xs[0].shape)] * (2 * count),
        out_shape=[jax.ShapeDtypeStruct((total, padded), HALF)] * 3
        + [jax.ShapeDtypeStruct(xs[0].shape, HALF)] * (2 * count),
        input_output_aliases={first_kept + i: i for i in range(3)} if chained else {},
        scratch_shapes=[pltpu.VMEM((rows, width), FLOAT)] * 2 + [pltpu.VMEM((rows, width), HALF)] * 2,
        compiler_params=pltpu.CompilerParams(vmem_limit_bytes=VMEM_LIMIT),
        cost_estimate=pl.CostEstimate(
            flops=12 * rows * width * padded,
            bytes_accessed=6 * width * padded + 6 * rows * padded + 8 * rows * width,
            transcendentals=rows * padded,
        ),
        name="expert_rows",
    )(*xs, *cs, *gates, gate_w, up_w, down_w, *(kept if chained else ()))


def fetch_rows(slots, rows, sems):
    length = slots[0].shape[0]
    copies = [
        pltpu.make_async_copy(slot, rows.at[pl.ds(i * length, length)], sems.at[i])
        for i, slot in enumerate(slots)
    ]
    for copy in copies:
        copy.start()
    for copy in copies:
        copy.wait()


def split_rows(source, core, kept, sent, first, size, columns):
    for j in range(kept.shape[0]):
        for target, parity in ((kept, core), (sent, 1 - core)):
            start = pl.multiple_of(first + (2 * j + parity) * size, 8)
            target[j, 0, :, columns] = source[pl.ds(start, size), : columns.stop - columns.start].astype(HALF)


def in_grad_kernel(count, units, core_ref, *refs):
    slots, grad = refs[:count], refs[count]
    kept, sent, share, rows, total, sems = refs[count + 1 :]
    step = pl.program_id(0)
    chunk = grad.shape[1]
    per_expert = pl.num_programs(0) // 2

    @pl.when(step == 0)
    def _():
        fetch_rows(slots, rows, sems)

    total[...] = matmul(rows[...], grad[...], (0, 0))
    core = core_ref[0]
    for part in range(per_expert):
        columns = slice(part * chunk, min((part + 1) * chunk, units))

        @pl.when(step % per_expert == part)
        def _():
            split_rows(total, core, kept, sent, 0, kept.shape[2], columns)

    @pl.when(step == per_expert - 1)
    def _():
        share[...] = total[:, units - (per_expert - 1) * chunk :].astype(HALF)


def in_grad(units, experts, copies, core, slots, grad):
    length, width = slots[0].shape
    total, padded = grad.shape
    per_expert = padded // experts // CHUNK
    part = (copies // 2, experts, width // copies, units)
    part_block = pl.BlockSpec((part[0], 1) + part[2:], lambda f, c: (0, f // per_expert, 0, 0))
    share = padded // experts - units
    return pl.pallas_call(
        functools.partial(in_grad_kernel, len(slots), units),
        grid_spec=pltpu.PrefetchScalarGridSpec(
            num_scalar_prefetch=1,
            grid=(padded // CHUNK,),
            in_specs=[pl.BlockSpec(memory_space=pl.ANY)] * len(slots)
            + [pl.BlockSpec((total, CHUNK), lambda f, c: (0, f))],
            out_specs=[part_block, part_block, whole_block((width, share))],
            scratch_shapes=[
                pltpu.VMEM((total, width), HALF),
                pltpu.VMEM((width, CHUNK), FLOAT),
                pltpu.SemaphoreType.DMA((len(slots),)),
            ],
        ),
        out_shape=[jax.ShapeDtypeStruct(part, HALF)] * 2 + [jax.ShapeDtypeStruct((width, share), HALF)],
        compiler_params=pltpu.CompilerParams(vmem_limit_bytes=VMEM_LIMIT),
        cost_estimate=pl.CostEstimate(
            flops=2 * total * width * padded, bytes_accessed=2 * (total + width) * (padded + width), transcendentals=0
        ),
        name="expert_in_grad",
    )(core, *slots, grad)


def out_grad_kernel(count, units, core_ref, *refs):
    slots, inner = refs[:count], refs[count]
    kept, sent, share, rows, total, sems = refs[count + 1 :]
    step = pl.program_id(0)
    chunk = inner.shape[1]
    per_expert = pl.num_programs(0) // 2

    @pl.when(step == 0)
    def _():
        fetch_rows(slots, rows, sems)

    part = step % per_expert
    total[pl.ds(pl.multiple_of(part * chunk, chunk), chunk)] = matmul(inner[...], rows[...], (0, 0))

    @pl.when(part == per_expert - 1)
    def _():
        split_rows(total, core_ref[0], kept, sent, 0, kept.shape[2], slice(0, kept.shape[3]))

    @pl.when(step == per_expert - 1)
    def _():
        share[...] = total[units:, :].astype(HALF)


def out_grad(units, experts, copies, core, slots, inner):
    length, width = slots[0].shape
    total, padded = inner.shape
    per_expert = padded // experts // CHUNK
    part = (copies // 2, experts, units // copies, width)
    part_block = pl.BlockSpec((part[0], 1) + part[2:], lambda f, c: (0, f // per_expert, 0, 0))
    share = padded // experts - units
    return pl.pallas_call(
        functools.partial(out_grad_kernel, len(slots), units),
        grid_spec=pltpu.PrefetchScalarGridSpec(
            num_scalar_prefetch=1,
            grid=(padded // CHUNK,),
            in_specs=[pl.BlockSpec(memory_space=pl.ANY)] * len(slots)
            + [pl.BlockSpec((total, CHUNK), lambda f, c: (0, f))],
            out_specs=[part_block, part_block, whole_block((share, width))],
            scratch_shapes=[
                pltpu.VMEM((total, width), HALF),
                pltpu.VMEM((padded // experts, width), FLOAT),
                pltpu.SemaphoreType.DMA((len(slots),)),
            ],
        ),
        out_shape=[jax.ShapeDtypeStruct(part, HALF)] * 2 + [jax.ShapeDtypeStruct((share, width), HALF)],
        compiler_params=pltpu.CompilerParams(vmem_limit_bytes=VMEM_LIMIT),
        cost_estimate=pl.CostEstimate(
            flops=2 * total * width * padded, bytes_accessed=2 * (total + width) * (padded + width), transcendentals=0
        ),
        name="expert_out_grad",
    )(core, *slots, inner)


def on_device(
    tokens,
    routes,
    gates,
    attn_gain,
    query_weight,
    key_weight,
    value_weight,
    output_weight,
    ffn_gain,
    shared_gate,
    shared_up,
    shared_down,
    expert_gate,
    expert_up,
    expert_down,
    cotangent,
):
    length, width = tokens.shape
    hidden_units = expert_gate.shape[2]
    local_experts = expert_gate.shape[0]
    group = lax.axis_size("narrow")
    copies = lax.axis_size("wide")
    place = lax.axis_index("narrow")
    experts = group * local_experts
    seq_len = length * group
    own_heads = group * HEAD_DIM
    spare_heads = width // HEAD_DIM - group

    order = jnp.asarray(ring_order(group), dtype=jnp.int32)
    ring_place = jnp.where(place % 2 == 0, place // 2, group - 1 - place // 2)
    slot_block = order[(ring_place + jnp.arange(group, dtype=jnp.int32)) % group]
    blocks = jnp.arange(group, dtype=jnp.int32)
    block_ring = jnp.where(blocks % 2 == 0, blocks // 2, group - 1 - blocks // 2)
    block_slot = (block_ring - ring_place) % group

    def by_slot(array):
        return jnp.take(array, slot_block, axis=0)

    def by_block(array):
        return jnp.take(array, block_slot, axis=0)

    inputs = tokens.astype(FLOAT)
    inv_one = lax.rsqrt(jnp.mean(inputs * inputs, axis=1, keepdims=True) + EPS)
    normed_one = inputs * inv_one
    attn_in = (normed_one * attn_gain).astype(HALF)
    attn_slots = ring_gather(attn_in)
    cot_slots = ring_gather(cotangent)

    expert_ids = jnp.arange(experts, dtype=jnp.int32)
    picked = routes[:, :, None] == expert_ids[None, None, :]
    token_gate = jnp.sum(jnp.where(picked, gates[:, :, None], 0.0), axis=1)
    own_gates = lax.all_to_all(
        token_gate.T.reshape(group, local_experts, length),
        "narrow",
        split_axis=0,
        concat_axis=0,
        tiled=True,
    )
    own_gates = by_slot(own_gates.transpose(0, 2, 1))

    def head_columns(weight):
        return lax.dynamic_slice_in_dim(weight, place * HEAD_DIM, HEAD_DIM, axis=1)

    own_weights = jnp.concatenate(
        [head_columns(query_weight), head_columns(key_weight), head_columns(value_weight)], axis=1
    )
    spare_weights = jnp.concatenate([key_weight[:, own_heads:], value_weight[:, own_heads:]], axis=1)
    spare_query_weight = query_weight[:, own_heads:]
    attn_all = jnp.concatenate(attn_slots, axis=0)
    positions = (
        slot_block[:, None] * length + jnp.arange(length, dtype=jnp.int32)[None, :]
    ).reshape(seq_len)
    half = HEAD_DIM // 2
    freq = 10000.0 ** (-(jnp.arange(half, dtype=FLOAT) * 2.0) / HEAD_DIM)
    angles = positions.astype(FLOAT)[:, None] * freq[None, :]
    cosine, sine = jnp.cos(angles), jnp.sin(angles)
    own_lin = matmul(attn_all, own_weights, (1, 0))
    spare_lin = matmul(attn_all, spare_weights, (1, 0))
    spare_query_lin = matmul(attn_in, spare_query_weight, (1, 0))

    heads = []
    own_q = rotate(own_lin[:, :HEAD_DIM], cosine, sine).astype(HALF)
    own_k = rotate(own_lin[:, HEAD_DIM : 2 * HEAD_DIM], cosine, sine).astype(HALF)
    own_v = own_lin[:, 2 * HEAD_DIM :].astype(HALF)
    heads.append((own_q, own_k, own_v, positions))
    for head in range(spare_heads):
        columns = slice(head * HEAD_DIM, (head + 1) * HEAD_DIM)
        value_columns = slice(
            (spare_heads + head) * HEAD_DIM, (spare_heads + head + 1) * HEAD_DIM
        )
        q = rotate(spare_query_lin[:, columns], cosine[:length], sine[:length]).astype(HALF)
        k = rotate(spare_lin[:, columns], cosine, sine).astype(HALF)
        v = spare_lin[:, value_columns].astype(HALF)
        heads.append((q, k, v, positions[:length]))
    outs = [causal_attention(q, k, v, pos, positions) for q, k, v, pos in heads]

    own_out = by_block(outs[0][0].reshape(group, length, HEAD_DIM))
    returned = lax.all_to_all(own_out, "narrow", split_axis=0, concat_axis=0, tiled=True)
    attended = jnp.concatenate(
        [returned.transpose(1, 0, 2).reshape(length, own_heads)] + [out for out, _ in outs[1:]],
        axis=1,
    )
    hidden = inputs + matmul(attended, output_weight, (1, 0))
    inv_two = lax.rsqrt(jnp.mean(hidden * hidden, axis=1, keepdims=True) + EPS)
    normed_two = hidden * inv_two
    ffn_in = (normed_two * ffn_gain).astype(HALF)

    share = hidden_units // (copies * group)
    taken = copies * share
    padded = -(-taken // 128) * 128
    column = jnp.arange(padded, dtype=jnp.int32)
    unit = jnp.where(
        column < taken, ((column // share) * group + place) * share + column % share, -1
    )
    choice = (jnp.arange(hidden_units, dtype=jnp.int32)[:, None] == unit[None, :]).astype(HALF)
    share_gate = matmul(shared_gate, choice, (1, 0)).astype(HALF)
    share_up = matmul(shared_up, choice, (1, 0)).astype(HALF)
    share_down = matmul(choice, shared_down, (0, 0)).astype(HALF)
    per_expert = -(-(hidden_units + padded) // CHUNK) * CHUNK
    spare_units = per_expert - hidden_units

    def packed(weight, share_part, axis):
        pieces = []
        for e in range(local_experts):
            pieces.append(weight[e])
            filler = share_part if e == 0 else jnp.zeros_like(share_part)
            pieces.append(filler)
        return jnp.concatenate(pieces, axis=axis)

    if padded < spare_units:
        share_gate = jnp.pad(share_gate, ((0, 0), (0, spare_units - padded)))
        share_up = jnp.pad(share_up, ((0, 0), (0, spare_units - padded)))
        share_down = jnp.pad(share_down, ((0, spare_units - padded), (0, 0)))
    gate_weight = packed(expert_gate, share_gate, 1)
    up_weight = packed(expert_up, share_up, 1)
    down_weight = packed(expert_down, share_down, 0)

    ffn_slots = ring_gather(ffn_in)
    half_ring = group // 2
    batches = [(0,), (1, group - 1), (2,), (half_ring, half_ring + 1), (half_ring - 1, half_ring + 2)]
    row_order = [slot for batch in batches if len(batch) == 2 for slot in batch]
    row_order += [slot for batch in batches if len(batch) == 1 for slot in batch]
    kept = None
    out_parts, row_parts = [None] * group, [None] * group
    for batch in batches:
        result = expert_rows(
            hidden_units,
            row_order.index(batch[0]) * length,
            seq_len,
            kept,
            [ffn_slots[j] for j in batch],
            [cot_slots[j] for j in batch],
            [own_gates[j] for j in batch],
            gate_weight,
            up_weight,
            down_weight,
        )
        kept = result[:3]
        for i, j in enumerate(batch):
            out_parts[j] = result[3 + i]
            row_parts[j] = result[3 + len(batch) + i]
    gated_inner, gate_grad, up_grad = kept
    ffn_in_grad = ring_scatter(row_parts)

    core = (lax.axis_index("wide") % 2).astype(jnp.int32).reshape(1)
    ordered_cots = [cot_slots[j] for j in row_order]
    ordered_rows = [ffn_slots[j] for j in row_order]
    down_kept, down_sent, down_share = out_grad(
        hidden_units, local_experts, copies, core, ordered_cots, gated_inner
    )
    gate_kept, gate_sent, gate_share = in_grad(
        hidden_units, local_experts, copies, core, ordered_rows, gate_grad
    )
    up_kept, up_sent, up_share = in_grad(
        hidden_units, local_experts, copies, core, ordered_rows, up_grad
    )
    expert_down_grad = wide_finish(down_kept, down_sent)
    expert_gate_grad = wide_finish(gate_kept, gate_sent)
    expert_up_grad = wide_finish(up_kept, up_sent)
    shared_down_grad = wide_scatter(down_share[:taken].reshape(copies, share, width)).astype(FLOAT)

    hidden_grad = cotangent.astype(FLOAT) + norm_back(ffn_in_grad, normed_two, inv_two, ffn_gain)
    branch_grad = hidden_grad.astype(HALF)
    attended_grad = matmul(branch_grad, output_weight, (1, 1)).astype(HALF)
    own_out_grad = lax.all_to_all(
        attended_grad[:, :own_heads].reshape(length, group, HEAD_DIM).transpose(1, 0, 2),
        "narrow",
        split_axis=0,
        concat_axis=0,
        tiled=True,
    )
    own_out_grad = by_slot(own_out_grad).reshape(seq_len, HEAD_DIM)
    out_grads = [own_out_grad] + [
        attended_grad[:, own_heads + h * HEAD_DIM : own_heads + (h + 1) * HEAD_DIM]
        for h in range(spare_heads)
    ]
    mixed = (hidden + ring_scatter(out_parts)).astype(HALF)
    grads = [
        causal_back(q, k, v, pos, positions, log_total, out_grad)
        for (q, k, v, pos), (_, log_total), out_grad in zip(heads, outs, out_grads)
    ]
    own_grad = jnp.concatenate(
        [
            rotate(grads[0][0], cosine, -sine).astype(HALF),
            rotate(grads[0][1], cosine, -sine).astype(HALF),
            grads[0][2].astype(HALF),
        ],
        axis=1,
    )
    spare_grad = jnp.concatenate(
        [rotate(g[1], cosine, -sine).astype(HALF) for g in grads[1:]]
        + [g[2].astype(HALF) for g in grads[1:]],
        axis=1,
    )
    spare_query_grad = jnp.concatenate(
        [rotate(g[0], cosine[:length], -sine[:length]).astype(HALF) for g in grads[1:]], axis=1
    )
    attn_part = (
        matmul(own_grad, own_weights, (1, 1)) + matmul(spare_grad, spare_weights, (1, 1))
    ).astype(HALF)
    attn_part = attn_part.reshape(group, length, width)
    attn_in_grad = ring_scatter([attn_part[j] for j in range(group)]) + matmul(
        spare_query_grad, spare_query_weight, (1, 1)
    )
    tokens_grad = hidden_grad + norm_back(attn_in_grad, normed_one, inv_one, attn_gain)

    def spread(grad):
        return wide_scatter(grad.astype(HALF).reshape(copies, width // copies, grad.shape[1]))

    def exchange(part):
        return lax.all_to_all(
            part.reshape(group, part.shape[0] // group, part.shape[1]),
            "narrow",
            split_axis=0,
            concat_axis=0,
            tiled=True,
        ).astype(FLOAT)

    gain_terms = (ffn_in_grad * normed_two).astype(HALF)
    gain_column = matmul(gain_terms, jnp.ones((length, 128), HALF), (0, 0))
    out_wgrad = matmul(attended, branch_grad, (0, 0))
    first = exchange(
        jnp.concatenate(
            [
                spread(jnp.concatenate([out_wgrad, gain_column], axis=1)),
                spread(
                    jnp.concatenate(
                        [
                            gate_share[:, :taken],
                            up_share[:, :taken],
                        ],
                        axis=1,
                    )
                ),
            ],
            axis=1,
        )
    )
    summed = jnp.sum(first[:, :, : width + 128], axis=0)
    output_weight_grad = summed[:, :width]
    ffn_gain_grad = summed[:, width]

    def shared_columns(part):
        own = part.shape[1]
        return part.reshape(group, own, copies, share).transpose(1, 2, 0, 3).reshape(own, hidden_units)

    shared_gate_grad = shared_columns(first[:, :, width + 128 : width + 128 + taken])
    shared_up_grad = shared_columns(first[:, :, width + 128 + taken :])

    own_wgrad = matmul(attn_all, own_grad, (0, 0))
    spare_wgrad = jnp.concatenate(
        [matmul(attn_in, spare_query_grad, (0, 0)), matmul(attn_all, spare_grad, (0, 0))], axis=1
    )
    second = exchange(spread(jnp.concatenate([own_wgrad, spare_wgrad], axis=1)))
    spare_sum = jnp.sum(second[:, :, 3 * HEAD_DIM :], axis=0)
    spare_width = spare_heads * HEAD_DIM

    def head_grad(index):
        own = second[:, :, index * HEAD_DIM : (index + 1) * HEAD_DIM]
        own = own.transpose(1, 0, 2).reshape(own.shape[1], own_heads)
        return jnp.concatenate(
            [own, spare_sum[:, index * spare_width : (index + 1) * spare_width]], axis=1
        )

    query_weight_grad = head_grad(0)
    key_weight_grad = head_grad(1)
    value_weight_grad = head_grad(2)
    own_rows = width // (copies * group)
    first_row = (lax.axis_index("wide") * group + place) * own_rows

    def own_part(array):
        return lax.dynamic_slice_in_dim(array, first_row, own_rows, axis=0).astype(FLOAT)

    attn_gain_grad = (
        jnp.sum(
            query_weight_grad * own_part(query_weight)
            + key_weight_grad * own_part(key_weight)
            + value_weight_grad * own_part(value_weight),
            axis=1,
        )
        / own_part(attn_gain)
    )
    return (
        mixed,
        tokens_grad,
        attn_gain_grad,
        query_weight_grad,
        key_weight_grad,
        value_weight_grad,
        output_weight_grad,
        ffn_gain_grad,
        shared_gate_grad,
        shared_up_grad,
        shared_down_grad,
        expert_gate_grad,
        expert_up_grad,
        expert_down_grad,
    )


def solution(mesh):
    rows = P(("wide", "narrow"), None)
    vector = P(("wide", "narrow"))
    held = P("narrow", None, None)
    in_specs = (rows, rows, rows) + (P(),) * 9 + (held, held, held, rows)
    out_specs = (rows, rows, vector) + (rows,) * 4 + (vector,) + (rows,) * 3 + (P("narrow", "wide", None),) * 3
    return jax.shard_map(
        on_device, mesh=mesh, in_specs=in_specs, out_specs=out_specs, check_vma=False
    )
```

```python
import functools

import jax
import jax.numpy as jnp
from jax import lax
from jax.experimental import pallas as pl
from jax.experimental.pallas import tpu as pltpu
from jax.sharding import PartitionSpec as P

HEAD_DIM = 128
EPS = 1e-06
FLOAT = jnp.float32
HALF = jnp.bfloat16


def matmul(a, b, contract):
    return lax.dot_general(a, b, ((contract[:1], contract[1:]), ((), ())), preferred_element_type=FLOAT)


def ring_order(count):
    return list(range(0, count, 2)) + list(range(count - 1, 0, -2))


def ring_steps(count):
    order = ring_order(count)
    ahead = [(order[i], order[(i + 1) % count]) for i in range(count)]
    back = [(b, a) for a, b in ahead]
    return ahead, back


def after(value, *others):
    return lax.optimization_barrier((value, others))[0]


def ring_gather(block, work=None):
    count = lax.axis_size("narrow")
    ahead, back = ring_steps(count)
    slots = [None] * count
    slots[0] = block
    forward = backward = block
    done = ()
    for step in range(1, count // 2 + 1):
        sent_ahead, sent_back = after((forward, backward), *done)
        forward = lax.ppermute(sent_ahead, "narrow", ahead)
        if step < count // 2:
            backward = lax.ppermute(sent_back, "narrow", back)
        done = work(step - 1, slots) if work else ()
        slots[count - step] = forward
        if step < count // 2:
            slots[step] = backward
    return slots


def ring_scatter(parts, work=None):
    count = lax.axis_size("narrow")
    ahead, back = ring_steps(count)
    half = count // 2
    forward, backward = parts[half], parts[half + 1]
    before = done = ()
    for step in range(1, half + 1):
        forward, backward = after((forward, backward), *before)
        before = done
        forward = lax.ppermute(forward, "narrow", ahead)
        if step < half:
            backward = lax.ppermute(backward, "narrow", back)
        done = work(step, (forward, backward)) if work else ()
        if step < half:
            forward = (forward.astype(FLOAT) + parts[half - step].astype(FLOAT)).astype(HALF)
            if step < half - 1:
                backward = (
                    backward.astype(FLOAT) + parts[half + 1 + step].astype(FLOAT)
                ).astype(HALF)
    return parts[0].astype(FLOAT) + forward.astype(FLOAT) + backward.astype(FLOAT)


def wide_scatter(chunks):
    count = lax.axis_size("wide")
    place = lax.axis_index("wide")
    bit = 1
    while bit < count:
        pairs = chunks.reshape((chunks.shape[0] // 2, 2) + chunks.shape[1:])
        mine = (place // bit) % 2
        kept = lax.dynamic_index_in_dim(pairs, mine, axis=1, keepdims=False)
        sent = lax.dynamic_index_in_dim(pairs, 1 - mine, axis=1, keepdims=False)
        got = lax.ppermute(sent, "wide", [(i, i ^ bit) for i in range(count)])
        chunks = (kept.astype(FLOAT) + got.astype(FLOAT)).astype(HALF)
        bit *= 2
    return chunks[0]


def wide_finish(kept, sent):
    count = lax.axis_size("wide")
    place = lax.axis_index("wide")
    got = lax.ppermute(sent, "wide", [(i, i ^ 1) for i in range(count)])
    bit = 2
    while bit < count:
        mine = (place // bit) % 2

        def half(array, index):
            pairs = array.reshape((array.shape[0] // 2, 2) + array.shape[1:])
            return lax.dynamic_index_in_dim(pairs, index, axis=1, keepdims=False)

        def added(index):
            return (half(kept, index).astype(FLOAT) + half(got, index).astype(FLOAT)).astype(HALF)

        kept, got = added(mine), lax.ppermute(
            added(1 - mine), "wide", [(i, i ^ bit) for i in range(count)]
        )
        bit *= 2
    return kept[0].astype(FLOAT) + got[0].astype(FLOAT)


def norm_back(grad_out, normed, inv_scale, gain):
    scaled = grad_out * gain
    return inv_scale * (scaled - normed * jnp.mean(scaled * normed, axis=1, keepdims=True))


VMEM_LIMIT = 60 * 2**20
CHUNK = 512


def whole_block(shape):
    return pl.BlockSpec(shape, lambda *_: (0,) * len(shape))


def rows_kernel(count, units, chained, *refs):
    xs, cs, gates = refs[:count], refs[count : 2 * count], refs[2 * count : 3 * count]
    gate_w, up_w, down_w = refs[3 * count : 3 * count + 3]
    outs = refs[3 * count + 3 + (3 if chained else 0) :]
    inner, gate_g, up_g = outs[:3]
    ys, ds = outs[3 : 3 + count], outs[3 + count : 3 + 2 * count]
    y_sum, d_sum, x_rows, c_rows = outs[3 + 2 * count :]
    step = pl.program_id(0)
    length = xs[0].shape[0]
    chunk = gate_w.shape[1]
    per_expert = pl.num_programs(0) // gates[0].shape[1]

    @pl.when(step == 0)
    def _():
        for i in range(count):
            x_rows[i * length : (i + 1) * length] = xs[i][...]
            c_rows[i * length : (i + 1) * length] = cs[i][...]
        y_sum[...] = jnp.zeros_like(y_sum)
        d_sum[...] = jnp.zeros_like(d_sum)

    x, c = x_rows[...], c_rows[...]
    expert = step // per_expert
    column = (step % per_expert) * chunk + lax.broadcasted_iota(
        jnp.int32, (count * length, chunk), 1
    )
    picked = []
    for gate in gates:
        own = gate[:, 0:1]
        for e in range(1, gate.shape[1]):
            own = jnp.where(expert == e, gate[:, e : e + 1], own)
        picked.append(own)
    scale = jnp.where(column < units, jnp.concatenate(picked, axis=0), 1.0)
    gate_pre = matmul(x, gate_w[...], (1, 0))
    up_pre = matmul(x, up_w[...], (1, 0))
    inner_grad = matmul(c, down_w[...], (1, 1)) * scale
    sigma = 0.5 * jnp.tanh(0.5 * gate_pre) + 0.5
    active = gate_pre * sigma
    inner[...] = (active * up_pre * scale).astype(HALF)
    gate_g[...] = (inner_grad * up_pre * (sigma + active * (1.0 - sigma))).astype(HALF)
    up_g[...] = (inner_grad * active).astype(HALF)
    y_sum[...] += matmul(inner[...], down_w[...], (1, 0))
    d_sum[...] += matmul(gate_g[...], gate_w[...], (1, 1)) + matmul(up_g[...], up_w[...], (1, 1))

    @pl.when(step == pl.num_programs(0) - 1)
    def _():
        for i in range(count):
            ys[i][...] = y_sum[i * length : (i + 1) * length].astype(HALF)
            ds[i][...] = d_sum[i * length : (i + 1) * length].astype(HALF)


def expert_rows(units, place, total, kept, xs, cs, gates, gate_w, up_w, down_w):
    count = len(xs)
    length, width = xs[0].shape
    padded = gate_w.shape[1]
    rows = count * length
    column_block = pl.BlockSpec((width, CHUNK), lambda f: (0, f))
    row_block = pl.BlockSpec((CHUNK, width), lambda f: (f, 0))
    kept_block = pl.BlockSpec((rows, CHUNK), lambda f: (place // rows, f))
    chained = kept is not None
    first_kept = 3 * count + 3
    return pl.pallas_call(
        functools.partial(rows_kernel, count, units, chained),
        grid=(padded // CHUNK,),
        in_specs=[whole_block(xs[0].shape)] * (2 * count)
        + [whole_block(gates[0].shape)] * count
        + [column_block, column_block, row_block]
        + [pl.BlockSpec(memory_space=pl.ANY)] * (3 if chained else 0),
        out_specs=[kept_block] * 3 + [whole_block(xs[0].shape)] * (2 * count),
        out_shape=[jax.ShapeDtypeStruct((total, padded), HALF)] * 3
        + [jax.ShapeDtypeStruct(xs[0].shape, HALF)] * (2 * count),
        input_output_aliases={first_kept + i: i for i in range(3)} if chained else {},
        scratch_shapes=[pltpu.VMEM((rows, width), FLOAT)] * 2 + [pltpu.VMEM((rows, width), HALF)] * 2,
        compiler_params=pltpu.CompilerParams(vmem_limit_bytes=VMEM_LIMIT),
        cost_estimate=pl.CostEstimate(
            flops=12 * rows * width * padded,
            bytes_accessed=6 * width * padded + 6 * rows * padded + 8 * rows * width,
            transcendentals=rows * padded,
        ),
        name="expert_rows",
    )(*xs, *cs, *gates, gate_w, up_w, down_w, *(kept if chained else ()))


def pack_experts_kernel(units, choice, shared_gate, shared_up, shared_down, gate, up, down, *rest):
    gate_out, up_out, down_out, sems = rest
    experts = gate.shape[0]
    per_expert = gate_out.shape[1] // experts
    copies = []
    for e in range(experts):
        own = pl.ds(e * per_expert, units)
        for source, target in (
            (gate.at[e], gate_out.at[:, own]),
            (up.at[e], up_out.at[:, own]),
            (down.at[e], down_out.at[own]),
        ):
            copies.append(pltpu.make_async_copy(source, target, sems.at[len(copies)]))
    start_all(copies)
    for e in range(experts):
        gap = slice(e * per_expert + units, (e + 1) * per_expert)
        if e == 0:
            gate_out[:, gap] = matmul(shared_gate[...], choice[...], (1, 0)).astype(HALF)
            up_out[:, gap] = matmul(shared_up[...], choice[...], (1, 0)).astype(HALF)
            down_out[gap] = matmul(choice[...], shared_down[...], (0, 0)).astype(HALF)
        else:
            gate_out[:, gap] = jnp.zeros((gate_out.shape[0], per_expert - units), HALF)
            up_out[:, gap] = jnp.zeros((up_out.shape[0], per_expert - units), HALF)
            down_out[gap] = jnp.zeros((per_expert - units, down_out.shape[1]), HALF)
    wait_all(copies)


def pack_experts(per_expert, choice, shared_gate, shared_up, shared_down, gate, up, down):
    experts, width, units = gate.shape
    padded = experts * per_expert
    anywhere = pl.BlockSpec(memory_space=pl.ANY)
    shapes = [(width, padded), (width, padded), (padded, width)]
    return pl.pallas_call(
        functools.partial(pack_experts_kernel, units),
        in_specs=[pl.BlockSpec(memory_space=pltpu.VMEM)] * 4 + [anywhere] * 3,
        out_specs=[pl.BlockSpec(memory_space=pltpu.VMEM)] * 3,
        out_shape=[jax.ShapeDtypeStruct(shape, HALF) for shape in shapes],
        scratch_shapes=[pltpu.SemaphoreType.DMA((3 * experts,))],
        compiler_params=pltpu.CompilerParams(vmem_limit_bytes=VMEM_LIMIT),
        cost_estimate=pl.CostEstimate(flops=0, bytes_accessed=12 * width * padded, transcendentals=0),
        name="pack_experts",
    )(choice, shared_gate, shared_up, shared_down, gate, up, down)


def fetch_rows(slots, rows, sems):
    length = slots[0].shape[0]
    copies = [
        pltpu.make_async_copy(slot, rows.at[pl.ds(i * length, length)], sems.at[i])
        for i, slot in enumerate(slots)
    ]
    for copy in copies:
        copy.start()
    for copy in copies:
        copy.wait()


def split_rows(source, core, kept, sent, first, size, columns):
    for j in range(kept.shape[0]):
        for target, parity in ((kept, core), (sent, 1 - core)):
            start = pl.multiple_of(first + (2 * j + parity) * size, 8)
            target[j, 0, :, columns] = source[pl.ds(start, size), : columns.stop - columns.start].astype(HALF)


def in_grad_kernel(count, units, core_ref, *refs):
    slots, grad = refs[:count], refs[count]
    kept, sent, share, rows, total, sems = refs[count + 1 :]
    step = pl.program_id(0)
    chunk = grad.shape[1]
    per_expert = pl.num_programs(0) // 2

    @pl.when(step == 0)
    def _():
        fetch_rows(slots, rows, sems)

    total[...] = matmul(rows[...], grad[...], (0, 0))
    core = core_ref[0]
    for part in range(per_expert):
        columns = slice(part * chunk, min((part + 1) * chunk, units))

        @pl.when(step % per_expert == part)
        def _():
            split_rows(total, core, kept, sent, 0, kept.shape[2], columns)

    @pl.when(step == per_expert - 1)
    def _():
        share[...] = total[:, units - (per_expert - 1) * chunk :].astype(HALF)


def in_grad(units, experts, copies, core, slots, grad):
    length, width = slots[0].shape
    total, padded = grad.shape
    per_expert = padded // experts // CHUNK
    part = (copies // 2, experts, width // copies, units)
    part_block = pl.BlockSpec((part[0], 1) + part[2:], lambda f, c: (0, f // per_expert, 0, 0))
    share = padded // experts - units
    return pl.pallas_call(
        functools.partial(in_grad_kernel, len(slots), units),
        grid_spec=pltpu.PrefetchScalarGridSpec(
            num_scalar_prefetch=1,
            grid=(padded // CHUNK,),
            in_specs=[pl.BlockSpec(memory_space=pl.ANY)] * len(slots)
            + [pl.BlockSpec((total, CHUNK), lambda f, c: (0, f))],
            out_specs=[part_block, part_block, whole_block((width, share))],
            scratch_shapes=[
                pltpu.VMEM((total, width), HALF),
                pltpu.VMEM((width, CHUNK), FLOAT),
                pltpu.SemaphoreType.DMA((len(slots),)),
            ],
        ),
        out_shape=[jax.ShapeDtypeStruct(part, HALF)] * 2 + [jax.ShapeDtypeStruct((width, share), HALF)],
        compiler_params=pltpu.CompilerParams(vmem_limit_bytes=VMEM_LIMIT),
        cost_estimate=pl.CostEstimate(
            flops=2 * total * width * padded, bytes_accessed=2 * (total + width) * (padded + width), transcendentals=0
        ),
        name="expert_in_grad",
    )(core, *slots, grad)


def out_grad_kernel(count, units, core_ref, *refs):
    slots, inner = refs[:count], refs[count]
    kept, sent, share, rows, total, sems = refs[count + 1 :]
    step = pl.program_id(0)
    chunk = inner.shape[1]
    per_expert = pl.num_programs(0) // 2

    @pl.when(step == 0)
    def _():
        fetch_rows(slots, rows, sems)

    part = step % per_expert
    total[pl.ds(pl.multiple_of(part * chunk, chunk), chunk)] = matmul(inner[...], rows[...], (0, 0))

    @pl.when(part == per_expert - 1)
    def _():
        split_rows(total, core_ref[0], kept, sent, 0, kept.shape[2], slice(0, kept.shape[3]))

    @pl.when(step == per_expert - 1)
    def _():
        share[...] = total[units:, :].astype(HALF)


def out_grad(units, experts, copies, core, slots, inner):
    length, width = slots[0].shape
    total, padded = inner.shape
    per_expert = padded // experts // CHUNK
    part = (copies // 2, experts, units // copies, width)
    part_block = pl.BlockSpec((part[0], 1) + part[2:], lambda f, c: (0, f // per_expert, 0, 0))
    share = padded // experts - units
    return pl.pallas_call(
        functools.partial(out_grad_kernel, len(slots), units),
        grid_spec=pltpu.PrefetchScalarGridSpec(
            num_scalar_prefetch=1,
            grid=(padded // CHUNK,),
            in_specs=[pl.BlockSpec(memory_space=pl.ANY)] * len(slots)
            + [pl.BlockSpec((total, CHUNK), lambda f, c: (0, f))],
            out_specs=[part_block, part_block, whole_block((share, width))],
            scratch_shapes=[
                pltpu.VMEM((total, width), HALF),
                pltpu.VMEM((padded // experts, width), FLOAT),
                pltpu.SemaphoreType.DMA((len(slots),)),
            ],
        ),
        out_shape=[jax.ShapeDtypeStruct(part, HALF)] * 2 + [jax.ShapeDtypeStruct((share, width), HALF)],
        compiler_params=pltpu.CompilerParams(vmem_limit_bytes=VMEM_LIMIT),
        cost_estimate=pl.CostEstimate(
            flops=2 * total * width * padded, bytes_accessed=2 * (total + width) * (padded + width), transcendentals=0
        ),
        name="expert_out_grad",
    )(core, *slots, inner)


def turn(values, cosine, sine):
    return values * cosine + pltpu.roll(values, HEAD_DIM // 2, 1) * sine


def head_slice(index):
    return slice(index * HEAD_DIM, (index + 1) * HEAD_DIM)


def start_all(copies):
    for copy in copies:
        copy.start()


def wait_all(copies):
    for copy in copies:
        copy.wait()


def pack_heads_kernel(spare, place_ref, query, key, value, out, sems):
    width = query.shape[1]
    own = pl.ds(pl.multiple_of(place_ref[0] * HEAD_DIM, HEAD_DIM), HEAD_DIM)
    rest = pl.ds(width - spare * HEAD_DIM, spare * HEAD_DIM)
    pieces = [
        (query, own, 1),
        (key, own, 1),
        (key, rest, spare),
        (value, own, 1),
        (value, rest, spare),
        (query, rest, spare),
    ]
    copies, tile = [], 0
    for i, (source, columns, tiles) in enumerate(pieces):
        target = out.at[:, pl.ds(tile * HEAD_DIM, tiles * HEAD_DIM)]
        copies.append(pltpu.make_async_copy(source.at[:, columns], target, sems.at[i]))
        tile += tiles
    start_all(copies)
    wait_all(copies)


def pack_heads(place, spare, query, key, value):
    width = query.shape[0]
    columns = (3 + 3 * spare) * HEAD_DIM
    anywhere = pl.BlockSpec(memory_space=pl.ANY)
    return pl.pallas_call(
        functools.partial(pack_heads_kernel, spare),
        grid_spec=pltpu.PrefetchScalarGridSpec(
            num_scalar_prefetch=1,
            grid=(1,),
            in_specs=[anywhere] * 3,
            out_specs=whole_block((width, columns)),
            scratch_shapes=[pltpu.SemaphoreType.DMA((6,))],
        ),
        out_shape=jax.ShapeDtypeStruct((width, columns), HALF),
        compiler_params=pltpu.CompilerParams(vmem_limit_bytes=VMEM_LIMIT),
        cost_estimate=pl.CostEstimate(flops=0, bytes_accessed=4 * width * columns, transcendentals=0),
        name="pack_heads",
    )(place, query, key, value)


def project_kernel(turned, tiles, chained, block_ref, *refs):
    x, weight, cosine, sine = refs[:4]
    outs = refs[5 if chained else 4 :]
    lin = matmul(x[...], weight[...], (1, 0))
    for tile in range(weight.shape[1] // HEAD_DIM):
        part = lin[:, head_slice(tile)]
        if tile < turned or tile >= tiles:
            part = turn(part, cosine[0], sine[0])
        if tile < tiles:
            outs[0][0, :, head_slice(tile)] = part.astype(HALF)
        else:
            outs[1][:, head_slice(tile - tiles)] = part.astype(HALF)


def project(blocks, slot, x, weight, cosine, sine, turned, tiles, packed):
    length, width = x.shape
    count = cosine.shape[0]
    extra = weight.shape[1] - tiles * HEAD_DIM if packed is None else 0
    columns = tiles * HEAD_DIM + extra
    chained = packed is not None
    table = pl.BlockSpec((1, length, HEAD_DIM), lambda i, b: (b[slot], 0, 0))
    packed_shape = (count, length, tiles * HEAD_DIM)
    out_specs = [pl.BlockSpec((1,) + packed_shape[1:], lambda i, b: (b[slot], 0, 0))]
    out_shape = [jax.ShapeDtypeStruct(packed_shape, HALF)]
    if extra:
        out_specs.append(whole_block((length, extra)))
        out_shape.append(jax.ShapeDtypeStruct((length, extra), HALF))
    return pl.pallas_call(
        functools.partial(project_kernel, turned, tiles, chained),
        grid_spec=pltpu.PrefetchScalarGridSpec(
            num_scalar_prefetch=1,
            grid=(1,),
            in_specs=[whole_block(x.shape), whole_block((width, columns)), table, table]
            + ([pl.BlockSpec(memory_space=pl.ANY)] if chained else []),
            out_specs=out_specs,
        ),
        out_shape=out_shape,
        input_output_aliases={5: 0} if chained else {},
        compiler_params=pltpu.CompilerParams(vmem_limit_bytes=VMEM_LIMIT),
        cost_estimate=pl.CostEstimate(
            flops=2 * length * width * columns,
            bytes_accessed=2 * (length * width + (length + width) * columns),
            transcendentals=0,
        ),
        name="project",
    )(blocks, x, weight, cosine, sine, *([packed] if chained else []))


EXP_SCALE = HEAD_DIM**-0.5 * 1.4426950408889634


def masked_scores(query, keys, first):
    scores = matmul(query, keys, (1, 1)) * EXP_SCALE
    row = lax.broadcasted_iota(jnp.int32, scores.shape, 0)
    column = lax.broadcasted_iota(jnp.int32, scores.shape, 1)
    return jnp.where(column <= row + first, scores, -1e30)


def attend(query, keys, values, first):
    scores = masked_scores(query, keys, first)
    peak = jnp.max(scores, axis=1, keepdims=True)
    shifted = jnp.exp2(scores - peak)
    total = jnp.sum(shifted, axis=1, keepdims=True)
    out = matmul(shifted.astype(HALF), values, (1, 0)) / total
    level = jnp.broadcast_to(peak + jnp.log2(total), (query.shape[0], HEAD_DIM))
    return out.astype(HALF), level


def attention_kernel(spare, place_ref, packed, spare_q, out, spare_out, level, spare_level):
    count, length = packed.shape[:2]
    keys_at, values_at = head_slice(1), head_slice(2 + spare)

    def rows(columns, blocks):
        return packed[:blocks, :, columns].reshape(blocks * length, HEAD_DIM)

    for block in range(count):
        out[block], level[block] = attend(
            packed[block, :, head_slice(0)],
            rows(keys_at, block + 1),
            rows(values_at, block + 1),
            block * length,
        )
    for head in range(spare):
        spare_out[:, head_slice(head)], spare_level[head] = attend(
            spare_q[:, head_slice(head)],
            rows(head_slice(2 + head), count),
            rows(head_slice(3 + spare + head), count),
            place_ref[0] * length,
        )


def attention(place, packed, spare_q):
    count, length, columns = packed.shape
    spare = spare_q.shape[1] // HEAD_DIM
    area = (count * (count + 1) // 2 + spare * count) * length * length
    shapes = [
        ((count, length, HEAD_DIM), HALF),
        (spare_q.shape, HALF),
        ((count, length, HEAD_DIM), FLOAT),
        ((spare, length, HEAD_DIM), FLOAT),
    ]
    return pl.pallas_call(
        functools.partial(attention_kernel, spare),
        grid_spec=pltpu.PrefetchScalarGridSpec(
            num_scalar_prefetch=1,
            grid=(1,),
            in_specs=[whole_block(packed.shape), whole_block(spare_q.shape)],
            out_specs=[whole_block(shape) for shape, _ in shapes],
        ),
        out_shape=[jax.ShapeDtypeStruct(shape, kind) for shape, kind in shapes],
        compiler_params=pltpu.CompilerParams(vmem_limit_bytes=VMEM_LIMIT),
        cost_estimate=pl.CostEstimate(
            flops=8 * area * HEAD_DIM, bytes_accessed=4 * count * length * columns, transcendentals=area
        ),
        name="attention",
    )(place, packed, spare_q)


def attend_back(query, keys, values, first, level, out, out_grad):
    scores = masked_scores(query, keys, first)
    probs = jnp.exp2(scores - level[:, :1])
    prob_grad = matmul(out_grad, values, (1, 1))
    shared = jnp.sum(out_grad.astype(FLOAT) * out.astype(FLOAT), axis=1, keepdims=True)
    score_grad = (probs * (prob_grad - shared)).astype(HALF)
    value_grad = matmul(probs.astype(HALF), out_grad, (0, 0))
    query_grad = matmul(score_grad, keys, (1, 0)) * HEAD_DIM**-0.5
    key_grad = matmul(score_grad, query, (0, 0)) * HEAD_DIM**-0.5
    return query_grad, key_grad, value_grad


def attention_back_kernel(
    spare, place_ref, packed, spare_q, out, spare_out, level, spare_level, out_grad, spare_out_grad,
    cosine, sine, grad, spare_grad, key_sum, value_sum
):
    count, length = packed.shape[:2]
    keys_at, values_at = head_slice(1), head_slice(2 + spare)

    def rows(columns, blocks):
        return packed[:blocks, :, columns].reshape(blocks * length, HEAD_DIM)

    key_sum[...] = jnp.zeros_like(key_sum)
    value_sum[...] = jnp.zeros_like(value_sum)
    for block in range(count):
        query_grad, key_grad, value_grad = attend_back(
            packed[block, :, head_slice(0)],
            rows(keys_at, block + 1),
            rows(values_at, block + 1),
            block * length,
            level[block],
            out[block],
            out_grad[block],
        )
        grad[block, :, head_slice(0)] = turn(query_grad, cosine[block], -sine[block]).astype(HALF)
        seen = (block + 1) * length
        key_sum[:seen] += key_grad
        value_sum[:seen] += value_grad

    def put(index, values, turned):
        for block in range(count):
            part = values[block * length : (block + 1) * length]
            if turned:
                part = turn(part, cosine[block], -sine[block])
            grad[block, :, head_slice(index)] = part.astype(HALF)

    put(1, key_sum[...], True)
    put(2 + spare, value_sum[...], False)
    place = place_ref[0]
    for head in range(spare):
        query_grad, key_grad, value_grad = attend_back(
            spare_q[:, head_slice(head)],
            rows(head_slice(2 + head), count),
            rows(head_slice(3 + spare + head), count),
            place * length,
            spare_level[head],
            spare_out[:, head_slice(head)],
            spare_out_grad[:, head_slice(head)],
        )
        spare_grad[:, head_slice(head)] = turn(query_grad, cosine[place], -sine[place]).astype(HALF)
        put(2 + head, key_grad, True)
        put(3 + spare + head, value_grad, False)


def attention_back(place, packed, spare_q, out, spare_out, level, spare_level, out_grad, spare_out_grad, cosine, sine):
    count, length, columns = packed.shape
    spare = spare_q.shape[1] // HEAD_DIM
    area = (count * (count + 1) // 2 + spare * count) * length * length
    operands = (packed, spare_q, out, spare_out, level, spare_level, out_grad, spare_out_grad, cosine, sine)
    return pl.pallas_call(
        functools.partial(attention_back_kernel, spare),
        grid_spec=pltpu.PrefetchScalarGridSpec(
            num_scalar_prefetch=1,
            grid=(1,),
            in_specs=[whole_block(array.shape) for array in operands],
            out_specs=[whole_block(packed.shape), whole_block(spare_q.shape)],
            scratch_shapes=[pltpu.VMEM((count * length, HEAD_DIM), FLOAT)] * 2,
        ),
        out_shape=[jax.ShapeDtypeStruct(packed.shape, HALF), jax.ShapeDtypeStruct(spare_q.shape, HALF)],
        compiler_params=pltpu.CompilerParams(vmem_limit_bytes=VMEM_LIMIT),
        cost_estimate=pl.CostEstimate(
            flops=20 * area * HEAD_DIM, bytes_accessed=8 * count * length * columns, transcendentals=area
        ),
        name="attention_back",
    )(place, *operands)


def part_kernel(slots, blocks_ref, grad, weight, *outs):
    for slot, out in zip(slots, outs):
        out[...] = matmul(grad[blocks_ref[slot]], weight[...], (1, 1)).astype(HALF)


def attn_parts(blocks, slots, grad, weight):
    length, columns = grad.shape[1:]
    width = weight.shape[0]
    count = len(slots)
    return pl.pallas_call(
        functools.partial(part_kernel, slots),
        grid_spec=pltpu.PrefetchScalarGridSpec(
            num_scalar_prefetch=1,
            grid=(1,),
            in_specs=[whole_block(grad.shape), whole_block((width, columns))],
            out_specs=[whole_block((length, width))] * count,
        ),
        out_shape=[jax.ShapeDtypeStruct((length, width), HALF)] * count,
        compiler_params=pltpu.CompilerParams(vmem_limit_bytes=VMEM_LIMIT),
        cost_estimate=pl.CostEstimate(
            flops=2 * count * length * width * columns,
            bytes_accessed=2 * (count * length + columns) * width,
            transcendentals=0,
        ),
        name="attn_parts",
    )(blocks, grad, weight)


def attn_wgrad_kernel(count, blocks_ref, core_ref, *refs):
    slots, own, grad, spare_grad = refs[:count], refs[count], refs[count + 1], refs[count + 2]
    kept, sent, rows, total, sems = refs[count + 3 :]
    length = own.shape[0]
    copies = [
        pltpu.make_async_copy(
            slot, rows.at[pl.ds(pl.multiple_of(blocks_ref[i] * length, length), length)], sems.at[i]
        )
        for i, slot in enumerate(slots)
    ]
    for copy in copies:
        copy.start()
    columns = grad.shape[2]
    total[:, columns:] = matmul(own[...], spare_grad[...], (0, 0))
    for copy in copies:
        copy.wait()
    total[:, :columns] = matmul(rows[...], grad[...].reshape(count * length, columns), (0, 0))
    size = kept.shape[1]
    for j in range(kept.shape[0]):
        for target, parity in ((kept, core_ref[0]), (sent, 1 - core_ref[0])):
            start = pl.multiple_of((2 * j + parity) * size, 8)
            target[j] = total[pl.ds(start, size)].astype(HALF)


def attn_wgrad(blocks, core, copies, slots, grad, spare_grad):
    length, width = slots[0].shape
    count, _, columns = grad.shape
    wide = columns + spare_grad.shape[1]
    part = (copies // 2, width // copies, wide)
    return pl.pallas_call(
        functools.partial(attn_wgrad_kernel, count),
        grid_spec=pltpu.PrefetchScalarGridSpec(
            num_scalar_prefetch=2,
            grid=(1,),
            in_specs=[pl.BlockSpec(memory_space=pl.ANY)] * count
            + [whole_block(slots[0].shape), whole_block(grad.shape), whole_block(spare_grad.shape)],
            out_specs=[whole_block(part)] * 2,
            scratch_shapes=[
                pltpu.VMEM((count * length, width), HALF),
                pltpu.VMEM((width, wide), FLOAT),
                pltpu.SemaphoreType.DMA((count,)),
            ],
        ),
        out_shape=[jax.ShapeDtypeStruct(part, HALF)] * 2,
        compiler_params=pltpu.CompilerParams(vmem_limit_bytes=VMEM_LIMIT),
        cost_estimate=pl.CostEstimate(
            flops=2 * count * length * width * wide,
            bytes_accessed=2 * (count * length + wide) * width,
            transcendentals=0,
        ),
        name="attn_wgrad",
    )(blocks, core, *slots, slots[0], grad, spare_grad)


def on_device(
    tokens,
    routes,
    gates,
    attn_gain,
    query_weight,
    key_weight,
    value_weight,
    output_weight,
    ffn_gain,
    shared_gate,
    shared_up,
    shared_down,
    expert_gate,
    expert_up,
    expert_down,
    cotangent,
):
    length, width = tokens.shape
    hidden_units = expert_gate.shape[2]
    local_experts = expert_gate.shape[0]
    group = lax.axis_size("narrow")
    copies = lax.axis_size("wide")
    place = lax.axis_index("narrow")
    experts = group * local_experts
    seq_len = length * group
    own_heads = group * HEAD_DIM
    spare_heads = width // HEAD_DIM - group

    order = jnp.asarray(ring_order(group), dtype=jnp.int32)
    ring_place = jnp.where(place % 2 == 0, place // 2, group - 1 - place // 2)
    slot_block = order[(ring_place + jnp.arange(group, dtype=jnp.int32)) % group]
    blocks = jnp.arange(group, dtype=jnp.int32)
    block_ring = jnp.where(blocks % 2 == 0, blocks // 2, group - 1 - blocks // 2)
    block_slot = (block_ring - ring_place) % group

    def by_slot(array):
        return jnp.take(array, slot_block, axis=0)

    def by_block(array):
        return jnp.take(array, block_slot, axis=0)

    inputs = tokens.astype(FLOAT)
    inv_one = lax.rsqrt(jnp.mean(inputs * inputs, axis=1, keepdims=True) + EPS)
    normed_one = inputs * inv_one
    attn_in = (normed_one * attn_gain).astype(HALF)
    expert_ids = jnp.arange(experts, dtype=jnp.int32)
    picked = after(routes, attn_in)[:, :, None] == expert_ids[None, None, :]
    token_gate = jnp.sum(jnp.where(picked, gates[:, :, None], 0.0), axis=1)
    own_gates = lax.all_to_all(
        token_gate.T.reshape(group, local_experts, length),
        "narrow",
        split_axis=0,
        concat_axis=0,
        tiled=True,
    )
    own_gates = by_slot(own_gates.transpose(0, 2, 1))

    own_place = place.astype(jnp.int32).reshape(1)
    packed_weight = pack_heads(own_place, spare_heads, query_weight, key_weight, value_weight)
    spare_query_weight = query_weight[:, own_heads:]
    turned, tiles = 2 + spare_heads, 3 + 2 * spare_heads
    half = HEAD_DIM // 2
    freq = 10000.0 ** (-(jnp.arange(half, dtype=FLOAT) * 2.0) / HEAD_DIM)
    angles = jnp.arange(seq_len, dtype=FLOAT)[:, None] * freq[None, :]
    cosine, sine = jnp.cos(angles), jnp.sin(angles)
    cosine = jnp.concatenate([cosine, cosine], axis=1).reshape(group, length, HEAD_DIM)
    sine = jnp.concatenate([-sine, sine], axis=1).reshape(group, length, HEAD_DIM)

    share = hidden_units // (copies * group)
    taken = copies * share
    padded = -(-taken // 128) * 128
    per_expert = -(-(hidden_units + padded) // CHUNK) * CHUNK
    gap = per_expert - hidden_units
    column = jnp.arange(gap, dtype=jnp.int32)
    unit = jnp.where(
        column < taken, ((column // share) * group + place) * share + column % share, -1
    )
    choice = (jnp.arange(hidden_units, dtype=jnp.int32)[:, None] == unit[None, :]).astype(HALF)

    heads = {}

    def project_slots(step, slots):
        for slot in (step, group - step) if step else (0,):
            result = project(
                slot_block,
                slot,
                slots[slot],
                packed_weight,
                cosine,
                sine,
                turned,
                tiles,
                heads.get("packed"),
            )
            heads["packed"] = result[0]
            if slot == 0:
                heads["spare"] = result[1]
        if step == 0:
            heads["gates"] = own_gates
        if step == 1:
            heads["experts"] = pack_experts(
                per_expert,
                *after((choice, shared_gate, shared_up, shared_down, expert_gate, expert_up, expert_down), slots[1]),
            )
        return tuple(heads.values())

    half_ring = group // 2
    attn_slots = ring_gather(attn_in, project_slots)
    gate_weight, up_weight, down_weight = heads["experts"]
    (packed_heads,) = project(
        slot_block,
        half_ring,
        attn_slots[half_ring],
        packed_weight,
        cosine,
        sine,
        turned,
        tiles,
        heads["packed"],
    )
    spare_q = heads["spare"]
    cot_slots = ring_gather(after(cotangent, attn_slots[half_ring]))
    own_out, spare_out, level, spare_level = attention(own_place, packed_heads, spare_q)
    returned = lax.all_to_all(own_out, "narrow", split_axis=0, concat_axis=0, tiled=True)
    attended = jnp.concatenate(
        [returned.transpose(1, 0, 2).reshape(length, own_heads), spare_out], axis=1
    )
    hidden = inputs + matmul(attended, output_weight, (1, 0))
    inv_two = lax.rsqrt(jnp.mean(hidden * hidden, axis=1, keepdims=True) + EPS)
    normed_two = hidden * inv_two
    ffn_in = (normed_two * ffn_gain).astype(HALF)

    batches = [(0,)] + [(k, group - k) for k in range(1, half_ring)] + [(half_ring,)]
    row_order = [slot for batch in batches if len(batch) == 2 for slot in batch] + [0, half_ring]
    experts_state = {"kept": None}
    out_parts, row_parts = [None] * group, [None] * group

    def expert_batch(step, slots):
        batch = batches[step]
        result = expert_rows(
            hidden_units,
            row_order.index(batch[0]) * length,
            seq_len,
            experts_state["kept"],
            [slots[j] for j in batch],
            [cot_slots[j] for j in batch],
            [own_gates[j] for j in batch],
            gate_weight,
            up_weight,
            down_weight,
        )
        experts_state["kept"] = result[:3]
        for i, j in enumerate(batch):
            out_parts[j] = result[3 + i]
            row_parts[j] = result[3 + len(batch) + i]
        return tuple(result[3:])

    ffn_slots = ring_gather(ffn_in, expert_batch)
    expert_batch(half_ring, ffn_slots)
    gated_inner, gate_grad, up_grad = experts_state["kept"]

    core = (lax.axis_index("wide") % 2).astype(jnp.int32).reshape(1)
    ordered_cots = [cot_slots[j] for j in row_order]
    ordered_rows = [ffn_slots[j] for j in row_order]
    weight_grads = {}

    def expert_weights(step, arrived):
        if step == 2:
            weight_grads["down"] = out_grad(
                hidden_units, local_experts, copies, core, ordered_cots, after(gated_inner, *arrived)
            )
            return tuple(weight_grads["down"])
        if step == 1:
            weight_grads["gate"] = in_grad(
                hidden_units, local_experts, copies, core, ordered_rows, after(gate_grad, *arrived)
            )
            return tuple(weight_grads["gate"])
        if step == 3:
            weight_grads["up"] = in_grad(
                hidden_units, local_experts, copies, core, ordered_rows, after(up_grad, *arrived)
            )
            return tuple(weight_grads["up"])
        return ()

    ffn_in_grad = ring_scatter(row_parts, expert_weights)
    down_kept, down_sent, down_share = weight_grads["down"]
    gate_kept, gate_sent, gate_share = weight_grads["gate"]
    up_kept, up_sent, up_share = weight_grads["up"]
    expert_down_grad = wide_finish(down_kept, down_sent)
    expert_gate_grad = wide_finish(gate_kept, gate_sent)
    expert_up_grad = wide_finish(up_kept, up_sent)
    shared_down_grad = wide_scatter(down_share[:taken].reshape(copies, share, width)).astype(FLOAT)

    hidden_grad = cotangent.astype(FLOAT) + norm_back(ffn_in_grad, normed_two, inv_two, ffn_gain)
    branch_grad = hidden_grad.astype(HALF)
    attended_grad = matmul(branch_grad, output_weight, (1, 1)).astype(HALF)
    own_out_grad = lax.all_to_all(
        attended_grad[:, :own_heads].reshape(length, group, HEAD_DIM).transpose(1, 0, 2),
        "narrow",
        split_axis=0,
        concat_axis=0,
        tiled=True,
    )
    late_parts = list(out_parts)
    late_parts[half_ring], late_parts[half_ring + 1] = after(
        (out_parts[half_ring], out_parts[half_ring + 1]), ffn_in_grad
    )
    mixed = (hidden + ring_scatter(late_parts)).astype(HALF)
    head_grad, spare_query_grad = attention_back(
        own_place,
        packed_heads,
        spare_q,
        own_out,
        spare_out,
        level,
        spare_level,
        own_out_grad,
        attended_grad[:, own_heads:],
        cosine,
        sine,
    )
    far = (half_ring, half_ring + 1)
    near = tuple(j for j in range(group) if j not in far)
    attn_part = dict(zip(far, attn_parts(slot_block, far, head_grad, packed_weight)))
    attn_part.update(zip(near, attn_parts(slot_block, near, head_grad, packed_weight)))
    attn_in_grad = ring_scatter([attn_part[j] for j in range(group)])
    attn_in_grad = attn_in_grad + matmul(spare_query_grad, spare_query_weight, (1, 1))
    tokens_grad = hidden_grad + norm_back(attn_in_grad, normed_one, inv_one, attn_gain)

    def spread(grad):
        return wide_scatter(grad.astype(HALF).reshape(copies, width // copies, grad.shape[1]))

    def exchange(part):
        return lax.all_to_all(
            part.reshape(group, part.shape[0] // group, part.shape[1]),
            "narrow",
            split_axis=0,
            concat_axis=0,
            tiled=True,
        ).astype(FLOAT)

    gain_terms = (ffn_in_grad * normed_two).astype(HALF)
    gain_column = matmul(gain_terms, jnp.ones((length, 128), HALF), (0, 0))
    out_wgrad = matmul(attended, branch_grad, (0, 0))
    first = exchange(
        jnp.concatenate(
            [
                spread(jnp.concatenate([out_wgrad, gain_column], axis=1)),
                spread(
                    jnp.concatenate(
                        [
                            gate_share[:, :padded],
                            up_share[:, :padded],
                        ],
                        axis=1,
                    )
                ),
            ],
            axis=1,
        )
    )
    summed = jnp.sum(first[:, :, : width + 128], axis=0)
    output_weight_grad = summed[:, :width]
    ffn_gain_grad = summed[:, width]

    spot = jnp.arange(group * padded, dtype=jnp.int32)
    spot_column = spot % padded
    spot_unit = jnp.where(
        spot_column < taken,
        ((spot_column // share) * group + spot // padded) * share + spot_column % share,
        -1,
    )
    to_units = (spot_unit[:, None] == jnp.arange(hidden_units, dtype=jnp.int32)[None, :]).astype(HALF)
    to_units = to_units.reshape(group, padded, hidden_units)

    def shared_columns(part):
        return jnp.einsum("grc,gcu->ru", part.astype(HALF), to_units, preferred_element_type=FLOAT)

    shared_gate_grad = shared_columns(first[:, :, width + 128 : width + 128 + padded])
    shared_up_grad = shared_columns(first[:, :, width + 128 + padded :])

    attn_kept, attn_sent = attn_wgrad(
        slot_block, core, copies, attn_slots, head_grad, spare_query_grad
    )
    second = exchange(wide_finish(attn_kept, attn_sent).astype(HALF))
    packed_sum = jnp.sum(second, axis=0)
    spare_width = spare_heads * HEAD_DIM

    def head_grads(own_tile, spare_tile):
        own = second[:, :, head_slice(own_tile)]
        own = own.transpose(1, 0, 2).reshape(own.shape[1], own_heads)
        first = spare_tile * HEAD_DIM
        return jnp.concatenate([own, packed_sum[:, first : first + spare_width]], axis=1)

    query_weight_grad = head_grads(0, tiles)
    key_weight_grad = head_grads(1, 2)
    value_weight_grad = head_grads(turned, turned + 1)
    own_rows = width // (copies * group)
    first_row = (lax.axis_index("wide") * group + place) * own_rows

    def own_part(array):
        return lax.dynamic_slice_in_dim(array, first_row, own_rows, axis=0).astype(FLOAT)

    attn_gain_grad = (
        jnp.sum(
            query_weight_grad * own_part(query_weight)
            + key_weight_grad * own_part(key_weight)
            + value_weight_grad * own_part(value_weight),
            axis=1,
        )
        / own_part(attn_gain)
    )
    return (
        mixed,
        tokens_grad,
        attn_gain_grad,
        query_weight_grad,
        key_weight_grad,
        value_weight_grad,
        output_weight_grad,
        ffn_gain_grad,
        shared_gate_grad,
        shared_up_grad,
        shared_down_grad,
        expert_gate_grad,
        expert_up_grad,
        expert_down_grad,
    )


def solution(mesh):
    rows = P(("wide", "narrow"), None)
    vector = P(("wide", "narrow"))
    held = P("narrow", None, None)
    in_specs = (rows, rows, rows) + (P(),) * 9 + (held, held, held, rows)
    out_specs = (rows, rows, vector) + (rows,) * 4 + (vector,) + (rows,) * 3 + (P("narrow", "wide", None),) * 3
    return jax.shard_map(
        on_device, mesh=mesh, in_specs=in_specs, out_specs=out_specs, check_vma=False
    )
```

```python
import functools

import jax
import jax.numpy as jnp
from jax import lax
from jax.experimental import pallas as pl
from jax.experimental.pallas import tpu as pltpu
from jax.sharding import PartitionSpec as P

HEAD_DIM = 128
EPS = 1e-06
FLOAT = jnp.float32
HALF = jnp.bfloat16


def matmul(a, b, contract):
    return lax.dot_general(a, b, ((contract[:1], contract[1:]), ((), ())), preferred_element_type=FLOAT)


def ring_order(count):
    return list(range(0, count, 2)) + list(range(count - 1, 0, -2))


def ring_steps(count):
    order = ring_order(count)
    ahead = [(order[i], order[(i + 1) % count]) for i in range(count)]
    back = [(b, a) for a, b in ahead]
    return ahead, back


def after(value, *others):
    return lax.optimization_barrier((value, others))[0]


def ring_gather(block, work=None):
    count = lax.axis_size("narrow")
    ahead, back = ring_steps(count)
    slots = [None] * count
    slots[0] = block
    forward = backward = block
    done = ()
    for step in range(1, count // 2 + 1):
        sent_ahead, sent_back = after((forward, backward), *done)
        forward = lax.ppermute(sent_ahead, "narrow", ahead)
        if step < count // 2:
            backward = lax.ppermute(sent_back, "narrow", back)
        done = work(step - 1, slots) if work else ()
        slots[count - step] = forward
        if step < count // 2:
            slots[step] = backward
    return slots


class RingSum:
    def __init__(self, parts):
        self.parts = parts
        self.half = len(parts) // 2
        self.step = 0
        self.forward, self.backward = parts[self.half], parts[self.half + 1]

    def hop(self, *others):
        ahead, back = ring_steps(len(self.parts))
        self.step += 1
        forward, backward = after((self.forward, self.backward), *others)
        self.forward = lax.ppermute(forward, "narrow", ahead)
        if self.step < self.half:
            self.backward = lax.ppermute(backward, "narrow", back)
        return self.forward, self.backward

    def add(self):
        own_forward = self.parts[self.half - self.step]
        if self.step < self.half - 1:
            own_backward = self.parts[self.half + 1 + self.step]
            self.forward, self.backward = add_pairs(
                (self.forward, self.backward), (own_forward, own_backward)
            )
        else:
            (self.forward,) = add_pairs((self.forward,), (own_forward,))

    def last(self):
        return self.parts[0], self.forward, self.backward


def add_kernel(count, *refs):
    for i in range(count):
        total = refs[i][...].astype(FLOAT) + refs[count + i][...].astype(FLOAT)
        refs[2 * count + i][...] = total.astype(HALF)


def add_pairs(left, right):
    count = len(left)
    shape = left[0].shape
    return pl.pallas_call(
        functools.partial(add_kernel, count),
        out_shape=[jax.ShapeDtypeStruct(shape, HALF)] * count,
        compiler_params=pltpu.CompilerParams(vmem_limit_bytes=VMEM_LIMIT),
        cost_estimate=pl.CostEstimate(
            flops=count * left[0].size, bytes_accessed=6 * count * left[0].size, transcendentals=0
        ),
        name="add_pairs",
    )(*left, *right)


def wide_first(sent):
    count = lax.axis_size("wide")
    return lax.ppermute(sent, "wide", [(i, i ^ 1) for i in range(count)])


def wide_rest(kept, got):
    count = lax.axis_size("wide")
    place = lax.axis_index("wide")
    terms = [kept, got]
    bit = 2
    while bit < count:
        mine = (place // bit) % 2

        def half(array, index):
            pairs = array.reshape((array.shape[0] // 2, 2) + array.shape[1:])
            return lax.dynamic_index_in_dim(pairs, index, axis=1, keepdims=False)

        sent = sum(half(term, 1 - mine).astype(FLOAT) for term in terms).astype(HALF)
        swap = [(i, i ^ bit) for i in range(count)]
        terms = [half(term, mine) for term in terms] + [lax.ppermute(sent, "wide", swap)]
        bit *= 2
    return terms


def wide_total(terms):
    return sum(term[0].astype(FLOAT) for term in terms)


VMEM_LIMIT = 60 * 2**20
CHUNK = 512


def whole_block(shape):
    return pl.BlockSpec(shape, lambda *_: (0,) * len(shape))


def rows_kernel(slots, units, chained, blocks_ref, *refs):
    count = len(slots)
    xs, cs, gates = refs[:count], refs[count : 2 * count], refs[2 * count]
    gate_w, up_w, down_w = refs[2 * count + 1 : 2 * count + 4]
    outs = refs[2 * count + 4 + (3 if chained else 0) :]
    inner, gate_g, up_g = outs[:3]
    ys, ds = outs[3 : 3 + count], outs[3 + count : 3 + 2 * count]
    y_sum, d_sum, x_rows, c_rows = outs[3 + 2 * count :]
    step = pl.program_id(0)
    length = xs[0].shape[0]
    chunk = gate_w.shape[1]
    per_expert = pl.num_programs(0) // gates.shape[2]

    @pl.when(step == 0)
    def _():
        for i in range(count):
            x_rows[i * length : (i + 1) * length] = xs[i][...]
            c_rows[i * length : (i + 1) * length] = cs[i][...]
        y_sum[...] = jnp.zeros_like(y_sum)
        d_sum[...] = jnp.zeros_like(d_sum)

    x, c = x_rows[...], c_rows[...]
    expert = step // per_expert
    column = (step % per_expert) * chunk + lax.broadcasted_iota(
        jnp.int32, (count * length, chunk), 1
    )
    picked = []
    for slot in slots:
        gate = gates[blocks_ref[slot]]
        own = gate[:, 0:1]
        for e in range(1, gate.shape[1]):
            own = jnp.where(expert == e, gate[:, e : e + 1], own)
        picked.append(own)
    scale = jnp.where(column < units, jnp.concatenate(picked, axis=0), 1.0)
    gate_pre = matmul(x, gate_w[...], (1, 0))
    up_pre = matmul(x, up_w[...], (1, 0))
    inner_grad = matmul(c, down_w[...], (1, 1)) * scale
    sigma = 0.5 * jnp.tanh(0.5 * gate_pre) + 0.5
    active = gate_pre * sigma
    inner[...] = (active * up_pre * scale).astype(HALF)
    gate_g[...] = (inner_grad * up_pre * (sigma + active * (1.0 - sigma))).astype(HALF)
    up_g[...] = (inner_grad * active).astype(HALF)
    y_sum[...] += matmul(inner[...], down_w[...], (1, 0))
    d_sum[...] += matmul(gate_g[...], gate_w[...], (1, 1)) + matmul(up_g[...], up_w[...], (1, 1))

    @pl.when(step == pl.num_programs(0) - 1)
    def _():
        for i in range(count):
            ys[i][...] = y_sum[i * length : (i + 1) * length].astype(HALF)
            ds[i][...] = d_sum[i * length : (i + 1) * length].astype(HALF)


def expert_rows(units, slots, place, total, kept, blocks, xs, cs, gates, gate_w, up_w, down_w):
    count = len(xs)
    length, width = xs[0].shape
    padded = gate_w.shape[1]
    rows = count * length
    column_block = pl.BlockSpec((width, CHUNK), lambda f, b: (0, f))
    row_block = pl.BlockSpec((CHUNK, width), lambda f, b: (f, 0))
    kept_block = pl.BlockSpec((rows, CHUNK), lambda f, b: (place // rows, f))
    chained = kept is not None
    first_kept = 1 + 2 * count + 4
    return pl.pallas_call(
        functools.partial(rows_kernel, slots, units, chained),
        grid_spec=pltpu.PrefetchScalarGridSpec(
            num_scalar_prefetch=1,
            grid=(padded // CHUNK,),
            in_specs=[whole_block(xs[0].shape)] * (2 * count)
            + [whole_block(gates.shape), column_block, column_block, row_block]
            + [pl.BlockSpec(memory_space=pl.ANY)] * (3 if chained else 0),
            out_specs=[kept_block] * 3 + [whole_block(xs[0].shape)] * (2 * count),
            scratch_shapes=[pltpu.VMEM((rows, width), FLOAT)] * 2
            + [pltpu.VMEM((rows, width), HALF)] * 2,
        ),
        out_shape=[jax.ShapeDtypeStruct((total, padded), HALF)] * 3
        + [jax.ShapeDtypeStruct(xs[0].shape, HALF)] * (2 * count),
        input_output_aliases={first_kept + i: i for i in range(3)} if chained else {},
        compiler_params=pltpu.CompilerParams(vmem_limit_bytes=VMEM_LIMIT),
        cost_estimate=pl.CostEstimate(
            flops=12 * rows * width * padded,
            bytes_accessed=6 * width * padded + 6 * rows * padded + 8 * rows * width,
            transcendentals=rows * padded,
        ),
        name="expert_rows",
    )(blocks, *xs, *cs, gates, gate_w, up_w, down_w, *(kept if chained else ()))


def pack_experts_kernel(units, choice, shared_gate, shared_up, shared_down, gate, up, down, *rest):
    gate_out, up_out, down_out, sems = rest
    experts = gate.shape[0]
    per_expert = gate_out.shape[1] // experts
    copies = []
    for e in range(experts):
        own = pl.ds(e * per_expert, units)
        for source, target in (
            (gate.at[e], gate_out.at[:, own]),
            (up.at[e], up_out.at[:, own]),
            (down.at[e], down_out.at[own]),
        ):
            copies.append(pltpu.make_async_copy(source, target, sems.at[len(copies)]))
    start_all(copies)
    for e in range(experts):
        gap = slice(e * per_expert + units, (e + 1) * per_expert)
        if e == 0:
            gate_out[:, gap] = matmul(shared_gate[...], choice[...], (1, 0)).astype(HALF)
            up_out[:, gap] = matmul(shared_up[...], choice[...], (1, 0)).astype(HALF)
            down_out[gap] = matmul(choice[...], shared_down[...], (0, 0)).astype(HALF)
        else:
            gate_out[:, gap] = jnp.zeros((gate_out.shape[0], per_expert - units), HALF)
            up_out[:, gap] = jnp.zeros((up_out.shape[0], per_expert - units), HALF)
            down_out[gap] = jnp.zeros((per_expert - units, down_out.shape[1]), HALF)
    wait_all(copies)


def pack_experts(per_expert, choice, shared_gate, shared_up, shared_down, gate, up, down):
    experts, width, units = gate.shape
    padded = experts * per_expert
    anywhere = pl.BlockSpec(memory_space=pl.ANY)
    shapes = [(width, padded), (width, padded), (padded, width)]
    return pl.pallas_call(
        functools.partial(pack_experts_kernel, units),
        in_specs=[pl.BlockSpec(memory_space=pltpu.VMEM)] * 4 + [anywhere] * 3,
        out_specs=[pl.BlockSpec(memory_space=pltpu.VMEM)] * 3,
        out_shape=[jax.ShapeDtypeStruct(shape, HALF) for shape in shapes],
        scratch_shapes=[pltpu.SemaphoreType.DMA((3 * experts,))],
        compiler_params=pltpu.CompilerParams(vmem_limit_bytes=VMEM_LIMIT),
        cost_estimate=pl.CostEstimate(flops=0, bytes_accessed=12 * width * padded, transcendentals=0),
        name="pack_experts",
    )(choice, shared_gate, shared_up, shared_down, gate, up, down)


def fetch_rows(slots, rows, sems):
    length = slots[0].shape[0]
    copies = [
        pltpu.make_async_copy(slot, rows.at[pl.ds(i * length, length)], sems.at[i])
        for i, slot in enumerate(slots)
    ]
    for copy in copies:
        copy.start()
    for copy in copies:
        copy.wait()


def split_rows(source, core, kept, sent, first, size, columns):
    for j in range(kept.shape[0]):
        for target, parity in ((kept, core), (sent, 1 - core)):
            start = pl.multiple_of(first + (2 * j + parity) * size, 8)
            target[j, 0, :, columns] = source[pl.ds(start, size), : columns.stop - columns.start].astype(HALF)


def in_grad_kernel(count, units, core_ref, *refs):
    slots, grad = refs[:count], refs[count]
    kept, sent, share, rows, total, sems = refs[count + 1 :]
    step = pl.program_id(0)
    chunk = grad.shape[1]
    per_expert = pl.num_programs(0) // 2

    @pl.when(step == 0)
    def _():
        fetch_rows(slots, rows, sems)

    total[...] = matmul(rows[...], grad[...], (0, 0))
    core = core_ref[0]
    for part in range(per_expert):
        columns = slice(part * chunk, min((part + 1) * chunk, units))

        @pl.when(step % per_expert == part)
        def _():
            split_rows(total, core, kept, sent, 0, kept.shape[2], columns)

    @pl.when(step == per_expert - 1)
    def _():
        share[...] = total[:, units - (per_expert - 1) * chunk :]


def in_grad(units, experts, copies, core, slots, grad):
    length, width = slots[0].shape
    total, padded = grad.shape
    per_expert = padded // experts // CHUNK
    part = (copies // 2, experts, width // copies, units)
    part_block = pl.BlockSpec((part[0], 1) + part[2:], lambda f, c: (0, f // per_expert, 0, 0))
    share = padded // experts - units
    return pl.pallas_call(
        functools.partial(in_grad_kernel, len(slots), units),
        grid_spec=pltpu.PrefetchScalarGridSpec(
            num_scalar_prefetch=1,
            grid=(padded // CHUNK,),
            in_specs=[pl.BlockSpec(memory_space=pl.ANY)] * len(slots)
            + [pl.BlockSpec((total, CHUNK), lambda f, c: (0, f))],
            out_specs=[part_block, part_block, whole_block((width, share))],
            scratch_shapes=[
                pltpu.VMEM((total, width), HALF),
                pltpu.VMEM((width, CHUNK), FLOAT),
                pltpu.SemaphoreType.DMA((len(slots),)),
            ],
        ),
        out_shape=[jax.ShapeDtypeStruct(part, HALF)] * 2 + [jax.ShapeDtypeStruct((width, share), FLOAT)],
        compiler_params=pltpu.CompilerParams(vmem_limit_bytes=VMEM_LIMIT),
        cost_estimate=pl.CostEstimate(
            flops=2 * total * width * padded, bytes_accessed=2 * (total + width) * (padded + width), transcendentals=0
        ),
        name="expert_in_grad",
    )(core, *slots, grad)


def out_grad_kernel(count, units, core_ref, *refs):
    slots, inner = refs[:count], refs[count]
    kept, sent, rows, total, sems = refs[count + 1 :]
    step = pl.program_id(0)
    chunk = inner.shape[1]
    per_expert = total.shape[0] // chunk
    experts = pl.num_programs(0) // per_expert
    copies = 2 * kept.shape[0]

    @pl.when(step == 0)
    def _():
        fetch_rows(slots, rows, sems)

    part = step % per_expert
    total[pl.ds(pl.multiple_of(part * chunk, chunk), chunk)] = matmul(inner[...], rows[...], (0, 0))

    def split(first, size, row):
        for j in range(kept.shape[0]):
            for target, parity in ((kept, core_ref[0]), (sent, 1 - core_ref[0])):
                start = pl.multiple_of(first + (2 * j + parity) * size, 8)
                target[j, row : row + size] = total[pl.ds(start, size)].astype(HALF)

    for e in range(experts):

        @pl.when(step == (e + 1) * per_expert - 1)
        def _():
            split(0, units // copies, e * (units // copies))
            if e == 0:
                split(units, (total.shape[0] - units) // copies, experts * (units // copies))


def out_grad(units, experts, copies, core, slots, inner):
    length, width = slots[0].shape
    total, padded = inner.shape
    share = padded // experts - units
    part = (copies // 2, (experts * units + share) // copies, width)
    return pl.pallas_call(
        functools.partial(out_grad_kernel, len(slots), units),
        grid_spec=pltpu.PrefetchScalarGridSpec(
            num_scalar_prefetch=1,
            grid=(padded // CHUNK,),
            in_specs=[pl.BlockSpec(memory_space=pl.ANY)] * len(slots)
            + [pl.BlockSpec((total, CHUNK), lambda f, c: (0, f))],
            out_specs=[whole_block(part)] * 2,
            scratch_shapes=[
                pltpu.VMEM((total, width), HALF),
                pltpu.VMEM((padded // experts, width), FLOAT),
                pltpu.SemaphoreType.DMA((len(slots),)),
            ],
        ),
        out_shape=[jax.ShapeDtypeStruct(part, HALF)] * 2,
        compiler_params=pltpu.CompilerParams(vmem_limit_bytes=VMEM_LIMIT),
        cost_estimate=pl.CostEstimate(
            flops=2 * total * width * padded, bytes_accessed=2 * (total + width) * (padded + width), transcendentals=0
        ),
        name="expert_out_grad",
    )(core, *slots, inner)


def scaled_rows(values):
    scale = lax.rsqrt(jnp.mean(values * values, axis=1, keepdims=True) + EPS)
    return values * scale, scale


def mix_kernel(returned, spare_out, weight, tokens, gain, hidden, attended, ffn_in):
    for head in range(returned.shape[0]):
        attended[:, head_slice(head)] = returned[head]
    attended[:, returned.shape[0] * HEAD_DIM :] = spare_out[...]
    hidden[...] = tokens[...].astype(FLOAT) + matmul(attended[...], weight[...], (1, 0))
    ffn_in[...] = (scaled_rows(hidden[...])[0] * gain[...]).astype(HALF)


def mix(returned, spare_out, weight, tokens, gain):
    shape = tokens.shape
    return pl.pallas_call(
        mix_kernel,
        out_shape=[
            jax.ShapeDtypeStruct(shape, FLOAT),
            jax.ShapeDtypeStruct(shape, HALF),
            jax.ShapeDtypeStruct(shape, HALF),
        ],
        compiler_params=pltpu.CompilerParams(vmem_limit_bytes=VMEM_LIMIT),
        cost_estimate=pl.CostEstimate(
            flops=2 * shape[0] * shape[1] ** 2, bytes_accessed=2 * shape[1] ** 2 + 12 * shape[0] * shape[1], transcendentals=0
        ),
        name="mix",
    )(returned, spare_out, weight, tokens, gain)


def norm_grad(grad_out, normed, scale, gain):
    scaled = grad_out * gain
    return scale * (scaled - normed * jnp.mean(scaled * normed, axis=1, keepdims=True))


def back_kernel(
    own, forward, backward, hidden, cotangent, gain, weight, hidden_grad, branch, out_grad, spare_grad, terms
):
    ffn_in_grad = own[...].astype(FLOAT) + forward[...].astype(FLOAT) + backward[...].astype(FLOAT)
    normed, scale = scaled_rows(hidden[...])
    terms[...] = (ffn_in_grad * normed).astype(HALF)
    hidden_grad[...] = cotangent[...].astype(FLOAT) + norm_grad(ffn_in_grad, normed, scale, gain[...])
    branch[...] = hidden_grad[...].astype(HALF)
    attended_grad = matmul(branch[...], weight[...], (1, 1)).astype(HALF)
    for head in range(out_grad.shape[0]):
        out_grad[head] = attended_grad[:, head_slice(head)]
    spare_grad[...] = attended_grad[:, out_grad.shape[0] * HEAD_DIM :]


def back(arrived, hidden, cotangent, gain, weight, heads):
    length, width = hidden.shape
    shapes = [
        ((length, width), FLOAT),
        ((length, width), HALF),
        ((heads, length, HEAD_DIM), HALF),
        ((length, width - heads * HEAD_DIM), HALF),
        ((length, width), HALF),
    ]
    return pl.pallas_call(
        back_kernel,
        out_shape=[jax.ShapeDtypeStruct(shape, kind) for shape, kind in shapes],
        compiler_params=pltpu.CompilerParams(vmem_limit_bytes=VMEM_LIMIT),
        cost_estimate=pl.CostEstimate(
            flops=2 * length * width**2, bytes_accessed=2 * width**2 + 24 * length * width, transcendentals=0
        ),
        name="back",
    )(*arrived, hidden, cotangent, gain, weight)


def dense_wgrad_kernel(core_ref, attended, branch, terms, gate_share, up_share, kept, sent, total):
    width = attended.shape[1]
    total[:, :width] = matmul(attended[...], branch[...], (0, 0))
    ones = jnp.ones((terms.shape[0], HEAD_DIM), HALF)
    total[:, width : width + HEAD_DIM] = matmul(terms[...], ones, (0, 0))
    size = kept.shape[1]
    for j in range(kept.shape[0]):
        for target, parity in ((kept, core_ref[0]), (sent, 1 - core_ref[0])):
            start = pl.multiple_of((2 * j + parity) * size, 8)
            rows = pl.ds(start, size)
            column = width + HEAD_DIM
            target[j, :, :column] = total[rows].astype(HALF)
            for share in (gate_share, up_share):
                target[j, :, column : column + share.shape[1]] = share[rows, :].astype(HALF)
                column += share.shape[1]


def dense_wgrad(core, copies, attended, branch, terms, gate_share, up_share):
    length, width = attended.shape
    columns = width + HEAD_DIM + gate_share.shape[1] + up_share.shape[1]
    part = (copies // 2, width // copies, columns)
    operands = (attended, branch, terms, gate_share, up_share)
    return pl.pallas_call(
        dense_wgrad_kernel,
        grid_spec=pltpu.PrefetchScalarGridSpec(
            num_scalar_prefetch=1,
            grid=(1,),
            in_specs=[whole_block(array.shape) for array in operands],
            out_specs=[whole_block(part)] * 2,
            scratch_shapes=[pltpu.VMEM((width, width + HEAD_DIM), FLOAT)],
        ),
        out_shape=[jax.ShapeDtypeStruct(part, HALF)] * 2,
        compiler_params=pltpu.CompilerParams(vmem_limit_bytes=VMEM_LIMIT),
        cost_estimate=pl.CostEstimate(
            flops=2 * length * width**2, bytes_accessed=2 * width * columns + 8 * length * width, transcendentals=0
        ),
        name="dense_wgrad",
    )(core, *operands)


def tokens_grad_kernel(own, forward, backward, spare_grad, weight, tokens, gain, hidden_grad, out):
    attn_in_grad = (
        own[...].astype(FLOAT)
        + forward[...].astype(FLOAT)
        + backward[...].astype(FLOAT)
        + matmul(spare_grad[...], weight[...], (1, 1))
    )
    normed, scale = scaled_rows(tokens[...].astype(FLOAT))
    out[...] = hidden_grad[...] + norm_grad(attn_in_grad, normed, scale, gain[...])


def input_grad(arrived, spare_grad, weight, tokens, gain, hidden_grad):
    length, width = tokens.shape
    return pl.pallas_call(
        tokens_grad_kernel,
        out_shape=jax.ShapeDtypeStruct((length, width), FLOAT),
        compiler_params=pltpu.CompilerParams(vmem_limit_bytes=VMEM_LIMIT),
        cost_estimate=pl.CostEstimate(
            flops=2 * length * width * weight.shape[1], bytes_accessed=16 * length * width, transcendentals=0
        ),
        name="tokens_grad",
    )(*arrived, spare_grad, weight, tokens, gain, hidden_grad)


def turn(values, cosine, sine):
    return values * cosine + pltpu.roll(values, HEAD_DIM // 2, 1) * sine


def head_slice(index):
    return slice(index * HEAD_DIM, (index + 1) * HEAD_DIM)


def start_all(copies):
    for copy in copies:
        copy.start()


def wait_all(copies):
    for copy in copies:
        copy.wait()


def pack_heads_kernel(spare, place_ref, query, key, value, out, sems):
    width = query.shape[1]
    own = pl.ds(pl.multiple_of(place_ref[0] * HEAD_DIM, HEAD_DIM), HEAD_DIM)
    rest = pl.ds(width - spare * HEAD_DIM, spare * HEAD_DIM)
    pieces = [
        (query, own, 1),
        (key, own, 1),
        (key, rest, spare),
        (value, own, 1),
        (value, rest, spare),
        (query, rest, spare),
    ]
    copies, tile = [], 0
    for i, (source, columns, tiles) in enumerate(pieces):
        target = out.at[:, pl.ds(tile * HEAD_DIM, tiles * HEAD_DIM)]
        copies.append(pltpu.make_async_copy(source.at[:, columns], target, sems.at[i]))
        tile += tiles
    start_all(copies)
    wait_all(copies)


def pack_heads(place, spare, query, key, value):
    width = query.shape[0]
    columns = (3 + 3 * spare) * HEAD_DIM
    anywhere = pl.BlockSpec(memory_space=pl.ANY)
    return pl.pallas_call(
        functools.partial(pack_heads_kernel, spare),
        grid_spec=pltpu.PrefetchScalarGridSpec(
            num_scalar_prefetch=1,
            grid=(1,),
            in_specs=[anywhere] * 3,
            out_specs=whole_block((width, columns)),
            scratch_shapes=[pltpu.SemaphoreType.DMA((6,))],
        ),
        out_shape=jax.ShapeDtypeStruct((width, columns), HALF),
        compiler_params=pltpu.CompilerParams(vmem_limit_bytes=VMEM_LIMIT),
        cost_estimate=pl.CostEstimate(flops=0, bytes_accessed=4 * width * columns, transcendentals=0),
        name="pack_heads",
    )(place, query, key, value)


def project_kernel(turned, tiles, chained, block_ref, *refs):
    x, gain, weight, cosine, sine = refs[:5]
    outs = refs[6 if chained else 5 :]
    outs[1][...] = (scaled_rows(x[...].astype(FLOAT))[0] * gain[...]).astype(HALF)
    lin = matmul(outs[1][...], weight[...], (1, 0))
    for tile in range(weight.shape[1] // HEAD_DIM):
        part = lin[:, head_slice(tile)]
        if tile < turned or tile >= tiles:
            part = turn(part, cosine[0], sine[0])
        if tile < tiles:
            outs[0][0, :, head_slice(tile)] = part.astype(HALF)
        else:
            outs[2][:, head_slice(tile - tiles)] = part.astype(HALF)


def project(blocks, slot, x, gain, weight, cosine, sine, turned, tiles, packed):
    length, width = x.shape
    count = cosine.shape[0]
    chained = packed is not None
    extra = 0 if chained else weight.shape[1] - tiles * HEAD_DIM
    columns = tiles * HEAD_DIM + extra
    table = pl.BlockSpec((1, length, HEAD_DIM), lambda i, b: (b[slot], 0, 0))
    packed_shape = (count, length, tiles * HEAD_DIM)
    out_specs = [
        pl.BlockSpec((1,) + packed_shape[1:], lambda i, b: (b[slot], 0, 0)),
        whole_block(x.shape),
    ]
    out_shape = [jax.ShapeDtypeStruct(packed_shape, HALF), jax.ShapeDtypeStruct(x.shape, HALF)]
    if extra:
        out_specs.append(whole_block((length, extra)))
        out_shape.append(jax.ShapeDtypeStruct((length, extra), HALF))
    return pl.pallas_call(
        functools.partial(project_kernel, turned, tiles, chained),
        grid_spec=pltpu.PrefetchScalarGridSpec(
            num_scalar_prefetch=1,
            grid=(1,),
            in_specs=[whole_block(x.shape), whole_block(gain.shape), whole_block((width, columns)), table, table]
            + ([pl.BlockSpec(memory_space=pl.ANY)] if chained else []),
            out_specs=out_specs,
        ),
        out_shape=out_shape,
        input_output_aliases={6: 0} if chained else {},
        compiler_params=pltpu.CompilerParams(vmem_limit_bytes=VMEM_LIMIT),
        cost_estimate=pl.CostEstimate(
            flops=2 * length * width * columns,
            bytes_accessed=2 * (length * width + (length + width) * columns),
            transcendentals=0,
        ),
        name="project",
    )(blocks, x, gain, weight, cosine, sine, *([packed] if chained else []))


EXP_SCALE = HEAD_DIM**-0.5 * 1.4426950408889634


def masked_scores(query, keys, first):
    scores = matmul(query, keys, (1, 1)) * EXP_SCALE
    row = lax.broadcasted_iota(jnp.int32, scores.shape, 0)
    column = lax.broadcasted_iota(jnp.int32, scores.shape, 1)
    return jnp.where(column <= row + first, scores, -1e30)


def attend(query, keys, values, first):
    scores = masked_scores(query, keys, first)
    peak = jnp.max(scores, axis=1, keepdims=True)
    shifted = jnp.exp2(scores - peak)
    total = jnp.sum(shifted, axis=1, keepdims=True)
    out = matmul(shifted.astype(HALF), values, (1, 0)) / total
    level = jnp.broadcast_to(peak + jnp.log2(total), (query.shape[0], HEAD_DIM))
    return out.astype(HALF), level


def attention_kernel(spare, place_ref, packed, spare_q, out, spare_out, level, spare_level):
    count, length = packed.shape[:2]
    keys_at, values_at = head_slice(1), head_slice(2 + spare)

    def rows(columns, blocks):
        return packed[:blocks, :, columns].reshape(blocks * length, HEAD_DIM)

    for block in range(count):
        out[block], level[block] = attend(
            packed[block, :, head_slice(0)],
            rows(keys_at, block + 1),
            rows(values_at, block + 1),
            block * length,
        )
    for head in range(spare):
        spare_out[:, head_slice(head)], spare_level[head] = attend(
            spare_q[:, head_slice(head)],
            rows(head_slice(2 + head), count),
            rows(head_slice(3 + spare + head), count),
            place_ref[0] * length,
        )


def attention(place, packed, spare_q):
    count, length, columns = packed.shape
    spare = spare_q.shape[1] // HEAD_DIM
    area = (count * (count + 1) // 2 + spare * count) * length * length
    shapes = [
        ((count, length, HEAD_DIM), HALF),
        (spare_q.shape, HALF),
        ((count, length, HEAD_DIM), FLOAT),
        ((spare, length, HEAD_DIM), FLOAT),
    ]
    return pl.pallas_call(
        functools.partial(attention_kernel, spare),
        grid_spec=pltpu.PrefetchScalarGridSpec(
            num_scalar_prefetch=1,
            grid=(1,),
            in_specs=[whole_block(packed.shape), whole_block(spare_q.shape)],
            out_specs=[whole_block(shape) for shape, _ in shapes],
        ),
        out_shape=[jax.ShapeDtypeStruct(shape, kind) for shape, kind in shapes],
        compiler_params=pltpu.CompilerParams(vmem_limit_bytes=VMEM_LIMIT),
        cost_estimate=pl.CostEstimate(
            flops=8 * area * HEAD_DIM, bytes_accessed=4 * count * length * columns, transcendentals=area
        ),
        name="attention",
    )(place, packed, spare_q)


def attend_back(query, keys, values, first, level, out, out_grad):
    scores = masked_scores(query, keys, first)
    probs = jnp.exp2(scores - level[:, :1])
    prob_grad = matmul(out_grad, values, (1, 1))
    shared = jnp.sum(out_grad.astype(FLOAT) * out.astype(FLOAT), axis=1, keepdims=True)
    score_grad = (probs * (prob_grad - shared)).astype(HALF)
    value_grad = matmul(probs.astype(HALF), out_grad, (0, 0))
    query_grad = matmul(score_grad, keys, (1, 0)) * HEAD_DIM**-0.5
    key_grad = matmul(score_grad, query, (0, 0)) * HEAD_DIM**-0.5
    return query_grad, key_grad, value_grad


def attention_back_kernel(
    spare, place_ref, packed, spare_q, out, spare_out, level, spare_level, out_grad, spare_out_grad,
    cosine, sine, grad, spare_grad, key_sum, value_sum
):
    count, length = packed.shape[:2]
    keys_at, values_at = head_slice(1), head_slice(2 + spare)

    def rows(columns, blocks):
        return packed[:blocks, :, columns].reshape(blocks * length, HEAD_DIM)

    key_sum[...] = jnp.zeros_like(key_sum)
    value_sum[...] = jnp.zeros_like(value_sum)
    for block in range(count):
        query_grad, key_grad, value_grad = attend_back(
            packed[block, :, head_slice(0)],
            rows(keys_at, block + 1),
            rows(values_at, block + 1),
            block * length,
            level[block],
            out[block],
            out_grad[block],
        )
        grad[block, :, head_slice(0)] = turn(query_grad, cosine[block], -sine[block]).astype(HALF)
        seen = (block + 1) * length
        key_sum[:seen] += key_grad
        value_sum[:seen] += value_grad

    def put(index, values, turned):
        for block in range(count):
            part = values[block * length : (block + 1) * length]
            if turned:
                part = turn(part, cosine[block], -sine[block])
            grad[block, :, head_slice(index)] = part.astype(HALF)

    put(1, key_sum[...], True)
    put(2 + spare, value_sum[...], False)
    place = place_ref[0]
    for head in range(spare):
        query_grad, key_grad, value_grad = attend_back(
            spare_q[:, head_slice(head)],
            rows(head_slice(2 + head), count),
            rows(head_slice(3 + spare + head), count),
            place * length,
            spare_level[head],
            spare_out[:, head_slice(head)],
            spare_out_grad[:, head_slice(head)],
        )
        spare_grad[:, head_slice(head)] = turn(query_grad, cosine[place], -sine[place]).astype(HALF)
        put(2 + head, key_grad, True)
        put(3 + spare + head, value_grad, False)


def attention_back(place, packed, spare_q, out, spare_out, level, spare_level, out_grad, spare_out_grad, cosine, sine):
    count, length, columns = packed.shape
    spare = spare_q.shape[1] // HEAD_DIM
    area = (count * (count + 1) // 2 + spare * count) * length * length
    operands = (packed, spare_q, out, spare_out, level, spare_level, out_grad, spare_out_grad, cosine, sine)
    return pl.pallas_call(
        functools.partial(attention_back_kernel, spare),
        grid_spec=pltpu.PrefetchScalarGridSpec(
            num_scalar_prefetch=1,
            grid=(1,),
            in_specs=[whole_block(array.shape) for array in operands],
            out_specs=[whole_block(packed.shape), whole_block(spare_q.shape)],
            scratch_shapes=[pltpu.VMEM((count * length, HEAD_DIM), FLOAT)] * 2,
        ),
        out_shape=[jax.ShapeDtypeStruct(packed.shape, HALF), jax.ShapeDtypeStruct(spare_q.shape, HALF)],
        compiler_params=pltpu.CompilerParams(vmem_limit_bytes=VMEM_LIMIT),
        cost_estimate=pl.CostEstimate(
            flops=20 * area * HEAD_DIM, bytes_accessed=8 * count * length * columns, transcendentals=area
        ),
        name="attention_back",
    )(place, *operands)


def part_kernel(slots, blocks_ref, grad, weight, *outs):
    for slot, out in zip(slots, outs):
        out[...] = matmul(grad[blocks_ref[slot]], weight[...], (1, 1)).astype(HALF)


def attn_parts(blocks, slots, grad, weight):
    length, columns = grad.shape[1:]
    width = weight.shape[0]
    count = len(slots)
    return pl.pallas_call(
        functools.partial(part_kernel, slots),
        grid_spec=pltpu.PrefetchScalarGridSpec(
            num_scalar_prefetch=1,
            grid=(1,),
            in_specs=[whole_block(grad.shape), whole_block((width, columns))],
            out_specs=[whole_block((length, width))] * count,
        ),
        out_shape=[jax.ShapeDtypeStruct((length, width), HALF)] * count,
        compiler_params=pltpu.CompilerParams(vmem_limit_bytes=VMEM_LIMIT),
        cost_estimate=pl.CostEstimate(
            flops=2 * count * length * width * columns,
            bytes_accessed=2 * (count * length + columns) * width,
            transcendentals=0,
        ),
        name="attn_parts",
    )(blocks, grad, weight)


def attn_wgrad_kernel(count, blocks_ref, core_ref, *refs):
    slots, own, grad, spare_grad = refs[:count], refs[count], refs[count + 1], refs[count + 2]
    kept, sent, rows, total, sems = refs[count + 3 :]
    length = own.shape[0]
    copies = [
        pltpu.make_async_copy(
            slot, rows.at[pl.ds(pl.multiple_of(blocks_ref[i] * length, length), length)], sems.at[i]
        )
        for i, slot in enumerate(slots)
    ]
    for copy in copies:
        copy.start()
    columns = grad.shape[2]
    total[:, columns:] = matmul(own[...], spare_grad[...], (0, 0))
    for copy in copies:
        copy.wait()
    total[:, :columns] = matmul(rows[...], grad[...].reshape(count * length, columns), (0, 0))
    size = kept.shape[1]
    for j in range(kept.shape[0]):
        for target, parity in ((kept, core_ref[0]), (sent, 1 - core_ref[0])):
            start = pl.multiple_of((2 * j + parity) * size, 8)
            target[j] = total[pl.ds(start, size)].astype(HALF)


def attn_wgrad(blocks, core, copies, slots, grad, spare_grad):
    length, width = slots[0].shape
    count, _, columns = grad.shape
    wide = columns + spare_grad.shape[1]
    part = (copies // 2, width // copies, wide)
    return pl.pallas_call(
        functools.partial(attn_wgrad_kernel, count),
        grid_spec=pltpu.PrefetchScalarGridSpec(
            num_scalar_prefetch=2,
            grid=(1,),
            in_specs=[pl.BlockSpec(memory_space=pl.ANY)] * count
            + [whole_block(slots[0].shape), whole_block(grad.shape), whole_block(spare_grad.shape)],
            out_specs=[whole_block(part)] * 2,
            scratch_shapes=[
                pltpu.VMEM((count * length, width), HALF),
                pltpu.VMEM((width, wide), FLOAT),
                pltpu.SemaphoreType.DMA((count,)),
            ],
        ),
        out_shape=[jax.ShapeDtypeStruct(part, HALF)] * 2,
        compiler_params=pltpu.CompilerParams(vmem_limit_bytes=VMEM_LIMIT),
        cost_estimate=pl.CostEstimate(
            flops=2 * count * length * width * wide,
            bytes_accessed=2 * (count * length + wide) * width,
            transcendentals=0,
        ),
        name="attn_wgrad",
    )(blocks, core, *slots, slots[0], grad, spare_grad)


def on_device(
    tokens,
    routes,
    gates,
    attn_gain,
    query_weight,
    key_weight,
    value_weight,
    output_weight,
    ffn_gain,
    shared_gate,
    shared_up,
    shared_down,
    expert_gate,
    expert_up,
    expert_down,
    cotangent,
):
    length, width = tokens.shape
    hidden_units = expert_gate.shape[2]
    local_experts = expert_gate.shape[0]
    group = lax.axis_size("narrow")
    copies = lax.axis_size("wide")
    place = lax.axis_index("narrow")
    experts = group * local_experts
    seq_len = length * group
    own_heads = group * HEAD_DIM
    spare_heads = width // HEAD_DIM - group

    order = jnp.asarray(ring_order(group), dtype=jnp.int32)
    ring_place = jnp.where(place % 2 == 0, place // 2, group - 1 - place // 2)
    slot_block = order[(ring_place + jnp.arange(group, dtype=jnp.int32)) % group]
    attn_gain_row = attn_gain.astype(FLOAT).reshape(1, width)
    ffn_gain_row = ffn_gain.astype(FLOAT).reshape(1, width)
    core = (lax.axis_index("wide") % 2).astype(jnp.int32).reshape(1)

    own_place = place.astype(jnp.int32).reshape(1)
    packed_weight = pack_heads(own_place, spare_heads, query_weight, key_weight, value_weight)
    spare_query_weight = query_weight[:, own_heads:]
    turned, tiles = 2 + spare_heads, 3 + 2 * spare_heads
    half = HEAD_DIM // 2
    freq = 10000.0 ** (-(jnp.arange(half, dtype=FLOAT) * 2.0) / HEAD_DIM)
    angles = jnp.arange(seq_len, dtype=FLOAT)[:, None] * freq[None, :]
    cosine, sine = jnp.cos(angles), jnp.sin(angles)
    cosine = jnp.concatenate([cosine, cosine], axis=1).reshape(group, length, HEAD_DIM)
    sine = jnp.concatenate([-sine, sine], axis=1).reshape(group, length, HEAD_DIM)

    share = hidden_units // (copies * group)
    per_expert = -(-(hidden_units + copies * share) // CHUNK) * CHUNK
    gap = per_expert - hidden_units
    spacing = gap // copies
    column = jnp.arange(gap, dtype=jnp.int32)
    unit = jnp.where(
        column % spacing < share,
        ((column // spacing) * group + place) * share + column % spacing,
        -1,
    )
    choice = (jnp.arange(hidden_units, dtype=jnp.int32)[:, None] == unit[None, :]).astype(HALF)

    heads = {}
    attn_slots = [None] * group

    def project_slot(slot, x):
        result = project(
            slot_block,
            slot,
            x,
            attn_gain_row,
            packed_weight,
            cosine,
            sine,
            turned,
            tiles,
            heads.get("packed"),
        )
        heads["packed"], attn_slots[slot] = result[:2]
        if slot == 0:
            heads["spare"] = result[2]

    def project_slots(step, slots):
        for slot in (step, group - step) if step else (0,):
            project_slot(slot, slots[slot])
        if step == 1:
            expert_ids = jnp.arange(experts, dtype=jnp.int32)
            picked = after(routes, slots[1])[:, :, None] == expert_ids[None, None, :]
            token_gate = jnp.sum(jnp.where(picked, gates[:, :, None], 0.0), axis=1)
            arrived = lax.all_to_all(
                token_gate.T.reshape(group, local_experts, length),
                "narrow",
                split_axis=0,
                concat_axis=0,
                tiled=True,
            )
            heads["gates"] = arrived.transpose(0, 2, 1)
        return (heads["packed"],)

    half_ring = group // 2
    token_slots = ring_gather(tokens, project_slots)
    cot_slots = ring_gather(after(cotangent, token_slots[half_ring]))
    project_slot(half_ring, token_slots[half_ring])
    packed_heads, spare_q, own_gates = heads["packed"], heads["spare"], heads["gates"]
    own_out, spare_out, level, spare_level = attention(own_place, packed_heads, spare_q)
    returned = lax.all_to_all(own_out, "narrow", split_axis=0, concat_axis=0, tiled=True)
    gate_weight, up_weight, down_weight = pack_experts(
        per_expert,
        *after((choice, shared_gate, shared_up, shared_down, expert_gate, expert_up, expert_down), own_out),
    )
    hidden, attended, ffn_in = mix(returned, spare_out, output_weight, tokens, ffn_gain_row)

    batches = [(0,), (1, group - 1), (2,), (half_ring, half_ring + 1), (half_ring - 1, half_ring + 2)]
    row_order = [slot for batch in batches if len(batch) == 2 for slot in batch]
    row_order += [slot for batch in batches if len(batch) == 1 for slot in batch]
    rows_state = {"kept": None}
    out_parts, row_parts = [None] * group, [None] * group

    def expert_batch(batch, slots):
        result = expert_rows(
            hidden_units,
            batch,
            row_order.index(batch[0]) * length,
            seq_len,
            rows_state["kept"],
            slot_block,
            [slots[j] for j in batch],
            [cot_slots[j] for j in batch],
            own_gates,
            gate_weight,
            up_weight,
            down_weight,
        )
        rows_state["kept"] = result[:3]
        for i, j in enumerate(batch):
            out_parts[j] = result[3 + i]
            row_parts[j] = result[3 + len(batch) + i]
        return tuple(result[3:])

    ffn_slots = ring_gather(
        ffn_in, lambda step, slots: expert_batch(batches[step], slots) if step < 3 else ()
    )
    expert_batch(batches[3], ffn_slots)
    row_sum, out_sum = RingSum(row_parts), RingSum(out_parts)
    row_first = row_sum.hop()
    out_sum.hop()
    expert_batch(batches[4], ffn_slots)
    gated_inner, gate_grad, up_grad = rows_state["kept"]
    ordered_cots = [cot_slots[j] for j in row_order]
    ordered_rows = [ffn_slots[j] for j in row_order]
    row_sum.add()
    row_second = row_sum.hop()
    down_kept, down_sent = out_grad(
        hidden_units, local_experts, copies, core, ordered_cots, after(gated_inner, *row_first)
    )
    down_got = wide_first(down_sent)
    row_sum.add()
    row_sum.hop(down_kept)
    gate_kept, gate_sent, gate_share = in_grad(
        hidden_units, local_experts, copies, core, ordered_rows, after(gate_grad, *row_second)
    )
    gate_got = wide_first(gate_sent)
    row_sum.add()
    row_last = row_sum.hop(gate_kept)

    hidden_grad, branch_grad, out_grads, spare_out_grad, gain_terms = back(
        row_sum.last(), hidden, cotangent, ffn_gain_row, output_weight, group
    )
    out_sum.add()
    out_sum.hop(*row_last)
    own_out_grad = lax.all_to_all(out_grads, "narrow", split_axis=0, concat_axis=0, tiled=True)
    up_kept, up_sent, up_share = in_grad(
        hidden_units, local_experts, copies, core, ordered_rows, after(up_grad, out_grads)
    )
    up_got = wide_first(up_sent)
    down_terms = wide_rest(*after((down_kept, down_got), out_grads))
    gate_terms = wide_rest(*after((gate_kept, gate_got), up_kept))
    dense_kept, dense_sent = dense_wgrad(
        core, copies, attended, branch_grad, gain_terms, gate_share, up_share
    )
    dense_got = wide_first(dense_sent)
    out_sum.add()
    out_sum.hop(own_out_grad)
    head_grad, spare_query_grad = attention_back(
        own_place,
        packed_heads,
        spare_q,
        own_out,
        spare_out,
        level,
        spare_level,
        own_out_grad,
        spare_out_grad,
        cosine,
        sine,
    )
    attn_part = [None] * group

    def attn_batch(slots, grad):
        for j, part in zip(slots, attn_parts(slot_block, slots, grad, packed_weight)):
            attn_part[j] = part

    attn_batch((half_ring, half_ring + 1), head_grad)
    attn_sum = RingSum(attn_part)
    attn_first = attn_sum.hop()
    attn_kept, attn_sent = attn_wgrad(
        slot_block, core, copies, attn_slots, after(head_grad, *attn_part[half_ring : half_ring + 2]), spare_query_grad
    )
    attn_got = wide_first(attn_sent)
    attn_batch((half_ring - 1, half_ring + 2), after(head_grad, attn_kept))
    attn_sum.add()
    attn_second = attn_sum.hop()
    rest = tuple(j for j in range(group) if attn_part[j] is None)
    attn_batch(rest, after(head_grad, *attn_first))
    attn_terms = wide_rest(*after((attn_kept, attn_got), attn_part[rest[0]]))
    dense_terms = wide_rest(*after((dense_kept, dense_got), head_grad))
    up_terms = wide_rest(*after((up_kept, up_got), head_grad))
    out_sum.add()
    out_sum.hop(*attn_first)
    attn_sum.add()
    attn_third = attn_sum.hop(attn_part[rest[0]])
    attn_sum.add()
    attn_last = attn_sum.hop()
    tokens_grad = input_grad(
        attn_sum.last(), spare_query_grad, spare_query_weight, tokens, attn_gain_row, hidden_grad
    )
    mixed = (hidden + sum(part.astype(FLOAT) for part in out_sum.last())).astype(HALF)
    down_total = wide_total(after(down_terms, *attn_first))
    expert_down_grad = down_total[: -spacing].reshape(local_experts, hidden_units // copies, width)
    shared_down_grad = down_total[-spacing:][:share]
    expert_gate_grad = wide_total(after(gate_terms, *attn_second))
    expert_up_grad = wide_total(after(up_terms, *attn_third))

    def exchange(part):
        return lax.all_to_all(
            part.reshape(group, part.shape[0] // group, part.shape[1]),
            "narrow",
            split_axis=0,
            concat_axis=0,
            tiled=True,
        )

    first = exchange(wide_total(after(dense_terms, *attn_second)).astype(HALF))
    summed = jnp.sum(first[:, :, : width + 128].astype(FLOAT), axis=0)
    output_weight_grad = summed[:, :width]
    ffn_gain_grad = summed[:, width]

    spot = jnp.arange(group * gap, dtype=jnp.int32)
    spot_column = spot % gap
    spot_unit = jnp.where(
        spot_column % spacing < share,
        ((spot_column // spacing) * group + spot // gap) * share + spot_column % spacing,
        -1,
    )
    to_units = (spot_unit[:, None] == jnp.arange(hidden_units, dtype=jnp.int32)[None, :]).astype(HALF)
    to_units = to_units.reshape(group, gap, hidden_units)

    def shared_columns(part):
        return jnp.einsum("grc,gcu->ru", part, to_units, preferred_element_type=FLOAT)

    shared_gate_grad = shared_columns(first[:, :, width + 128 : width + 128 + gap])
    shared_up_grad = shared_columns(first[:, :, width + 128 + gap :])

    second = exchange(wide_total(attn_terms).astype(HALF)).astype(FLOAT)
    packed_sum = jnp.sum(second, axis=0)
    spare_width = spare_heads * HEAD_DIM

    def head_grads(own_tile, spare_tile):
        own = second[:, :, head_slice(own_tile)]
        own = own.transpose(1, 0, 2).reshape(own.shape[1], own_heads)
        first = spare_tile * HEAD_DIM
        return jnp.concatenate([own, packed_sum[:, first : first + spare_width]], axis=1)

    query_weight_grad = head_grads(0, tiles)
    key_weight_grad = head_grads(1, 2)
    value_weight_grad = head_grads(turned, turned + 1)
    own_rows = width // (copies * group)
    first_row = (lax.axis_index("wide") * group + place) * own_rows

    def own_part(array):
        return lax.dynamic_slice_in_dim(array, first_row, own_rows, axis=0).astype(FLOAT)

    attn_gain_grad = (
        jnp.sum(
            query_weight_grad * own_part(query_weight)
            + key_weight_grad * own_part(key_weight)
            + value_weight_grad * own_part(value_weight),
            axis=1,
        )
        / own_part(attn_gain)
    )
    return (
        mixed,
        tokens_grad,
        attn_gain_grad,
        query_weight_grad,
        key_weight_grad,
        value_weight_grad,
        output_weight_grad,
        ffn_gain_grad,
        shared_gate_grad,
        shared_up_grad,
        shared_down_grad,
        expert_gate_grad,
        expert_up_grad,
        expert_down_grad,
    )


def solution(mesh):
    rows = P(("wide", "narrow"), None)
    vector = P(("wide", "narrow"))
    held = P("narrow", None, None)
    in_specs = (rows, rows, rows) + (P(),) * 9 + (held, held, held, rows)
    out_specs = (rows, rows, vector) + (rows,) * 4 + (vector,) + (rows,) * 3 + (P("narrow", "wide", None),) * 3
    return jax.shard_map(
        on_device, mesh=mesh, in_specs=in_specs, out_specs=out_specs, check_vma=False
    )
```

```python
import functools

import jax
import jax.numpy as jnp
import numpy as np
from jax import lax
from jax.experimental import pallas as pl
from jax.experimental.pallas import tpu as pltpu
from jax.sharding import PartitionSpec as P

HEAD_DIM = 128
EPS = 1e-06
FLOAT = jnp.float32
HALF = jnp.bfloat16


def matmul(a, b, contract):
    return lax.dot_general(a, b, ((contract[:1], contract[1:]), ((), ())), preferred_element_type=FLOAT)


def ring_order(count):
    return list(range(0, count, 2)) + list(range(count - 1, 0, -2))


def ring_steps(count):
    order = ring_order(count)
    ahead = [(order[i], order[(i + 1) % count]) for i in range(count)]
    back = [(b, a) for a, b in ahead]
    return ahead, back


def after(value, *others):
    return lax.optimization_barrier((value, others))[0]


class RingGather:
    def __init__(self, block, mirrored=False):
        count = lax.axis_size("narrow")
        self.half = count // 2
        self.mirrored = mirrored
        self.step = 0
        self.slots = [block] + [None] * (count - 1)

    def hop(self, *others):
        count = len(self.slots)
        ahead, back = ring_steps(count)
        forward, backward = after((self.slots[-self.step], self.slots[self.step]), *others)
        self.step += 1
        arrived = []
        if self.step < self.half or not self.mirrored:
            arrived.append(lax.ppermute(forward, "narrow", ahead))
            self.slots[count - self.step] = arrived[-1]
        if self.step < self.half or self.mirrored:
            arrived.append(lax.ppermute(backward, "narrow", back))
            self.slots[self.step] = arrived[-1]
        return arrived


class RingSum:
    def __init__(self, parts, mirrored=False):
        self.mirrored = mirrored
        self.parts = parts
        self.half = len(parts) // 2
        self.step = 0
        self.forward, self.backward = self.part(self.half), self.part(self.half + 1)

    def part(self, offset):
        return self.parts[-offset if self.mirrored else offset]

    def hop(self, *others):
        ahead, back = ring_steps(len(self.parts))
        if self.mirrored:
            ahead, back = back, ahead
        self.step += 1
        if self.step == self.half:
            self.forward = lax.ppermute(after(self.forward, *others), "narrow", ahead)
            return [self.forward]
        forward, backward = after((self.forward, self.backward), *others)
        self.forward = lax.ppermute(forward, "narrow", ahead)
        self.backward = lax.ppermute(backward, "narrow", back)
        return [self.forward, self.backward]

    def add(self, *deps):
        return add_rings([self], *deps)

    def terms(self):
        arrived = [self.forward]
        own = [self.part(self.half - self.step)]
        if self.step < self.half - 1:
            arrived.append(self.backward)
            own.append(self.part(self.half + 1 + self.step))
        return arrived, own

    def last(self):
        return self.parts[0], self.forward, self.backward


def add_rings(rings, *deps):
    arrived, own = [], []
    for ring in rings:
        ring_arrived, ring_own = ring.terms()
        arrived += ring_arrived
        own += ring_own
    sums = launch_whole(
        functools.partial(add_kernel, len(own)),
        arrived + own,
        [(own[0].shape, HALF)] * len(own),
        "add_pairs",
        deps=deps,
    )
    left = list(sums)
    for ring in rings:
        ring.forward = left.pop(0)
        if ring.step < ring.half - 1:
            ring.backward = left.pop(0)
    return list(sums)


def add_kernel(count, *refs):
    for i in range(count):
        total = refs[i][...].astype(FLOAT) + refs[count + i][...].astype(FLOAT)
        refs[2 * count + i][...] = total.astype(HALF)


def wide_first(sent):
    count = lax.axis_size("wide")
    return lax.ppermute(sent, "wide", [(i, i ^ 1) for i in range(count)])


def wide_swap(sent, bit):
    count = lax.axis_size("wide")
    return lax.ppermute(sent, "wide", [(i, i ^ bit) for i in range(count)])


def sum_kernel(count, kind, place_ref, *refs):
    total = refs[0][...].astype(FLOAT)
    for ref in refs[1:count]:
        total += ref[...].reshape(total.shape).astype(FLOAT)
    refs[count][...] = total.reshape(refs[count].shape).astype(kind)


def sum_halves(halved, others, index, kind, *deps):
    rest = halved[0].shape[1:]
    pairs = halved[0].shape[0] // 2
    shape = (pairs,) + rest
    operands = [array.reshape((pairs, 2) + rest) for array in halved] + list(others)
    half_block = pl.BlockSpec((pairs, 1) + rest, lambda i, p: (0, p[0]) + (0,) * len(rest))
    return launch(
        functools.partial(sum_kernel, len(operands), kind),
        operands,
        [half_block] * len(halved) + [whole_block(shape)] * len(others),
        whole_block(shape),
        jax.ShapeDtypeStruct(shape, kind),
        "sum_halves",
        prefetch=[index],
        deps=deps,
        moved=sum(array.size for array in operands),
    )


def wide_rest(kept, got, *deps, sent=None):
    bit, others = 2, []
    halved = [kept, got]
    while True:
        mine = ((lax.axis_index("wide") // bit) % 2).astype(jnp.int32).reshape(1)
        if sent is None or bit > 2:
            sent = sum_halves(halved, others, 1 - mine, HALF, *deps)
        arrived = wide_swap(sent, bit)
        if 2 * bit == lax.axis_size("wide"):
            return sent, arrived, (halved, [arrived], mine)
        halved = [sum_halves(halved, [], mine, HALF), arrived]
        bit *= 2


def widen_out_kernel(rows, source, experts, shared):
    total = source[...].astype(FLOAT)
    for e in range(experts.shape[0]):
        experts[e] = total[e * rows : (e + 1) * rows]
    first = experts.shape[0] * rows
    shared[...] = total[first : first + shared.shape[0]]


def widen_out(source, experts, rows, share, *deps):
    width = source.shape[1]
    return launch_whole(
        functools.partial(widen_out_kernel, rows),
        [source],
        [((experts, rows, width), FLOAT), ((share, width), FLOAT)],
        "widen_out",
        deps=deps,
    )


def finish_dense_kernel(parts, to_units, out, gain, gate, up):
    group = parts.shape[0]
    width = out.shape[1]
    total = parts[0, :, : width + HEAD_DIM].astype(FLOAT)
    for g in range(1, group):
        total += parts[g, :, : width + HEAD_DIM].astype(FLOAT)
    out[...] = total[:, :width]
    gain[...] = total[:, width:]
    column = width + HEAD_DIM
    gap = to_units.shape[1]
    for share in (gate, up):
        share[...] = sum(
            matmul(parts[g, :, column : column + gap], to_units[g], (1, 0)) for g in range(group)
        )
        column += gap


def finish_dense(parts, to_units, width):
    rows, units = parts.shape[1], to_units.shape[2]
    shapes = [(rows, width), (rows, HEAD_DIM), (rows, units), (rows, units)]
    return launch_whole(
        finish_dense_kernel, [parts, to_units], [(shape, FLOAT) for shape in shapes], "finish_dense"
    )


def finish_attn_kernel(spare, parts, *refs):
    weights, grads, gain = refs[:3], refs[3:6], refs[6]
    group = parts.shape[0]
    total = 0.0
    tiles = ((0, 3 + 2 * spare), (1, 2), (2 + spare, 3 + spare))
    for weight, grad, (own, first) in zip(weights, grads, tiles):
        for g in range(group):
            grad[:, head_slice(g)] = parts[g, :, head_slice(own)].astype(FLOAT)
        columns = slice(first * HEAD_DIM, (first + spare) * HEAD_DIM)
        grad[:, group * HEAD_DIM :] = sum(
            parts[g, :, columns].astype(FLOAT) for g in range(group)
        )
        total += jnp.sum(grad[...] * weight[...].astype(FLOAT), axis=1, keepdims=True)
    gain[...] = jnp.broadcast_to(total, gain.shape)


def finish_attn(spare, parts, weights):
    rows, width = weights[0].shape
    shapes = [(rows, width)] * 3 + [(rows, HEAD_DIM)]
    return launch_whole(
        functools.partial(finish_attn_kernel, spare),
        [parts, *weights],
        [(shape, FLOAT) for shape in shapes],
        "finish_attn",
    )


def widen_kernel(source, target):
    target[...] = source[...].astype(FLOAT)


def widen(array, *deps):
    return launch_whole(widen_kernel, [array], [(array.shape, FLOAT)], "widen", deps=deps)[0]


VMEM_LIMIT = 60 * 2**20
CHUNK = 512


def whole_block(shape):
    return pl.BlockSpec(shape, lambda *_: (0,) * len(shape))


ANYWHERE = pl.BlockSpec(memory_space=pl.ANY)


def launch(
    kernel, operands, in_specs, out_specs, out_shape, name, prefetch=(), deps=(), through=(), grid=(1,), scratch=(), aliases=None, flops=0, moved=0
):
    inputs = len(prefetch) + len(operands)
    idle = len(deps) + len(through)
    aliases = dict(aliases or {})
    if through:
        out_specs, out_shape = list(out_specs), list(out_shape)
        for i, array in enumerate(through):
            aliases[inputs + len(deps) + i] = len(out_shape)
            out_specs.append(ANYWHERE)
            out_shape.append(jax.ShapeDtypeStruct(array.shape, array.dtype))

    def body(*refs):
        results = refs[inputs + idle : len(refs) - len(scratch)]
        own = results[: len(results) - len(through)]
        kernel(*refs[:inputs], *own, *refs[len(refs) - len(scratch) :])

    return pl.pallas_call(
        body,
        grid_spec=pltpu.PrefetchScalarGridSpec(
            num_scalar_prefetch=len(prefetch),
            grid=grid,
            in_specs=list(in_specs) + [ANYWHERE] * idle,
            out_specs=out_specs,
            scratch_shapes=list(scratch),
        ),
        out_shape=out_shape,
        input_output_aliases=aliases,
        compiler_params=pltpu.CompilerParams(vmem_limit_bytes=VMEM_LIMIT),
        cost_estimate=pl.CostEstimate(flops=int(flops), bytes_accessed=int(moved), transcendentals=0),
        name=name,
    )(*prefetch, *operands, *deps, *through)


def launch_whole(kernel, operands, shapes, name, **options):
    moved = sum(array.size * array.dtype.itemsize for array in operands)
    return launch(
        kernel,
        operands,
        [whole_block(array.shape) for array in operands],
        [whole_block(shape) for shape, _ in shapes],
        [jax.ShapeDtypeStruct(shape, kind) for shape, kind in shapes],
        name,
        moved=moved,
        **options,
    )


def rows_kernel(slots, units, chained, blocks_ref, *refs):
    count = len(slots)
    xs, cs, gates = refs[:count], refs[count : 2 * count], refs[2 * count]
    gate_w, up_w, down_w = refs[2 * count + 1 : 2 * count + 4]
    outs = refs[2 * count + 4 + (3 if chained else 0) :]
    inner, gate_g, up_g = outs[:3]
    ys, ds = outs[3 : 3 + count], outs[3 + count : 3 + 2 * count]
    y_sum, d_sum, x_rows, c_rows = outs[3 + 2 * count :]
    step = pl.program_id(0)
    length = xs[0].shape[0]
    chunk = gate_w.shape[1]
    per_expert = pl.num_programs(0) // gates.shape[2]

    @pl.when(step == 0)
    def _():
        for i in range(count):
            x_rows[i * length : (i + 1) * length] = xs[i][...]
            c_rows[i * length : (i + 1) * length] = cs[i][...]
        y_sum[...] = jnp.zeros_like(y_sum)
        d_sum[...] = jnp.zeros_like(d_sum)

    x, c = x_rows[...], c_rows[...]
    expert = step // per_expert
    column = (step % per_expert) * chunk + lax.broadcasted_iota(
        jnp.int32, (count * length, chunk), 1
    )
    picked = []
    for slot in slots:
        gate = gates[blocks_ref[slot]]
        own = gate[:, 0:1]
        for e in range(1, gate.shape[1]):
            own = jnp.where(expert == e, gate[:, e : e + 1], own)
        picked.append(own)
    scale = jnp.where(column < units, jnp.concatenate(picked, axis=0), 1.0)
    gate_pre = matmul(x, gate_w[...], (1, 0))
    up_pre = matmul(x, up_w[...], (1, 0))
    inner_grad = matmul(c, down_w[...], (1, 1)) * scale
    sigma = 0.5 * jnp.tanh(0.5 * gate_pre) + 0.5
    active = gate_pre * sigma
    inner[...] = (active * up_pre * scale).astype(HALF)
    gate_g[...] = (inner_grad * up_pre * (sigma + active * (1.0 - sigma))).astype(HALF)
    up_g[...] = (inner_grad * active).astype(HALF)
    y_sum[...] += matmul(inner[...], down_w[...], (1, 0))
    d_sum[...] += matmul(gate_g[...], gate_w[...], (1, 1)) + matmul(up_g[...], up_w[...], (1, 1))

    @pl.when(step == pl.num_programs(0) - 1)
    def _():
        for i in range(count):
            ys[i][...] = y_sum[i * length : (i + 1) * length].astype(HALF)
            ds[i][...] = d_sum[i * length : (i + 1) * length].astype(HALF)


def expert_rows(units, slots, place, total, kept, blocks, xs, cs, gates, gate_w, up_w, down_w, deps):
    count = len(xs)
    length, width = xs[0].shape
    padded = gate_w.shape[1]
    rows = count * length
    column_block = pl.BlockSpec((width, CHUNK), lambda f, b: (0, f))
    row_block = pl.BlockSpec((CHUNK, width), lambda f, b: (f, 0))
    kept_block = pl.BlockSpec((rows, CHUNK), lambda f, b: (place // rows, f))
    chained = kept is not None
    first_kept = 1 + 2 * count + 4
    return launch(
        functools.partial(rows_kernel, slots, units, chained),
        [*xs, *cs, gates, gate_w, up_w, down_w, *(kept if chained else ())],
        [whole_block(xs[0].shape)] * (2 * count)
        + [whole_block(gates.shape), column_block, column_block, row_block]
        + [ANYWHERE] * (3 if chained else 0),
        [kept_block] * 3 + [whole_block(xs[0].shape)] * (2 * count),
        [jax.ShapeDtypeStruct((total, padded), HALF)] * 3
        + [jax.ShapeDtypeStruct(xs[0].shape, HALF)] * (2 * count),
        "expert_rows",
        prefetch=[blocks],
        deps=deps,
        grid=(padded // CHUNK,),
        scratch=[pltpu.VMEM((rows, width), FLOAT)] * 2 + [pltpu.VMEM((rows, width), HALF)] * 2,
        aliases={first_kept + i: i for i in range(3)} if chained else {},
        flops=12 * rows * width * padded,
        moved=6 * width * padded + 6 * rows * padded + 8 * rows * width,
    )


def pack_in_kernel(units, choice, shared, weights, out, sems):
    experts = weights.shape[0]
    per_expert = out.shape[1] // experts
    copies = [
        pltpu.make_async_copy(weights.at[e], out.at[:, pl.ds(e * per_expert, units)], sems.at[e])
        for e in range(experts)
    ]
    start_all(copies)
    for e in range(experts):
        gap = slice(e * per_expert + units, (e + 1) * per_expert)
        if e == 0:
            out[:, gap] = matmul(shared[...], choice[...], (1, 0)).astype(HALF)
        else:
            out[:, gap] = jnp.zeros((out.shape[0], per_expert - units), HALF)
    wait_all(copies)


def pack_out_kernel(units, choice, shared, weights, out, sems):
    experts = weights.shape[0]
    per_expert = out.shape[0] // experts
    copies = [
        pltpu.make_async_copy(weights.at[e], out.at[pl.ds(e * per_expert, units)], sems.at[e])
        for e in range(experts)
    ]
    start_all(copies)
    for e in range(experts):
        gap = slice(e * per_expert + units, (e + 1) * per_expert)
        if e == 0:
            out[gap] = matmul(choice[...], shared[...], (0, 0)).astype(HALF)
        else:
            out[gap] = jnp.zeros((per_expert - units, out.shape[1]), HALF)
    wait_all(copies)


def pack_experts(kernel, units, shape, choice, shared, weights, *deps):
    return launch(
        functools.partial(kernel, units),
        [choice, shared, weights],
        [whole_block(choice.shape), whole_block(shared.shape), ANYWHERE],
        whole_block(shape),
        jax.ShapeDtypeStruct(shape, HALF),
        "pack_experts",
        deps=deps,
        scratch=[pltpu.SemaphoreType.DMA((weights.shape[0],))],
        moved=4 * shape[0] * shape[1],
    )


def fetch_rows(slots, rows, sems):
    length = slots[0].shape[0]
    copies = [
        pltpu.make_async_copy(slot, rows.at[pl.ds(i * length, length)], sems.at[i])
        for i, slot in enumerate(slots)
    ]
    for copy in copies:
        copy.start()
    for copy in copies:
        copy.wait()


def in_grad_kernel(count, units, split, *refs):
    core_ref, slots, grad = refs[0], refs[1 : 1 + count], refs[1 + count]
    outs, (share, rows, total, sems) = refs[2 + count : -4], refs[-4:]
    step = pl.program_id(0)
    chunk = grad.shape[1]
    per_expert = -(-units // chunk)

    @pl.when(step == 0)
    def _():
        fetch_rows(slots, rows, sems)

    total[...] = matmul(rows[...], grad[...], (0, 0))
    size = outs[0].shape[2]

    def copy_rows(columns):
        own = slice(0, columns.stop - columns.start)
        if not split:
            for i in range(outs[0].shape[0]):
                outs[0][i, 0, :, columns] = total[i * size : (i + 1) * size, own].astype(HALF)
            return
        for j in range(outs[0].shape[0]):
            for target, parity in zip(outs, (core_ref[0], 1 - core_ref[0])):
                start = pl.multiple_of((2 * j + parity) * size, 8)
                target[j, 0, :, columns] = total[pl.ds(start, size), own].astype(HALF)

    for part in range(per_expert):

        @pl.when(step % per_expert == part)
        def _():
            copy_rows(slice(part * chunk, min((part + 1) * chunk, units)))

    @pl.when(step == per_expert - 1)
    def _():
        share[...] = total[:, units - (per_expert - 1) * chunk :]


def in_grad(units, experts, copies, core, split, slots, grad, *deps):
    length, width = slots[0].shape
    total, padded = grad.shape
    per_expert = padded // experts // CHUNK
    share = padded // experts - units
    parts = 2 if split else 1
    shape = (copies // parts, experts, width // copies, units)
    block = pl.BlockSpec((shape[0], 1) + shape[2:], lambda f, c: (0, f // per_expert, 0, 0))
    return launch(
        functools.partial(in_grad_kernel, len(slots), units, split),
        [*slots, grad],
        [ANYWHERE] * len(slots) + [pl.BlockSpec((total, CHUNK), lambda f, c: (0, f))],
        [block] * parts + [whole_block((width, share))],
        [jax.ShapeDtypeStruct(shape, HALF)] * parts + [jax.ShapeDtypeStruct((width, share), FLOAT)],
        "expert_in_grad",
        prefetch=[core],
        deps=deps,
        grid=(padded // CHUNK,),
        scratch=[
            pltpu.VMEM((total, width), HALF),
            pltpu.VMEM((width, CHUNK), FLOAT),
            pltpu.SemaphoreType.DMA((len(slots),)),
        ],
        flops=2 * total * width * padded,
        moved=2 * (total + width) * (padded + width),
    )


def out_grad_kernel(count, units, *refs):
    slots, inner = refs[:count], refs[count]
    out, rows, total, sems = refs[count + 1 :]
    step = pl.program_id(0)
    chunk = inner.shape[1]
    per_expert = total.shape[0] // chunk
    experts = pl.num_programs(0) // per_expert
    copies = out.shape[0]

    @pl.when(step == 0)
    def _():
        fetch_rows(slots, rows, sems)

    part = step % per_expert
    total[pl.ds(pl.multiple_of(part * chunk, chunk), chunk)] = matmul(inner[...], rows[...], (0, 0))

    def split(first, size, row):
        for i in range(copies):
            out[i, row : row + size] = total[first + i * size : first + (i + 1) * size].astype(HALF)

    for e in range(experts):

        @pl.when(step == (e + 1) * per_expert - 1)
        def _():
            split(0, units // copies, e * (units // copies))
            if e == 0:
                split(units, (total.shape[0] - units) // copies, experts * (units // copies))


def out_grad(units, experts, copies, slots, inner, *deps):
    length, width = slots[0].shape
    total, padded = inner.shape
    share = padded // experts - units
    shape = (copies, (experts * units + share) // copies, width)
    return launch(
        functools.partial(out_grad_kernel, len(slots), units),
        [*slots, inner],
        [ANYWHERE] * len(slots) + [pl.BlockSpec((total, CHUNK), lambda f: (0, f))],
        whole_block(shape),
        jax.ShapeDtypeStruct(shape, HALF),
        "expert_out_grad",
        deps=deps,
        grid=(padded // CHUNK,),
        scratch=[
            pltpu.VMEM((total, width), HALF),
            pltpu.VMEM((padded // experts, width), FLOAT),
            pltpu.SemaphoreType.DMA((len(slots),)),
        ],
        flops=2 * total * width * padded,
        moved=2 * (total + width) * (padded + width),
    )


def scaled_rows(values):
    scale = lax.rsqrt(jnp.mean(values * values, axis=1, keepdims=True) + EPS)
    return values * scale, scale


def mix_kernel(returned, spare_out, weight, tokens, gain, hidden, attended, ffn_in):
    for head in range(returned.shape[0]):
        attended[:, head_slice(head)] = returned[head]
    attended[:, returned.shape[0] * HEAD_DIM :] = spare_out[...]
    hidden[...] = tokens[...].astype(FLOAT) + matmul(attended[...], weight[...], (1, 0))
    ffn_in[...] = (scaled_rows(hidden[...])[0] * gain[...]).astype(HALF)


def mix(returned, spare_out, weight, tokens, gain, *deps):
    return launch_whole(
        mix_kernel,
        [returned, spare_out, weight, tokens, gain],
        [(tokens.shape, FLOAT), (tokens.shape, HALF), (tokens.shape, HALF)],
        "mix",
        deps=deps,
        flops=2 * tokens.shape[0] * tokens.shape[1] ** 2,
    )


def norm_grad(grad_out, normed, scale, gain):
    scaled = grad_out * gain
    return scale * (scaled - normed * jnp.mean(scaled * normed, axis=1, keepdims=True))


def back_kernel(
    own, forward, backward, hidden, cotangent, gain, weight, hidden_grad, branch, out_grad, spare_grad, terms
):
    ffn_in_grad = own[...].astype(FLOAT) + forward[...].astype(FLOAT) + backward[...].astype(FLOAT)
    normed, scale = scaled_rows(hidden[...])
    terms[...] = (ffn_in_grad * normed).astype(HALF)
    hidden_grad[...] = cotangent[...].astype(FLOAT) + norm_grad(ffn_in_grad, normed, scale, gain[...])
    branch[...] = hidden_grad[...].astype(HALF)
    attended_grad = matmul(branch[...], weight[...], (1, 1)).astype(HALF)
    for head in range(out_grad.shape[0]):
        out_grad[head] = attended_grad[:, head_slice(head)]
    spare_grad[...] = attended_grad[:, out_grad.shape[0] * HEAD_DIM :]


def back(arrived, hidden, cotangent, gain, weight, heads, *deps):
    length, width = hidden.shape
    shapes = [
        ((length, width), FLOAT),
        ((length, width), HALF),
        ((heads, length, HEAD_DIM), HALF),
        ((length, width - heads * HEAD_DIM), HALF),
        ((length, width), HALF),
    ]
    return launch_whole(
        back_kernel,
        [*arrived, hidden, cotangent, gain, weight],
        shapes,
        "back",
        deps=deps,
        flops=2 * length * width**2,
    )


def dense_wgrad(attended, branch, terms, gate_share, up_share, out):
    width = attended.shape[1]
    ones = jnp.ones((terms.shape[0], HEAD_DIM), HALF)
    out[:, :width] = matmul(attended[...], branch[...], (0, 0)).astype(HALF)
    out[:, width : width + HEAD_DIM] = matmul(terms[...], ones, (0, 0)).astype(HALF)
    column = width + HEAD_DIM
    for share in (gate_share, up_share):
        out[:, column : column + share.shape[1]] = share[...].astype(HALF)
        column += share.shape[1]


def tokens_grad_kernel(own, forward, backward, spare_grad, weight, tokens, gain, hidden_grad, out):
    attn_in_grad = (
        own[...].astype(FLOAT)
        + forward[...].astype(FLOAT)
        + backward[...].astype(FLOAT)
        + matmul(spare_grad[...], weight[...], (1, 1))
    )
    normed, scale = scaled_rows(tokens[...].astype(FLOAT))
    out[...] = hidden_grad[...] + norm_grad(attn_in_grad, normed, scale, gain[...])


def input_grad(arrived, spare_grad, weight, tokens, gain, hidden_grad, *deps):
    length, width = tokens.shape
    return launch_whole(
        tokens_grad_kernel,
        [*arrived, spare_grad, weight, tokens, gain, hidden_grad],
        [((length, width), FLOAT)],
        "tokens_grad",
        deps=deps,
        flops=2 * length * width * weight.shape[1],
    )[0]


def turn(values, cosine, sine):
    return values * cosine + pltpu.roll(values, HEAD_DIM // 2, 1) * sine


def head_slice(index):
    return slice(index * HEAD_DIM, (index + 1) * HEAD_DIM)


def start_all(copies):
    for copy in copies:
        copy.start()


def wait_all(copies):
    for copy in copies:
        copy.wait()


def pack_heads_kernel(spare, place_ref, query, key, value, out, sems):
    width = query.shape[1]
    own = pl.ds(pl.multiple_of(place_ref[0] * HEAD_DIM, HEAD_DIM), HEAD_DIM)
    rest = pl.ds(width - spare * HEAD_DIM, spare * HEAD_DIM)
    pieces = [
        (query, own, 1),
        (key, own, 1),
        (key, rest, spare),
        (value, own, 1),
        (value, rest, spare),
        (query, rest, spare),
    ]
    copies, tile = [], 0
    for i, (source, columns, tiles) in enumerate(pieces):
        target = out.at[:, pl.ds(tile * HEAD_DIM, tiles * HEAD_DIM)]
        copies.append(pltpu.make_async_copy(source.at[:, columns], target, sems.at[i]))
        tile += tiles
    start_all(copies)
    wait_all(copies)


def pack_heads(place, spare, query, key, value):
    width = query.shape[0]
    columns = (3 + 3 * spare) * HEAD_DIM
    return launch(
        functools.partial(pack_heads_kernel, spare),
        [query, key, value],
        [ANYWHERE] * 3,
        whole_block((width, columns)),
        jax.ShapeDtypeStruct((width, columns), HALF),
        "pack_heads",
        prefetch=[place],
        scratch=[pltpu.SemaphoreType.DMA((6,))],
        moved=4 * width * columns,
    )


def project_kernel(count, turned, tiles, chained, block_ref, *refs):
    xs, (gain, weight) = refs[:count], refs[count : count + 2]
    tables = refs[count + 2 : 3 * count + 2]
    outs = refs[3 * count + (3 if chained else 2) :]
    packed, normed = outs[0], outs[1 : 1 + count]
    step = pl.program_id(0)
    for i in range(count):

        @pl.when(step == i)
        def _():
            cosine, sine = tables[2 * i][0], tables[2 * i + 1][0]
            normed[i][...] = (scaled_rows(xs[i][...].astype(FLOAT))[0] * gain[...]).astype(HALF)
            lin = matmul(normed[i][...], weight[...], (1, 0))
            for tile in range(weight.shape[1] // HEAD_DIM):
                part = lin[:, head_slice(tile)]
                if tile < turned or tile >= tiles:
                    part = turn(part, cosine, sine)
                if tile < tiles:
                    packed[0, :, head_slice(tile)] = part.astype(HALF)
                else:
                    outs[1 + count][:, head_slice(tile - tiles)] = part.astype(HALF)


def project(blocks, slots, xs, gain, weight, cosine, sine, turned, tiles, packed, deps):
    count = len(slots)
    length, width = xs[0].shape
    chained = packed is not None
    extra = 0 if chained else weight.shape[1] - tiles * HEAD_DIM
    columns = tiles * HEAD_DIM + extra
    packed_shape = cosine.shape[:2] + (tiles * HEAD_DIM,)

    def place(i, b):
        block = b[slots[0]]
        for step in range(1, count):
            block = jnp.where(i == step, b[slots[step]], block)
        return block, 0, 0

    def table(slot):
        return pl.BlockSpec((1, length, HEAD_DIM), lambda i, b: (b[slot], 0, 0))

    out_specs = [pl.BlockSpec((1,) + packed_shape[1:], place)] + [whole_block(xs[0].shape)] * count
    out_shape = [jax.ShapeDtypeStruct(packed_shape, HALF)]
    out_shape += [jax.ShapeDtypeStruct(xs[0].shape, HALF)] * count
    if extra:
        out_specs.append(whole_block((length, extra)))
        out_shape.append(jax.ShapeDtypeStruct((length, extra), HALF))
    return launch(
        functools.partial(project_kernel, count, turned, tiles, chained),
        [*xs, gain, weight] + [cosine, sine] * count + ([packed] if chained else []),
        [whole_block(x.shape) for x in xs]
        + [whole_block(gain.shape), whole_block((width, columns))]
        + [spec for slot in slots for spec in (table(slot), table(slot))]
        + ([ANYWHERE] if chained else []),
        out_specs,
        out_shape,
        "project",
        prefetch=[blocks],
        deps=deps,
        grid=(count,),
        aliases={3 * count + 3: 0} if chained else {},
        flops=2 * count * length * width * columns,
        moved=2 * (count * length * (width + columns) + width * columns),
    )


EXP_SCALE = HEAD_DIM**-0.5 * 1.4426950408889634


def masked_scores(query, keys, first):
    scores = matmul(query, keys, (1, 1)) * EXP_SCALE
    row = lax.broadcasted_iota(jnp.int32, scores.shape, 0)
    column = lax.broadcasted_iota(jnp.int32, scores.shape, 1)
    return jnp.where(column <= row + first, scores, -1e30)


def attend(query, keys, values, first):
    scores = masked_scores(query, keys, first)
    peak = jnp.max(scores, axis=1, keepdims=True)
    shifted = jnp.exp2(scores - peak)
    total = jnp.sum(shifted, axis=1, keepdims=True)
    out = matmul(shifted.astype(HALF), values, (1, 0)) / total
    level = jnp.broadcast_to(peak + jnp.log2(total), (query.shape[0], HEAD_DIM))
    return out.astype(HALF), level


def packed_rows(packed, columns, blocks):
    return packed[:blocks, :, columns].reshape(blocks * packed.shape[1], HEAD_DIM)


def attention_kernel(spare, packed, out, level):
    for block in range(packed.shape[0]):
        out[block], level[block] = attend(
            packed[block, :, head_slice(0)],
            packed_rows(packed, head_slice(1), block + 1),
            packed_rows(packed, head_slice(2 + spare), block + 1),
            block * packed.shape[1],
        )


def attention(spare, packed, *deps):
    count, length, columns = packed.shape
    area = count * (count + 1) // 2 * length * length
    shape = (count, length, HEAD_DIM)
    return launch_whole(
        functools.partial(attention_kernel, spare),
        [packed],
        [(shape, HALF), (shape, FLOAT)],
        "attention",
        deps=deps,
        flops=8 * area * HEAD_DIM,
    )


def spare_attention_kernel(spare, place_ref, packed, queries, out, level):
    count, length = packed.shape[:2]
    for head in range(spare):
        out[:, head_slice(head)], level[head] = attend(
            queries[:, head_slice(head)],
            packed_rows(packed, head_slice(2 + head), count),
            packed_rows(packed, head_slice(3 + spare + head), count),
            place_ref[0] * length,
        )


def spare_attention(place, packed, queries, *deps):
    count, length, columns = packed.shape
    spare = queries.shape[1] // HEAD_DIM
    area = spare * count * length * length
    level_shape = (spare, length, HEAD_DIM)
    return launch_whole(
        functools.partial(spare_attention_kernel, spare),
        [packed, queries],
        [(queries.shape, HALF), (level_shape, FLOAT)],
        "spare_attention",
        prefetch=[place],
        deps=deps,
        flops=8 * area * HEAD_DIM,
    )


def attend_back(query, keys, values, first, level, out, out_grad):
    scores = masked_scores(query, keys, first)
    probs = jnp.exp2(scores - level[:, :1])
    prob_grad = matmul(out_grad, values, (1, 1))
    shared = jnp.sum(out_grad.astype(FLOAT) * out.astype(FLOAT), axis=1, keepdims=True)
    score_grad = (probs * (prob_grad - shared)).astype(HALF)
    value_grad = matmul(probs.astype(HALF), out_grad, (0, 0))
    query_grad = matmul(score_grad, keys, (1, 0)) * HEAD_DIM**-0.5
    key_grad = matmul(score_grad, query, (0, 0)) * HEAD_DIM**-0.5
    return query_grad, key_grad, value_grad


def attention_back_kernel(
    spare, blocks_ref, packed, out, level, out_grad, cosine, sine, spare_back, weight, grad, *rest
):
    parts, (key_sum, value_sum) = rest[:-2], rest[-2:]
    count, length = packed.shape[:2]
    key_sum[...] = jnp.zeros_like(key_sum)
    value_sum[...] = jnp.zeros_like(value_sum)
    for block in range(count):
        query_grad, key_grad, value_grad = attend_back(
            packed[block, :, head_slice(0)],
            packed_rows(packed, head_slice(1), block + 1),
            packed_rows(packed, head_slice(2 + spare), block + 1),
            block * length,
            level[block],
            out[block],
            out_grad[block],
        )
        grad[block, :, head_slice(0)] = turn(query_grad, cosine[block], -sine[block]).astype(HALF)
        seen = (block + 1) * length
        key_sum[:seen] += key_grad
        value_sum[:seen] += value_grad
    for block in range(count):
        rows = slice(block * length, (block + 1) * length)
        grad[block, :, head_slice(1)] = turn(key_sum[rows], cosine[block], -sine[block]).astype(HALF)
        grad[block, :, head_slice(2 + spare)] = value_sum[rows].astype(HALF)
        for head in range(spare):
            grad[block, :, head_slice(2 + head)] = spare_back[block, :, head_slice(head)]
            grad[block, :, head_slice(3 + spare + head)] = spare_back[block, :, head_slice(spare + head)]
    for slot in range(count):
        parts[slot][...] = matmul(grad[blocks_ref[slot]], weight[...], (1, 1)).astype(HALF)


def attention_back(blocks, packed, out, level, out_grad, cosine, sine, spare_back, weight, through, *deps):
    count, length, columns = packed.shape
    width = weight.shape[0]
    spare = spare_back.shape[2] // (2 * HEAD_DIM)
    area = count * (count + 1) // 2 * length * length
    operands = (packed, out, level, out_grad, cosine, sine, spare_back)
    shapes = [packed.shape] + [(length, width)] * count
    return launch(
        functools.partial(attention_back_kernel, spare),
        [*operands, weight],
        [whole_block(array.shape) for array in operands] + [whole_block((width, columns))],
        [whole_block(shape) for shape in shapes],
        [jax.ShapeDtypeStruct(shape, HALF) for shape in shapes],
        "attention_back",
        prefetch=[blocks],
        deps=deps,
        through=through,
        scratch=[pltpu.VMEM((count * length, HEAD_DIM), FLOAT)] * 2,
        flops=20 * area * HEAD_DIM + 2 * count * length * width * columns,
        moved=8 * count * length * columns + 2 * (count * length + columns) * width,
    )


def spare_back_kernel(spare, place_ref, other_ref, packed, queries, out, level, out_grad, cosine, sine, *refs):
    dense, halves, (grad, query_out, dense_out, half_sum) = refs[:5], refs[5:7], refs[7:]
    half_sum[...] = (
        (halves[0][...].astype(FLOAT) + halves[1][...].astype(FLOAT)).reshape(half_sum.shape).astype(HALF)
    )
    count, length = packed.shape[:2]
    place = place_ref[0]
    dense_wgrad(*dense, dense_out)
    for head in range(spare):
        query_grad, key_grad, value_grad = attend_back(
            queries[:, head_slice(head)],
            packed_rows(packed, head_slice(2 + head), count),
            packed_rows(packed, head_slice(3 + spare + head), count),
            place * length,
            level[head],
            out[:, head_slice(head)],
            out_grad[:, head_slice(head)],
        )
        query_out[:, head_slice(head)] = turn(query_grad, cosine[place], -sine[place]).astype(HALF)
        for block in range(count):
            rows = slice(block * length, (block + 1) * length)
            grad[block, :, head_slice(head)] = turn(
                key_grad[rows], cosine[block], -sine[block]
            ).astype(HALF)
            grad[block, :, head_slice(spare + head)] = value_grad[rows].astype(HALF)


def spare_attention_back(place, packed, queries, out, level, out_grad, cosine, sine, dense, halves, other):
    count, length, columns = packed.shape
    spare = queries.shape[1] // HEAD_DIM
    area = spare * count * length * length
    operands = (packed, queries, out, level, out_grad, cosine, sine, *dense)
    width = dense[0].shape[1]
    dense_columns = width + HEAD_DIM + dense[3].shape[1] + dense[4].shape[1]
    shapes = [(count, length, 2 * spare * HEAD_DIM), queries.shape, (width, dense_columns)]
    rest = halves[0].shape[1:]
    pairs = halves[0].shape[0] // 2
    half_block = pl.BlockSpec((pairs, 1) + rest, lambda i, p, o: (0, o[0]) + (0,) * len(rest))
    shapes.append((pairs,) + rest)
    return launch(
        functools.partial(spare_back_kernel, spare),
        [*operands, *(array.reshape((pairs, 2) + rest) for array in halves)],
        [whole_block(array.shape) for array in operands] + [half_block] * 2,
        [whole_block(shape) for shape in shapes],
        [jax.ShapeDtypeStruct(shape, HALF) for shape in shapes],
        "spare_back",
        prefetch=[place, other],
        flops=20 * area * HEAD_DIM,
    )


def attn_wgrad_kernel(count, blocks_ref, core_ref, *refs):
    slots, own, grad, spare_grad = refs[:count], refs[count], refs[count + 1], refs[count + 2]
    kept, sent, rows, total, sems = refs[count + 3 :]
    length = own.shape[0]
    copies = [
        pltpu.make_async_copy(
            slot, rows.at[pl.ds(pl.multiple_of(blocks_ref[i] * length, length), length)], sems.at[i]
        )
        for i, slot in enumerate(slots)
    ]
    for copy in copies:
        copy.start()
    columns = grad.shape[2]
    total[:, columns:] = matmul(own[...], spare_grad[...], (0, 0))
    for copy in copies:
        copy.wait()
    total[:, :columns] = matmul(rows[...], grad[...].reshape(count * length, columns), (0, 0))
    size = kept.shape[1]
    for j in range(kept.shape[0]):
        for target, parity in ((kept, core_ref[0]), (sent, 1 - core_ref[0])):
            start = pl.multiple_of((2 * j + parity) * size, 8)
            target[j] = total[pl.ds(start, size)].astype(HALF)


def attn_wgrad(blocks, core, copies, slots, grad, spare_grad, *deps):
    length, width = slots[0].shape
    count, _, columns = grad.shape
    wide = columns + spare_grad.shape[1]
    part = (copies // 2, width // copies, wide)
    return launch(
        functools.partial(attn_wgrad_kernel, count),
        [*slots, slots[0], grad, spare_grad],
        [ANYWHERE] * count
        + [whole_block(slots[0].shape), whole_block(grad.shape), whole_block(spare_grad.shape)],
        [whole_block(part)] * 2,
        [jax.ShapeDtypeStruct(part, HALF)] * 2,
        "attn_wgrad",
        prefetch=[blocks, core],
        deps=deps,
        scratch=[
            pltpu.VMEM((count * length, width), HALF),
            pltpu.VMEM((width, wide), FLOAT),
            pltpu.SemaphoreType.DMA((count,)),
        ],
        flops=2 * count * length * width * wide,
        moved=2 * (count * length + wide) * width,
    )


def on_device(
    tokens,
    routes,
    gates,
    attn_gain,
    query_weight,
    key_weight,
    value_weight,
    output_weight,
    ffn_gain,
    shared_gate,
    shared_up,
    shared_down,
    expert_gate,
    expert_up,
    expert_down,
    cotangent,
):
    length, width = tokens.shape
    hidden_units = expert_gate.shape[2]
    local_experts = expert_gate.shape[0]
    group = lax.axis_size("narrow")
    copies = lax.axis_size("wide")
    place = lax.axis_index("narrow")
    experts = group * local_experts
    seq_len = length * group
    own_heads = group * HEAD_DIM
    spare_heads = width // HEAD_DIM - group

    ring_place = jnp.where(place % 2 == 0, place // 2, group - 1 - place // 2)
    ring_slot = (ring_place + jnp.arange(group, dtype=jnp.int32)) % group
    slot_block = jnp.where(ring_slot < group // 2, 2 * ring_slot, 2 * (group - ring_slot) - 1)
    attn_gain_row = attn_gain.astype(FLOAT).reshape(1, width)
    ffn_gain_row = ffn_gain.astype(FLOAT).reshape(1, width)
    core = (lax.axis_index("wide") % 2).astype(jnp.int32).reshape(1)

    own_place = place.astype(jnp.int32).reshape(1)
    packed_weight = pack_heads(own_place, spare_heads, query_weight, key_weight, value_weight)
    spare_query_weight = query_weight[:, own_heads:]
    turned, tiles = 2 + spare_heads, 3 + 2 * spare_heads
    half = HEAD_DIM // 2
    angles = np.arange(seq_len)[:, None] * 10000.0 ** (-2.0 * np.arange(half) / HEAD_DIM)[None, :]
    turns = np.stack([np.cos(angles), -np.sin(angles), np.sin(angles)]).astype(np.float32)
    cosine = jnp.asarray(np.concatenate([turns[0], turns[0]], axis=1).reshape(group, length, HEAD_DIM))
    sine = jnp.asarray(np.concatenate([turns[1], turns[2]], axis=1).reshape(group, length, HEAD_DIM))

    share = hidden_units // (copies * group)
    per_expert = -(-(hidden_units + copies * share) // CHUNK) * CHUNK
    gap = per_expert - hidden_units
    spacing = gap // copies
    column = jnp.arange(gap, dtype=jnp.int32)
    unit = jnp.where(
        column % spacing < share,
        ((column // spacing) * group + place) * share + column % spacing,
        -1,
    )
    choice = (jnp.arange(hidden_units, dtype=jnp.int32)[:, None] == unit[None, :]).astype(HALF)

    heads = {"packed": None}
    attn_slots = [None] * group

    def project_slots(*slots, deps=()):
        result = project(
            slot_block,
            slots,
            [token_ring.slots[j] for j in slots],
            attn_gain_row,
            packed_weight,
            cosine,
            sine,
            turned,
            tiles,
            heads["packed"],
            deps,
        )
        heads["packed"] = result[0]
        for i, j in enumerate(slots):
            attn_slots[j] = result[1 + i]
        return result

    half_ring = group // 2
    token_ring = RingGather(tokens)
    token_ring.hop()
    spare_q = project_slots(0)[2]
    padded = local_experts * per_expert
    token_ring.hop(spare_q)
    expert_ids = jnp.arange(experts, dtype=jnp.int32)
    picked = routes[:, :, None] == expert_ids[None, None, :]
    token_gate = jnp.sum(jnp.where(picked, gates[:, :, None], 0.0), axis=1)
    own_gates = lax.all_to_all(
        token_gate.T.reshape(group, local_experts, length),
        "narrow",
        split_axis=0,
        concat_axis=0,
        tiled=True,
    )
    project_slots(1, group - 1)
    gate_weight = pack_experts(
        pack_in_kernel, hidden_units, (width, padded), choice, shared_gate, expert_gate, heads["packed"]
    )
    token_ring.hop(gate_weight)
    project_slots(2, group - 2)
    up_weight = pack_experts(
        pack_in_kernel, hidden_units, (width, padded), choice, shared_up, expert_up, heads["packed"]
    )
    last_hop = token_ring.hop(up_weight)
    project_slots(half_ring - 1, half_ring + 1)
    cot_ring = RingGather(cotangent, mirrored=True)
    cot_ring.hop(*last_hop)
    project_slots(half_ring)
    packed_heads = heads["packed"]
    own_out, level = attention(spare_heads, packed_heads)
    cot_ring.hop(packed_heads)
    returned = lax.all_to_all(own_out, "narrow", split_axis=0, concat_axis=0, tiled=True)
    spare_out, spare_level = spare_attention(own_place, packed_heads, spare_q, own_out)
    down_weight = pack_experts(
        pack_out_kernel, hidden_units, (padded, width), choice, shared_down, expert_down, spare_out, own_gates
    )
    own_gates = own_gates.transpose(0, 2, 1)
    cot_ring.hop(own_out)
    hidden, attended, ffn_in = mix(
        returned, spare_out, output_weight, tokens, ffn_gain_row
    )

    pairs = [(half_ring, half_ring + 1), (2, group - 2)]
    singles = [0, 1, group - 1, half_ring - 1]
    row_order = [slot for pair in pairs for slot in pair] + singles
    rows_state = {"kept": None}
    out_parts, row_parts = [None] * group, [None] * group

    def expert_batch(*batch, deps=()):
        result = expert_rows(
            hidden_units,
            batch,
            row_order.index(batch[0]) * length,
            seq_len,
            rows_state["kept"],
            slot_block,
            [ffn_ring.slots[j] for j in batch],
            [cot_ring.slots[j] for j in batch],
            own_gates,
            gate_weight,
            up_weight,
            down_weight,
            deps,
        )
        rows_state["kept"] = result[:3]
        for i, j in enumerate(batch):
            out_parts[j] = result[3 + i]
            row_parts[j] = result[3 + len(batch) + i]
        return tuple(result[3:])

    ffn_ring = RingGather(ffn_in)
    ffn_ring.hop()
    row_done = expert_batch(0)
    ffn_ring.hop(*row_done)
    cot_ring.hop(*row_done)
    ffn_ring.hop(*expert_batch(1))
    ffn_ring.hop(*expert_batch(group - 1))
    expert_batch(half_ring - 1)
    expert_batch(*pairs[0])
    row_sum, out_sum = RingSum(row_parts), RingSum(out_parts, mirrored=True)
    row_sum.hop()
    out_sum.hop()
    expert_batch(*pairs[1])
    gated_inner, gate_grad, up_grad = rows_state["kept"]
    ordered_cots = [cot_ring.slots[j] for j in row_order]
    ordered_rows = [ffn_ring.slots[j] for j in row_order]

    def over_wide(parts):
        return lax.psum_scatter(parts, "wide", scatter_dimension=0, tiled=False)

    row_added = add_rings([row_sum, out_sum])
    row_sum.hop()
    out_sum.hop()
    down_grad = out_grad(
        hidden_units, local_experts, copies, ordered_cots, gated_inner, *row_added
    )
    row_added = add_rings([row_sum, out_sum])
    down_total = over_wide(after(down_grad, *row_added))
    row_sum.hop(down_grad)
    out_sum.hop(down_grad)
    gate_wgrad, gate_share = in_grad(
        hidden_units, local_experts, copies, core, False, ordered_rows, gate_grad, *row_added
    )
    row_added = add_rings([row_sum, out_sum])
    gate_total = over_wide(after(gate_wgrad, *row_added))
    row_last = row_sum.hop(gate_wgrad)
    out_last = out_sum.hop(gate_wgrad)
    up_kept, up_sent, up_share = in_grad(
        hidden_units, local_experts, copies, core, True, ordered_rows, up_grad, *row_added
    )

    hidden_grad, branch_grad, out_grads, spare_out_grad, gain_terms = back(
        row_sum.last(), after(hidden, up_kept), cotangent, ffn_gain_row, output_weight, group, out_last[0], out_sum.backward
    )
    up_got = wide_first(after(up_sent, out_grads))
    own_out_grad = lax.all_to_all(out_grads, "narrow", split_axis=0, concat_axis=0, tiled=True)
    other = (1 - (lax.axis_index("wide") // 2) % 2).astype(jnp.int32).reshape(1)
    spare_back, spare_query_grad, dense_grad, up_sent_half = spare_attention_back(
        own_place,
        packed_heads,
        spare_q,
        spare_out,
        spare_level,
        spare_out_grad,
        cosine,
        sine,
        (attended, branch_grad, gain_terms, gate_share, up_share),
        (up_kept, up_got),
        other,
    )
    _, up_cross, up_terms = wide_rest(up_kept, up_got, sent=up_sent_half)

    head_grad, *attn_part, dense_grad = attention_back(
        slot_block, packed_heads, own_out, level, own_out_grad, cosine, sine, spare_back, packed_weight, [dense_grad]
    )
    dense_total = over_wide(dense_grad.reshape(copies, width // copies, dense_grad.shape[1]))

    def exchange(part):
        return lax.all_to_all(
            part.reshape(group, part.shape[0] // group, part.shape[1]),
            "narrow",
            split_axis=0,
            concat_axis=0,
            tiled=True,
        )

    spot = jnp.arange(group * gap, dtype=jnp.int32)
    spot_column = spot % gap
    spot_unit = jnp.where(
        spot_column % spacing < share,
        ((spot_column // spacing) * group + spot // gap) * share + spot_column % spacing,
        -1,
    )
    to_units = (spot_unit[:, None] == jnp.arange(hidden_units, dtype=jnp.int32)[None, :]).astype(HALF)
    to_units = to_units.reshape(group, gap, hidden_units)

    attn_sum = RingSum(attn_part)
    attn_sum.hop()
    attn_kept, attn_sent = attn_wgrad(
        slot_block, core, copies, attn_slots, after(head_grad, *attn_part), spare_query_grad
    )
    attn_added = attn_sum.add()
    attn_got = wide_first(after(attn_sent, *attn_added))
    attn_sum.hop()
    attn_sent_half, attn_cross, attn_terms = wide_rest(attn_kept, attn_got, *attn_added)
    attn_added = attn_sum.add(attn_sent_half)
    attn_sum.hop()
    expert_down_grad, shared_down_grad = widen_out(
        down_total, local_experts, hidden_units // copies, share, *attn_added
    )
    gate_total = widen(gate_total, *attn_added)
    attn_added = attn_sum.add(attn_cross, expert_down_grad, gate_total)
    attn_last = attn_sum.hop()
    up_total = sum_halves(*up_terms, FLOAT, attn_last[0])[0]
    first = exchange(after(dense_total, *attn_added))
    output_weight_grad, ffn_gain_columns, shared_gate_grad, shared_up_grad = finish_dense(
        first, to_units, width
    )
    second = exchange(
        sum_halves(
            *attn_terms, HALF, attn_last[0], attn_sum.backward, up_cross, output_weight_grad
        )[0]
    )
    tokens_grad = input_grad(
        attn_sum.last(), spare_query_grad, spare_query_weight, tokens, attn_gain_row, hidden_grad
    )
    mixed = (hidden + sum(part.astype(FLOAT) for part in out_sum.last())).astype(HALF)
    expert_gate_grad, expert_up_grad = gate_total, up_total

    ffn_gain_grad = ffn_gain_columns[:, 0]
    own_rows = width // (copies * group)
    first_row = (lax.axis_index("wide") * group + place) * own_rows

    def own_part(array):
        return lax.dynamic_slice_in_dim(array, first_row, own_rows, axis=0)

    query_weight_grad, key_weight_grad, value_weight_grad, attn_gain_columns = finish_attn(
        spare_heads, second, [own_part(query_weight), own_part(key_weight), own_part(value_weight)]
    )
    attn_gain_grad = attn_gain_columns[:, 0] / own_part(attn_gain).astype(FLOAT)
    return (
        mixed,
        tokens_grad,
        attn_gain_grad,
        query_weight_grad,
        key_weight_grad,
        value_weight_grad,
        output_weight_grad,
        ffn_gain_grad,
        shared_gate_grad,
        shared_up_grad,
        shared_down_grad,
        expert_gate_grad,
        expert_up_grad,
        expert_down_grad,
    )


def solution(mesh):
    rows = P(("wide", "narrow"), None)
    vector = P(("wide", "narrow"))
    held = P("narrow", None, None)
    in_specs = (rows, rows, rows) + (P(),) * 9 + (held, held, held, rows)
    out_specs = (rows, rows, vector) + (rows,) * 4 + (vector,) + (rows,) * 3 + (P("narrow", "wide", None),) * 3
    return jax.shard_map(
        on_device, mesh=mesh, in_specs=in_specs, out_specs=out_specs, check_vma=False
    )
```

```python
import functools

import jax
import jax.numpy as jnp
import numpy as np
from jax import lax
from jax.experimental import pallas as pl
from jax.experimental.pallas import tpu as pltpu
from jax.sharding import PartitionSpec as P

HEAD_DIM = 128
EPS = 1e-06
FLOAT = jnp.float32
HALF = jnp.bfloat16


def matmul(a, b, contract):
    return lax.dot_general(a, b, ((contract[:1], contract[1:]), ((), ())), preferred_element_type=FLOAT)


def ring_order(count):
    return list(range(0, count, 2)) + list(range(count - 1, 0, -2))


def ring_steps(count):
    order = ring_order(count)
    ahead = [(order[i], order[(i + 1) % count]) for i in range(count)]
    back = [(b, a) for a, b in ahead]
    return ahead, back


def after(value, *others):
    return lax.optimization_barrier((value, others))[0]


class RingGather:
    def __init__(self, block, mirrored=False):
        count = lax.axis_size("narrow")
        self.half = count // 2
        self.mirrored = mirrored
        self.step = 0
        self.slots = [block] + [None] * (count - 1)

    def hop(self, *others):
        count = len(self.slots)
        ahead, back = ring_steps(count)
        forward, backward = after((self.slots[-self.step], self.slots[self.step]), *others)
        self.step += 1
        arrived = []
        if self.step < self.half or not self.mirrored:
            arrived.append(lax.ppermute(forward, "narrow", ahead))
            self.slots[count - self.step] = arrived[-1]
        if self.step < self.half or self.mirrored:
            arrived.append(lax.ppermute(backward, "narrow", back))
            self.slots[self.step] = arrived[-1]
        return arrived


class RingSum:
    def __init__(self, parts, mirrored=False):
        self.mirrored = mirrored
        self.parts = parts
        self.half = len(parts) // 2
        self.step = 0
        self.forward, self.backward = self.part(self.half), self.part(self.half + 1)

    def part(self, offset):
        return self.parts[-offset if self.mirrored else offset]

    def hop(self, *others):
        ahead, back = ring_steps(len(self.parts))
        if self.mirrored:
            ahead, back = back, ahead
        self.step += 1
        if self.step == self.half:
            self.forward = lax.ppermute(after(self.forward, *others), "narrow", ahead)
            return [self.forward]
        forward, backward = after((self.forward, self.backward), *others)
        self.forward = lax.ppermute(forward, "narrow", ahead)
        self.backward = lax.ppermute(backward, "narrow", back)
        return [self.forward, self.backward]

    def add(self, *deps):
        return add_rings([self], *deps)

    def terms(self):
        arrived = [self.forward]
        own = [self.part(self.half - self.step)]
        if self.step < self.half - 1:
            arrived.append(self.backward)
            own.append(self.part(self.half + 1 + self.step))
        return arrived, own

    def last(self):
        return self.parts[0], self.forward, self.backward


def add_rings(rings, *deps):
    arrived, own = [], []
    for ring in rings:
        ring_arrived, ring_own = ring.terms()
        arrived += ring_arrived
        own += ring_own
    sums = launch_whole(
        functools.partial(add_kernel, len(own)),
        arrived + own,
        [(own[0].shape, HALF)] * len(own),
        "add_pairs",
        deps=deps,
    )
    left = list(sums)
    for ring in rings:
        ring.forward = left.pop(0)
        if ring.step < ring.half - 1:
            ring.backward = left.pop(0)
    return list(sums)


def add_kernel(count, *refs):
    for i in range(count):
        total = refs[i][...].astype(FLOAT) + refs[count + i][...].astype(FLOAT)
        refs[2 * count + i][...] = total.astype(HALF)


def wide_first(sent):
    count = lax.axis_size("wide")
    return lax.ppermute(sent, "wide", [(i, i ^ 1) for i in range(count)])


def wide_swap(sent, bit):
    count = lax.axis_size("wide")
    return lax.ppermute(sent, "wide", [(i, i ^ bit) for i in range(count)])


def sum_kernel(count, kind, place_ref, *refs):
    total = refs[0][...].astype(FLOAT)
    for ref in refs[1:count]:
        total += ref[...].reshape(total.shape).astype(FLOAT)
    refs[count][...] = total.reshape(refs[count].shape).astype(kind)


def sum_halves(halved, others, index, kind, *deps):
    rest = halved[0].shape[1:]
    pairs = halved[0].shape[0] // 2
    shape = (pairs,) + rest
    operands = [array.reshape((pairs, 2) + rest) for array in halved] + list(others)
    half_block = pl.BlockSpec((pairs, 1) + rest, lambda i, p: (0, p[0]) + (0,) * len(rest))
    return launch(
        functools.partial(sum_kernel, len(operands), kind),
        operands,
        [half_block] * len(halved) + [whole_block(shape)] * len(others),
        whole_block(shape),
        jax.ShapeDtypeStruct(shape, kind),
        "sum_halves",
        prefetch=[index],
        deps=deps,
        moved=sum(array.size for array in operands),
    )


def wide_rest(kept, got, *deps, sent=None):
    bit, others = 2, []
    halved = [kept, got]
    while True:
        mine = ((lax.axis_index("wide") // bit) % 2).astype(jnp.int32).reshape(1)
        if sent is None or bit > 2:
            sent = sum_halves(halved, others, 1 - mine, HALF, *deps)
        arrived = wide_swap(sent, bit)
        if 2 * bit == lax.axis_size("wide"):
            return sent, arrived, (halved, [arrived], mine)
        halved = [sum_halves(halved, [], mine, HALF), arrived]
        bit *= 2


def widen_out_kernel(rows, source, experts, shared):
    total = source[...].astype(FLOAT)
    for e in range(experts.shape[0]):
        experts[e] = total[e * rows : (e + 1) * rows]
    first = experts.shape[0] * rows
    shared[...] = total[first : first + shared.shape[0]]


def widen_out(source, experts, rows, share, *deps):
    width = source.shape[1]
    return launch_whole(
        functools.partial(widen_out_kernel, rows),
        [source],
        [((experts, rows, width), FLOAT), ((share, width), FLOAT)],
        "widen_out",
        deps=deps,
    )


def finish_dense_kernel(parts, to_units, out, gain, gate, up):
    group = parts.shape[0]
    width = out.shape[1]
    total = parts[0, :, : width + HEAD_DIM].astype(FLOAT)
    for g in range(1, group):
        total += parts[g, :, : width + HEAD_DIM].astype(FLOAT)
    out[...] = total[:, :width]
    gain[...] = total[:, width:]
    column = width
    gap = to_units.shape[1]
    for share in (gate, up):
        share[...] = sum(
            matmul(parts[g, :, column : column + gap], to_units[g], (1, 0)) for g in range(group)
        )
        column += gap


def finish_dense(parts, to_units, width):
    rows, units = parts.shape[1], to_units.shape[2]
    shapes = [(rows, width), (rows, HEAD_DIM), (rows, units), (rows, units)]
    return launch_whole(
        finish_dense_kernel, [parts, to_units], [(shape, FLOAT) for shape in shapes], "finish_dense"
    )


def finish_attn_kernel(spare, parts, *refs):
    weights, grads, gain = refs[:3], refs[3:6], refs[6]
    group = parts.shape[0]
    total = 0.0
    tiles = ((0, 3 + 2 * spare), (1, 2), (2 + spare, 3 + spare))
    for weight, grad, (own, first) in zip(weights, grads, tiles):
        for g in range(group):
            grad[:, head_slice(g)] = parts[g, :, head_slice(own)].astype(FLOAT)
        columns = slice(first * HEAD_DIM, (first + spare) * HEAD_DIM)
        grad[:, group * HEAD_DIM :] = sum(
            parts[g, :, columns].astype(FLOAT) for g in range(group)
        )
        total += jnp.sum(grad[...] * weight[...].astype(FLOAT), axis=1, keepdims=True)
    gain[...] = jnp.broadcast_to(total, gain.shape)


def finish_attn(spare, parts, weights):
    rows, width = weights[0].shape
    shapes = [(rows, width)] * 3 + [(rows, HEAD_DIM)]
    return launch_whole(
        functools.partial(finish_attn_kernel, spare),
        [parts, *weights],
        [(shape, FLOAT) for shape in shapes],
        "finish_attn",
    )


def widen_kernel(source, target):
    target[...] = source[...].astype(FLOAT)


def widen(array, *deps):
    return launch_whole(widen_kernel, [array], [(array.shape, FLOAT)], "widen", deps=deps)[0]


VMEM_LIMIT = 60 * 2**20
CHUNK = 512


def whole_block(shape):
    return pl.BlockSpec(shape, lambda *_: (0,) * len(shape))


ANYWHERE = pl.BlockSpec(memory_space=pl.ANY)


def launch(
    kernel, operands, in_specs, out_specs, out_shape, name, prefetch=(), deps=(), through=(), grid=(1,), scratch=(), aliases=None, flops=0, moved=0
):
    inputs = len(prefetch) + len(operands)
    idle = len(deps) + len(through)
    aliases = dict(aliases or {})
    if through:
        out_specs, out_shape = list(out_specs), list(out_shape)
        for i, array in enumerate(through):
            aliases[inputs + len(deps) + i] = len(out_shape)
            out_specs.append(ANYWHERE)
            out_shape.append(jax.ShapeDtypeStruct(array.shape, array.dtype))

    def body(*refs):
        results = refs[inputs + idle : len(refs) - len(scratch)]
        own = results[: len(results) - len(through)]
        kernel(*refs[:inputs], *own, *refs[len(refs) - len(scratch) :])

    return pl.pallas_call(
        body,
        grid_spec=pltpu.PrefetchScalarGridSpec(
            num_scalar_prefetch=len(prefetch),
            grid=grid,
            in_specs=list(in_specs) + [ANYWHERE] * idle,
            out_specs=out_specs,
            scratch_shapes=list(scratch),
        ),
        out_shape=out_shape,
        input_output_aliases=aliases,
        compiler_params=pltpu.CompilerParams(vmem_limit_bytes=VMEM_LIMIT),
        cost_estimate=pl.CostEstimate(flops=int(flops), bytes_accessed=int(moved), transcendentals=0),
        name=name,
    )(*prefetch, *operands, *deps, *through)


def launch_whole(kernel, operands, shapes, name, **options):
    moved = sum(array.size * array.dtype.itemsize for array in operands)
    return launch(
        kernel,
        operands,
        [whole_block(array.shape) for array in operands],
        [whole_block(shape) for shape, _ in shapes],
        [jax.ShapeDtypeStruct(shape, kind) for shape, kind in shapes],
        name,
        moved=moved,
        **options,
    )


def rows_kernel(slots, units, chained, blocks_ref, *refs):
    count = len(slots)
    xs, cs, gates = refs[:count], refs[count : 2 * count], refs[2 * count]
    gate_w, up_w, down_w = refs[2 * count + 1 : 2 * count + 4]
    outs = refs[2 * count + 4 + (3 if chained else 0) :]
    inner, gate_g, up_g = outs[:3]
    ys, ds = outs[3 : 3 + count], outs[3 + count : 3 + 2 * count]
    y_sum, d_sum, x_rows, c_rows = outs[3 + 2 * count :]
    step = pl.program_id(0)
    length = xs[0].shape[0]
    chunk = gate_w.shape[1]
    per_expert = pl.num_programs(0) // gates.shape[2]

    @pl.when(step == 0)
    def _():
        for i in range(count):
            x_rows[i * length : (i + 1) * length] = xs[i][...]
            c_rows[i * length : (i + 1) * length] = cs[i][...]
        y_sum[...] = jnp.zeros_like(y_sum)
        d_sum[...] = jnp.zeros_like(d_sum)

    x, c = x_rows[...], c_rows[...]
    expert = step // per_expert
    column = (step % per_expert) * chunk + lax.broadcasted_iota(
        jnp.int32, (count * length, chunk), 1
    )
    picked = []
    for slot in slots:
        gate = gates[blocks_ref[slot]]
        own = gate[:, 0:1]
        for e in range(1, gate.shape[1]):
            own = jnp.where(expert == e, gate[:, e : e + 1], own)
        picked.append(own)
    scale = jnp.where(column < units, jnp.concatenate(picked, axis=0), 1.0)
    gate_pre = matmul(x, gate_w[...], (1, 0))
    up_pre = matmul(x, up_w[...], (1, 0))
    inner_grad = matmul(c, down_w[...], (1, 1)) * scale
    sigma = 0.5 * jnp.tanh(0.5 * gate_pre) + 0.5
    active = gate_pre * sigma
    inner[...] = (active * up_pre * scale).astype(HALF)
    gate_g[...] = (inner_grad * up_pre * (sigma + active * (1.0 - sigma))).astype(HALF)
    up_g[...] = (inner_grad * active).astype(HALF)
    y_sum[...] += matmul(inner[...], down_w[...], (1, 0))
    d_sum[...] += matmul(gate_g[...], gate_w[...], (1, 1)) + matmul(up_g[...], up_w[...], (1, 1))

    @pl.when(step == pl.num_programs(0) - 1)
    def _():
        for i in range(count):
            ys[i][...] = y_sum[i * length : (i + 1) * length].astype(HALF)
            ds[i][...] = d_sum[i * length : (i + 1) * length].astype(HALF)


def expert_rows(units, slots, place, total, kept, blocks, xs, cs, gates, gate_w, up_w, down_w, deps):
    count = len(xs)
    length, width = xs[0].shape
    padded = gate_w.shape[1]
    rows = count * length
    column_block = pl.BlockSpec((width, CHUNK), lambda f, b: (0, f))
    row_block = pl.BlockSpec((CHUNK, width), lambda f, b: (f, 0))
    kept_block = pl.BlockSpec((rows, CHUNK), lambda f, b: (place // rows, f))
    chained = kept is not None
    first_kept = 1 + 2 * count + 4
    return launch(
        functools.partial(rows_kernel, slots, units, chained),
        [*xs, *cs, gates, gate_w, up_w, down_w, *(kept if chained else ())],
        [whole_block(xs[0].shape)] * (2 * count)
        + [whole_block(gates.shape), column_block, column_block, row_block]
        + [ANYWHERE] * (3 if chained else 0),
        [kept_block] * 3 + [whole_block(xs[0].shape)] * (2 * count),
        [jax.ShapeDtypeStruct((total, padded), HALF)] * 3
        + [jax.ShapeDtypeStruct(xs[0].shape, HALF)] * (2 * count),
        "expert_rows",
        prefetch=[blocks],
        deps=deps,
        grid=(padded // CHUNK,),
        scratch=[pltpu.VMEM((rows, width), FLOAT)] * 2 + [pltpu.VMEM((rows, width), HALF)] * 2,
        aliases={first_kept + i: i for i in range(3)} if chained else {},
        flops=12 * rows * width * padded,
        moved=6 * width * padded + 6 * rows * padded + 8 * rows * width,
    )


def pack_in_kernel(units, choice, shared, weights, out, sems):
    experts = weights.shape[0]
    per_expert = out.shape[1] // experts
    copies = [
        pltpu.make_async_copy(weights.at[e], out.at[:, pl.ds(e * per_expert, units)], sems.at[e])
        for e in range(experts)
    ]
    start_all(copies)
    for e in range(experts):
        gap = slice(e * per_expert + units, (e + 1) * per_expert)
        if e == 0:
            out[:, gap] = matmul(shared[...], choice[...], (1, 0)).astype(HALF)
        else:
            out[:, gap] = jnp.zeros((out.shape[0], per_expert - units), HALF)
    wait_all(copies)


def pack_out_kernel(units, choice, shared, weights, out, sems):
    experts = weights.shape[0]
    per_expert = out.shape[0] // experts
    copies = [
        pltpu.make_async_copy(weights.at[e], out.at[pl.ds(e * per_expert, units)], sems.at[e])
        for e in range(experts)
    ]
    start_all(copies)
    for e in range(experts):
        gap = slice(e * per_expert + units, (e + 1) * per_expert)
        if e == 0:
            out[gap] = matmul(choice[...], shared[...], (0, 0)).astype(HALF)
        else:
            out[gap] = jnp.zeros((per_expert - units, out.shape[1]), HALF)
    wait_all(copies)


def pack_experts(kernel, units, shape, choice, shared, weights, *deps):
    return launch(
        functools.partial(kernel, units),
        [choice, shared, weights],
        [whole_block(choice.shape), whole_block(shared.shape), ANYWHERE],
        whole_block(shape),
        jax.ShapeDtypeStruct(shape, HALF),
        "pack_experts",
        deps=deps,
        scratch=[pltpu.SemaphoreType.DMA((weights.shape[0],))],
        moved=4 * shape[0] * shape[1],
    )


def fetch_rows(slots, rows, sems):
    length = slots[0].shape[0]
    copies = [
        pltpu.make_async_copy(slot, rows.at[pl.ds(i * length, length)], sems.at[i])
        for i, slot in enumerate(slots)
    ]
    for copy in copies:
        copy.start()
    for copy in copies:
        copy.wait()


def in_grad_kernel(count, units, split, *refs):
    core_ref, slots, grad = refs[0], refs[1 : 1 + count], refs[1 + count]
    outs, (share, rows, total, sems) = refs[2 + count : -4], refs[-4:]
    step = pl.program_id(0)
    chunk = grad.shape[1]
    per_expert = -(-units // chunk)

    @pl.when(step == 0)
    def _():
        fetch_rows(slots, rows, sems)

    total[...] = matmul(rows[...], grad[...], (0, 0))
    size = outs[0].shape[2]

    def copy_rows(columns):
        own = slice(0, columns.stop - columns.start)
        if not split:
            for i in range(outs[0].shape[0]):
                outs[0][i, 0, :, columns] = total[i * size : (i + 1) * size, own].astype(HALF)
            return
        for j in range(outs[0].shape[0]):
            for target, parity in zip(outs, (core_ref[0], 1 - core_ref[0])):
                start = pl.multiple_of((2 * j + parity) * size, 8)
                target[j, 0, :, columns] = total[pl.ds(start, size), own].astype(HALF)

    for part in range(per_expert):

        @pl.when(step % per_expert == part)
        def _():
            copy_rows(slice(part * chunk, min((part + 1) * chunk, units)))

    @pl.when(step == per_expert - 1)
    def _():
        share[...] = total[:, units - (per_expert - 1) * chunk :]


def in_grad(units, experts, copies, core, split, slots, grad, *deps):
    length, width = slots[0].shape
    total, padded = grad.shape
    per_expert = padded // experts // CHUNK
    share = padded // experts - units
    parts = 2 if split else 1
    shape = (copies // parts, experts, width // copies, units)
    block = pl.BlockSpec((shape[0], 1) + shape[2:], lambda f, c: (0, f // per_expert, 0, 0))
    return launch(
        functools.partial(in_grad_kernel, len(slots), units, split),
        [*slots, grad],
        [ANYWHERE] * len(slots) + [pl.BlockSpec((total, CHUNK), lambda f, c: (0, f))],
        [block] * parts + [whole_block((width, share))],
        [jax.ShapeDtypeStruct(shape, HALF)] * parts + [jax.ShapeDtypeStruct((width, share), FLOAT)],
        "expert_in_grad",
        prefetch=[core],
        deps=deps,
        grid=(padded // CHUNK,),
        scratch=[
            pltpu.VMEM((total, width), HALF),
            pltpu.VMEM((width, CHUNK), FLOAT),
            pltpu.SemaphoreType.DMA((len(slots),)),
        ],
        flops=2 * total * width * padded,
        moved=2 * (total + width) * (padded + width),
    )


def out_grad_kernel(count, units, *refs):
    slots, inner = refs[:count], refs[count]
    out, rows, total, sems = refs[count + 1 :]
    step = pl.program_id(0)
    chunk = inner.shape[1]
    per_expert = total.shape[0] // chunk
    experts = pl.num_programs(0) // per_expert
    copies = out.shape[0]

    @pl.when(step == 0)
    def _():
        fetch_rows(slots, rows, sems)

    part = step % per_expert
    total[pl.ds(pl.multiple_of(part * chunk, chunk), chunk)] = matmul(inner[...], rows[...], (0, 0))

    def split(first, size, row):
        for i in range(copies):
            out[i, row : row + size] = total[first + i * size : first + (i + 1) * size].astype(HALF)

    for e in range(experts):

        @pl.when(step == (e + 1) * per_expert - 1)
        def _():
            split(0, units // copies, e * (units // copies))
            if e == 0:
                split(units, (total.shape[0] - units) // copies, experts * (units // copies))


def out_grad(units, experts, copies, slots, inner, *deps):
    length, width = slots[0].shape
    total, padded = inner.shape
    share = padded // experts - units
    shape = (copies, (experts * units + share) // copies, width)
    return launch(
        functools.partial(out_grad_kernel, len(slots), units),
        [*slots, inner],
        [ANYWHERE] * len(slots) + [pl.BlockSpec((total, CHUNK), lambda f: (0, f))],
        whole_block(shape),
        jax.ShapeDtypeStruct(shape, HALF),
        "expert_out_grad",
        deps=deps,
        grid=(padded // CHUNK,),
        scratch=[
            pltpu.VMEM((total, width), HALF),
            pltpu.VMEM((padded // experts, width), FLOAT),
            pltpu.SemaphoreType.DMA((len(slots),)),
        ],
        flops=2 * total * width * padded,
        moved=2 * (total + width) * (padded + width),
    )


def scaled_rows(values):
    scale = lax.rsqrt(jnp.mean(values * values, axis=1, keepdims=True) + EPS)
    return values * scale, scale


def mix_kernel(returned, spare_out, weight, tokens, gain, hidden, attended, ffn_in):
    for head in range(returned.shape[0]):
        attended[:, head_slice(head)] = returned[head]
    attended[:, returned.shape[0] * HEAD_DIM :] = spare_out[...]
    hidden[...] = tokens[...].astype(FLOAT) + matmul(attended[...], weight[...], (1, 0))
    ffn_in[...] = (scaled_rows(hidden[...])[0] * gain[...]).astype(HALF)


def mix(returned, spare_out, weight, tokens, gain, *deps):
    return launch_whole(
        mix_kernel,
        [returned, spare_out, weight, tokens, gain],
        [(tokens.shape, FLOAT), (tokens.shape, HALF), (tokens.shape, HALF)],
        "mix",
        deps=deps,
        flops=2 * tokens.shape[0] * tokens.shape[1] ** 2,
    )


def norm_grad(grad_out, normed, scale, gain):
    scaled = grad_out * gain
    return scale * (scaled - normed * jnp.mean(scaled * normed, axis=1, keepdims=True))


def back_kernel(
    own, forward, backward, hidden, cotangent, gain, weight, hidden_grad, branch, out_grad, spare_grad, terms
):
    ffn_in_grad = own[...].astype(FLOAT) + forward[...].astype(FLOAT) + backward[...].astype(FLOAT)
    normed, scale = scaled_rows(hidden[...])
    terms[...] = (ffn_in_grad * normed).astype(HALF)
    hidden_grad[...] = cotangent[...].astype(FLOAT) + norm_grad(ffn_in_grad, normed, scale, gain[...])
    branch[...] = hidden_grad[...].astype(HALF)
    attended_grad = matmul(branch[...], weight[...], (1, 1)).astype(HALF)
    for head in range(out_grad.shape[0]):
        out_grad[head] = attended_grad[:, head_slice(head)]
    spare_grad[...] = attended_grad[:, out_grad.shape[0] * HEAD_DIM :]


def back(arrived, hidden, cotangent, gain, weight, heads, *deps):
    length, width = hidden.shape
    shapes = [
        ((length, width), FLOAT),
        ((length, width), HALF),
        ((heads, length, HEAD_DIM), HALF),
        ((length, width - heads * HEAD_DIM), HALF),
        ((length, width), HALF),
    ]
    return launch_whole(
        back_kernel,
        [*arrived, hidden, cotangent, gain, weight],
        shapes,
        "back",
        deps=deps,
        flops=2 * length * width**2,
    )


def dense_wgrad(share, attended, branch, terms, gate_share, up_share, out):
    width = attended.shape[1]
    gap = gate_share.shape[1]
    out[:, :width] = matmul(attended[...], branch[...], (0, 0)).astype(HALF)
    gain = matmul(terms[...], jnp.ones((terms.shape[0], gap), HALF), (0, 0))
    column = lax.broadcasted_iota(jnp.int32, gain.shape, 1)
    out[:, width : width + gap] = jnp.where(column == share, gain, gate_share[...]).astype(HALF)
    out[:, width + gap :] = up_share[...].astype(HALF)


def tokens_grad_kernel(own, forward, backward, spare_grad, weight, tokens, gain, hidden_grad, out):
    attn_in_grad = (
        own[...].astype(FLOAT)
        + forward[...].astype(FLOAT)
        + backward[...].astype(FLOAT)
        + matmul(spare_grad[...], weight[...], (1, 1))
    )
    normed, scale = scaled_rows(tokens[...].astype(FLOAT))
    out[...] = hidden_grad[...] + norm_grad(attn_in_grad, normed, scale, gain[...])


def input_grad(arrived, spare_grad, weight, tokens, gain, hidden_grad, *deps):
    length, width = tokens.shape
    return launch_whole(
        tokens_grad_kernel,
        [*arrived, spare_grad, weight, tokens, gain, hidden_grad],
        [((length, width), FLOAT)],
        "tokens_grad",
        deps=deps,
        flops=2 * length * width * weight.shape[1],
    )[0]


def turn(values, cosine, sine):
    return values * cosine + pltpu.roll(values, HEAD_DIM // 2, 1) * sine


def head_slice(index):
    return slice(index * HEAD_DIM, (index + 1) * HEAD_DIM)


def start_all(copies):
    for copy in copies:
        copy.start()


def wait_all(copies):
    for copy in copies:
        copy.wait()


def pack_heads_kernel(spare, place_ref, query, key, value, out, sems):
    width = query.shape[1]
    own = pl.ds(pl.multiple_of(place_ref[0] * HEAD_DIM, HEAD_DIM), HEAD_DIM)
    rest = pl.ds(width - spare * HEAD_DIM, spare * HEAD_DIM)
    pieces = [
        (query, own, 1),
        (key, own, 1),
        (key, rest, spare),
        (value, own, 1),
        (value, rest, spare),
        (query, rest, spare),
    ]
    copies, tile = [], 0
    for i, (source, columns, tiles) in enumerate(pieces):
        target = out.at[:, pl.ds(tile * HEAD_DIM, tiles * HEAD_DIM)]
        copies.append(pltpu.make_async_copy(source.at[:, columns], target, sems.at[i]))
        tile += tiles
    start_all(copies)
    wait_all(copies)


def pack_heads(place, spare, query, key, value):
    width = query.shape[0]
    columns = (3 + 3 * spare) * HEAD_DIM
    return launch(
        functools.partial(pack_heads_kernel, spare),
        [query, key, value],
        [ANYWHERE] * 3,
        whole_block((width, columns)),
        jax.ShapeDtypeStruct((width, columns), HALF),
        "pack_heads",
        prefetch=[place],
        scratch=[pltpu.SemaphoreType.DMA((6,))],
        moved=4 * width * columns,
    )


def project_kernel(count, turned, tiles, chained, block_ref, *refs):
    xs, (gain, weight) = refs[:count], refs[count : count + 2]
    tables = refs[count + 2 : 3 * count + 2]
    outs = refs[3 * count + (3 if chained else 2) :]
    packed, normed = outs[0], outs[1 : 1 + count]
    step = pl.program_id(0)
    for i in range(count):

        @pl.when(step == i)
        def _():
            cosine, sine = tables[2 * i][0], tables[2 * i + 1][0]
            normed[i][...] = (scaled_rows(xs[i][...].astype(FLOAT))[0] * gain[...]).astype(HALF)
            lin = matmul(normed[i][...], weight[...], (1, 0))
            for tile in range(weight.shape[1] // HEAD_DIM):
                part = lin[:, head_slice(tile)]
                if tile < turned or tile >= tiles:
                    part = turn(part, cosine, sine)
                if tile < tiles:
                    packed[0, :, head_slice(tile)] = part.astype(HALF)
                else:
                    outs[1 + count][:, head_slice(tile - tiles)] = part.astype(HALF)


def project(blocks, slots, xs, gain, weight, cosine, sine, turned, tiles, packed, deps):
    count = len(slots)
    length, width = xs[0].shape
    chained = packed is not None
    extra = 0 if chained else weight.shape[1] - tiles * HEAD_DIM
    columns = tiles * HEAD_DIM + extra
    packed_shape = cosine.shape[:2] + (tiles * HEAD_DIM,)

    def place(i, b):
        block = b[slots[0]]
        for step in range(1, count):
            block = jnp.where(i == step, b[slots[step]], block)
        return block, 0, 0

    def table(slot):
        return pl.BlockSpec((1, length, HEAD_DIM), lambda i, b: (b[slot], 0, 0))

    out_specs = [pl.BlockSpec((1,) + packed_shape[1:], place)] + [whole_block(xs[0].shape)] * count
    out_shape = [jax.ShapeDtypeStruct(packed_shape, HALF)]
    out_shape += [jax.ShapeDtypeStruct(xs[0].shape, HALF)] * count
    if extra:
        out_specs.append(whole_block((length, extra)))
        out_shape.append(jax.ShapeDtypeStruct((length, extra), HALF))
    return launch(
        functools.partial(project_kernel, count, turned, tiles, chained),
        [*xs, gain, weight] + [cosine, sine] * count + ([packed] if chained else []),
        [whole_block(x.shape) for x in xs]
        + [whole_block(gain.shape), whole_block((width, columns))]
        + [spec for slot in slots for spec in (table(slot), table(slot))]
        + ([ANYWHERE] if chained else []),
        out_specs,
        out_shape,
        "project",
        prefetch=[blocks],
        deps=deps,
        grid=(count,),
        aliases={3 * count + 3: 0} if chained else {},
        flops=2 * count * length * width * columns,
        moved=2 * (count * length * (width + columns) + width * columns),
    )


EXP_SCALE = HEAD_DIM**-0.5 * 1.4426950408889634


def masked_scores(query, keys, first):
    scores = matmul(query, keys, (1, 1)) * EXP_SCALE
    row = lax.broadcasted_iota(jnp.int32, scores.shape, 0)
    column = lax.broadcasted_iota(jnp.int32, scores.shape, 1)
    return jnp.where(column <= row + first, scores, -1e30)


def attend(query, keys, values, first):
    scores = masked_scores(query, keys, first)
    peak = jnp.max(scores, axis=1, keepdims=True)
    shifted = jnp.exp2(scores - peak)
    total = jnp.sum(shifted, axis=1, keepdims=True)
    out = matmul(shifted.astype(HALF), values, (1, 0)) / total
    level = jnp.broadcast_to(peak + jnp.log2(total), (query.shape[0], HEAD_DIM))
    return out.astype(HALF), level


def packed_rows(packed, columns, blocks):
    return packed[:blocks, :, columns].reshape(blocks * packed.shape[1], HEAD_DIM)


def attention_kernel(spare, packed, out, level):
    for block in range(packed.shape[0]):
        out[block], level[block] = attend(
            packed[block, :, head_slice(0)],
            packed_rows(packed, head_slice(1), block + 1),
            packed_rows(packed, head_slice(2 + spare), block + 1),
            block * packed.shape[1],
        )


def attention(spare, packed, *deps):
    count, length, columns = packed.shape
    area = count * (count + 1) // 2 * length * length
    shape = (count, length, HEAD_DIM)
    return launch_whole(
        functools.partial(attention_kernel, spare),
        [packed],
        [(shape, HALF), (shape, FLOAT)],
        "attention",
        deps=deps,
        flops=8 * area * HEAD_DIM,
    )


def spare_attention_kernel(spare, place_ref, packed, queries, out, level):
    count, length = packed.shape[:2]
    for head in range(spare):
        out[:, head_slice(head)], level[head] = attend(
            queries[:, head_slice(head)],
            packed_rows(packed, head_slice(2 + head), count),
            packed_rows(packed, head_slice(3 + spare + head), count),
            place_ref[0] * length,
        )


def spare_attention(place, packed, queries, *deps):
    count, length, columns = packed.shape
    spare = queries.shape[1] // HEAD_DIM
    area = spare * count * length * length
    level_shape = (spare, length, HEAD_DIM)
    return launch_whole(
        functools.partial(spare_attention_kernel, spare),
        [packed, queries],
        [(queries.shape, HALF), (level_shape, FLOAT)],
        "spare_attention",
        prefetch=[place],
        deps=deps,
        flops=8 * area * HEAD_DIM,
    )


def attend_back(query, keys, values, first, level, out, out_grad):
    scores = masked_scores(query, keys, first)
    probs = jnp.exp2(scores - level[:, :1])
    prob_grad = matmul(out_grad, values, (1, 1))
    shared = jnp.sum(out_grad.astype(FLOAT) * out.astype(FLOAT), axis=1, keepdims=True)
    score_grad = (probs * (prob_grad - shared)).astype(HALF)
    value_grad = matmul(probs.astype(HALF), out_grad, (0, 0))
    query_grad = matmul(score_grad, keys, (1, 0)) * HEAD_DIM**-0.5
    key_grad = matmul(score_grad, query, (0, 0)) * HEAD_DIM**-0.5
    return query_grad, key_grad, value_grad


def attention_back_kernel(
    spare, blocks_ref, packed, out, level, out_grad, cosine, sine, spare_back, weight, grad, *rest
):
    parts, (key_sum, value_sum) = rest[:-2], rest[-2:]
    count, length = packed.shape[:2]
    key_sum[...] = jnp.zeros_like(key_sum)
    value_sum[...] = jnp.zeros_like(value_sum)
    for block in range(count):
        query_grad, key_grad, value_grad = attend_back(
            packed[block, :, head_slice(0)],
            packed_rows(packed, head_slice(1), block + 1),
            packed_rows(packed, head_slice(2 + spare), block + 1),
            block * length,
            level[block],
            out[block],
            out_grad[block],
        )
        grad[block, :, head_slice(0)] = turn(query_grad, cosine[block], -sine[block]).astype(HALF)
        seen = (block + 1) * length
        key_sum[:seen] += key_grad
        value_sum[:seen] += value_grad
    for block in range(count):
        rows = slice(block * length, (block + 1) * length)
        grad[block, :, head_slice(1)] = turn(key_sum[rows], cosine[block], -sine[block]).astype(HALF)
        grad[block, :, head_slice(2 + spare)] = value_sum[rows].astype(HALF)
        for head in range(spare):
            grad[block, :, head_slice(2 + head)] = spare_back[block, :, head_slice(head)]
            grad[block, :, head_slice(3 + spare + head)] = spare_back[block, :, head_slice(spare + head)]
    for slot in range(count):
        parts[slot][...] = matmul(grad[blocks_ref[slot]], weight[...], (1, 1)).astype(HALF)


def attention_back(blocks, packed, out, level, out_grad, cosine, sine, spare_back, weight, through, *deps):
    count, length, columns = packed.shape
    width = weight.shape[0]
    spare = spare_back.shape[2] // (2 * HEAD_DIM)
    area = count * (count + 1) // 2 * length * length
    operands = (packed, out, level, out_grad, cosine, sine, spare_back)
    shapes = [packed.shape] + [(length, width)] * count
    return launch(
        functools.partial(attention_back_kernel, spare),
        [*operands, weight],
        [whole_block(array.shape) for array in operands] + [whole_block((width, columns))],
        [whole_block(shape) for shape in shapes],
        [jax.ShapeDtypeStruct(shape, HALF) for shape in shapes],
        "attention_back",
        prefetch=[blocks],
        deps=deps,
        through=through,
        scratch=[pltpu.VMEM((count * length, HEAD_DIM), FLOAT)] * 2,
        flops=20 * area * HEAD_DIM + 2 * count * length * width * columns,
        moved=8 * count * length * columns + 2 * (count * length + columns) * width,
    )


def spare_back_kernel(spare, share, place_ref, other_ref, packed, queries, out, level, out_grad, cosine, sine, *refs):
    dense, halves, (grad, query_out, dense_out, half_sum) = refs[:5], refs[5:7], refs[7:]
    half_sum[...] = (
        (halves[0][...].astype(FLOAT) + halves[1][...].astype(FLOAT)).reshape(half_sum.shape).astype(HALF)
    )
    count, length = packed.shape[:2]
    place = place_ref[0]
    dense_wgrad(share, *dense, dense_out)
    for head in range(spare):
        query_grad, key_grad, value_grad = attend_back(
            queries[:, head_slice(head)],
            packed_rows(packed, head_slice(2 + head), count),
            packed_rows(packed, head_slice(3 + spare + head), count),
            place * length,
            level[head],
            out[:, head_slice(head)],
            out_grad[:, head_slice(head)],
        )
        query_out[:, head_slice(head)] = turn(query_grad, cosine[place], -sine[place]).astype(HALF)
        for block in range(count):
            rows = slice(block * length, (block + 1) * length)
            grad[block, :, head_slice(head)] = turn(
                key_grad[rows], cosine[block], -sine[block]
            ).astype(HALF)
            grad[block, :, head_slice(spare + head)] = value_grad[rows].astype(HALF)


def spare_attention_back(place, packed, queries, out, level, out_grad, cosine, sine, dense, share, halves, other):
    count, length, columns = packed.shape
    spare = queries.shape[1] // HEAD_DIM
    area = spare * count * length * length
    operands = (packed, queries, out, level, out_grad, cosine, sine, *dense)
    width = dense[0].shape[1]
    dense_columns = width + dense[3].shape[1] + dense[4].shape[1]
    shapes = [(count, length, 2 * spare * HEAD_DIM), queries.shape, (width, dense_columns)]
    rest = halves[0].shape[1:]
    pairs = halves[0].shape[0] // 2
    half_block = pl.BlockSpec((pairs, 1) + rest, lambda i, p, o: (0, o[0]) + (0,) * len(rest))
    shapes.append((pairs,) + rest)
    return launch(
        functools.partial(spare_back_kernel, spare, share),
        [*operands, *(array.reshape((pairs, 2) + rest) for array in halves)],
        [whole_block(array.shape) for array in operands] + [half_block] * 2,
        [whole_block(shape) for shape in shapes],
        [jax.ShapeDtypeStruct(shape, HALF) for shape in shapes],
        "spare_back",
        prefetch=[place, other],
        flops=20 * area * HEAD_DIM,
    )


def attn_wgrad_kernel(count, blocks_ref, core_ref, *refs):
    slots, own, grad, spare_grad = refs[:count], refs[count], refs[count + 1], refs[count + 2]
    kept, sent, rows, total, sems = refs[count + 3 :]
    length = own.shape[0]
    copies = [
        pltpu.make_async_copy(
            slot, rows.at[pl.ds(pl.multiple_of(blocks_ref[i] * length, length), length)], sems.at[i]
        )
        for i, slot in enumerate(slots)
    ]
    for copy in copies:
        copy.start()
    columns = grad.shape[2]
    total[:, columns:] = matmul(own[...], spare_grad[...], (0, 0))
    for copy in copies:
        copy.wait()
    total[:, :columns] = matmul(rows[...], grad[...].reshape(count * length, columns), (0, 0))
    size = kept.shape[1]
    for j in range(kept.shape[0]):
        for target, parity in ((kept, core_ref[0]), (sent, 1 - core_ref[0])):
            start = pl.multiple_of((2 * j + parity) * size, 8)
            target[j] = total[pl.ds(start, size)].astype(HALF)


def attn_wgrad(blocks, core, copies, slots, grad, spare_grad, *deps):
    length, width = slots[0].shape
    count, _, columns = grad.shape
    wide = columns + spare_grad.shape[1]
    part = (copies // 2, width // copies, wide)
    return launch(
        functools.partial(attn_wgrad_kernel, count),
        [*slots, slots[0], grad, spare_grad],
        [ANYWHERE] * count
        + [whole_block(slots[0].shape), whole_block(grad.shape), whole_block(spare_grad.shape)],
        [whole_block(part)] * 2,
        [jax.ShapeDtypeStruct(part, HALF)] * 2,
        "attn_wgrad",
        prefetch=[blocks, core],
        deps=deps,
        scratch=[
            pltpu.VMEM((count * length, width), HALF),
            pltpu.VMEM((width, wide), FLOAT),
            pltpu.SemaphoreType.DMA((count,)),
        ],
        flops=2 * count * length * width * wide,
        moved=2 * (count * length + wide) * width,
    )


def on_device(
    tokens,
    routes,
    gates,
    attn_gain,
    query_weight,
    key_weight,
    value_weight,
    output_weight,
    ffn_gain,
    shared_gate,
    shared_up,
    shared_down,
    expert_gate,
    expert_up,
    expert_down,
    cotangent,
):
    length, width = tokens.shape
    hidden_units = expert_gate.shape[2]
    local_experts = expert_gate.shape[0]
    group = lax.axis_size("narrow")
    copies = lax.axis_size("wide")
    place = lax.axis_index("narrow")
    experts = group * local_experts
    seq_len = length * group
    own_heads = group * HEAD_DIM
    spare_heads = width // HEAD_DIM - group

    ring_place = jnp.where(place % 2 == 0, place // 2, group - 1 - place // 2)
    ring_slot = (ring_place + jnp.arange(group, dtype=jnp.int32)) % group
    slot_block = jnp.where(ring_slot < group // 2, 2 * ring_slot, 2 * (group - ring_slot) - 1)
    attn_gain_row = attn_gain.astype(FLOAT).reshape(1, width)
    ffn_gain_row = ffn_gain.astype(FLOAT).reshape(1, width)
    core = (lax.axis_index("wide") % 2).astype(jnp.int32).reshape(1)

    own_place = place.astype(jnp.int32).reshape(1)
    packed_weight = pack_heads(own_place, spare_heads, query_weight, key_weight, value_weight)
    spare_query_weight = query_weight[:, own_heads:]
    turned, tiles = 2 + spare_heads, 3 + 2 * spare_heads
    half = HEAD_DIM // 2
    angles = np.arange(seq_len)[:, None] * 10000.0 ** (-2.0 * np.arange(half) / HEAD_DIM)[None, :]
    turns = np.stack([np.cos(angles), -np.sin(angles), np.sin(angles)]).astype(np.float32)
    cosine = jnp.asarray(np.concatenate([turns[0], turns[0]], axis=1).reshape(group, length, HEAD_DIM))
    sine = jnp.asarray(np.concatenate([turns[1], turns[2]], axis=1).reshape(group, length, HEAD_DIM))

    share = hidden_units // (copies * group)
    per_expert = -(-(hidden_units + copies * share) // CHUNK) * CHUNK
    gap = per_expert - hidden_units
    spacing = gap // copies
    column = jnp.arange(gap, dtype=jnp.int32)
    unit = jnp.where(
        column % spacing < share,
        ((column // spacing) * group + place) * share + column % spacing,
        -1,
    )
    choice = (jnp.arange(hidden_units, dtype=jnp.int32)[:, None] == unit[None, :]).astype(HALF)

    heads = {"packed": None}
    attn_slots = [None] * group

    def project_slots(*slots, deps=()):
        result = project(
            slot_block,
            slots,
            [token_ring.slots[j] for j in slots],
            attn_gain_row,
            packed_weight,
            cosine,
            sine,
            turned,
            tiles,
            heads["packed"],
            deps,
        )
        heads["packed"] = result[0]
        for i, j in enumerate(slots):
            attn_slots[j] = result[1 + i]
        return result

    half_ring = group // 2
    token_ring = RingGather(tokens)
    token_ring.hop()
    spare_q = project_slots(0)[2]
    padded = local_experts * per_expert
    token_ring.hop(spare_q)
    expert_ids = jnp.arange(experts, dtype=jnp.int32)
    picked = routes[:, :, None] == expert_ids[None, None, :]
    token_gate = jnp.sum(jnp.where(picked, gates[:, :, None], 0.0), axis=1)
    own_gates = lax.all_to_all(
        token_gate.T.reshape(group, local_experts, length),
        "narrow",
        split_axis=0,
        concat_axis=0,
        tiled=True,
    )
    project_slots(1, group - 1)
    gate_weight = pack_experts(
        pack_in_kernel, hidden_units, (width, padded), choice, shared_gate, expert_gate, heads["packed"]
    )
    token_ring.hop(gate_weight)
    project_slots(2, group - 2)
    up_weight = pack_experts(
        pack_in_kernel, hidden_units, (width, padded), choice, shared_up, expert_up, heads["packed"]
    )
    last_hop = token_ring.hop(up_weight)
    project_slots(half_ring - 1, half_ring + 1)
    cot_ring = RingGather(cotangent, mirrored=True)
    cot_ring.hop(*last_hop)
    project_slots(half_ring)
    packed_heads = heads["packed"]
    own_out, level = attention(spare_heads, packed_heads)
    cot_ring.hop(packed_heads)
    returned = lax.all_to_all(own_out, "narrow", split_axis=0, concat_axis=0, tiled=True)
    spare_out, spare_level = spare_attention(own_place, packed_heads, spare_q, own_out)
    down_weight = pack_experts(
        pack_out_kernel, hidden_units, (padded, width), choice, shared_down, expert_down, spare_out, own_gates
    )
    own_gates = own_gates.transpose(0, 2, 1)
    cot_ring.hop(own_out)
    hidden, attended, ffn_in = mix(
        returned, spare_out, output_weight, tokens, ffn_gain_row
    )

    pairs = [(half_ring, half_ring + 1), (2, group - 2)]
    singles = [0, 1, group - 1, half_ring - 1]
    row_order = [slot for pair in pairs for slot in pair] + singles
    rows_state = {"kept": None}
    out_parts, row_parts = [None] * group, [None] * group

    def expert_batch(*batch, deps=()):
        result = expert_rows(
            hidden_units,
            batch,
            row_order.index(batch[0]) * length,
            seq_len,
            rows_state["kept"],
            slot_block,
            [ffn_ring.slots[j] for j in batch],
            [cot_ring.slots[j] for j in batch],
            own_gates,
            gate_weight,
            up_weight,
            down_weight,
            deps,
        )
        rows_state["kept"] = result[:3]
        for i, j in enumerate(batch):
            out_parts[j] = result[3 + i]
            row_parts[j] = result[3 + len(batch) + i]
        return tuple(result[3:])

    ffn_ring = RingGather(ffn_in)
    ffn_ring.hop()
    row_done = expert_batch(0)
    ffn_ring.hop(*row_done)
    cot_ring.hop(*row_done)
    ffn_ring.hop(*expert_batch(1))
    ffn_ring.hop(*expert_batch(group - 1))
    expert_batch(half_ring - 1)
    expert_batch(*pairs[0])
    row_sum, out_sum = RingSum(row_parts), RingSum(out_parts, mirrored=True)
    row_sum.hop()
    out_sum.hop()
    expert_batch(*pairs[1])
    gated_inner, gate_grad, up_grad = rows_state["kept"]
    ordered_cots = [cot_ring.slots[j] for j in row_order]
    ordered_rows = [ffn_ring.slots[j] for j in row_order]

    def over_wide(parts):
        return lax.psum_scatter(parts, "wide", scatter_dimension=0, tiled=False)

    row_added = add_rings([row_sum, out_sum])
    row_sum.hop()
    out_sum.hop()
    down_grad = out_grad(
        hidden_units, local_experts, copies, ordered_cots, gated_inner, *row_added
    )
    row_added = add_rings([row_sum, out_sum])
    down_total = over_wide(after(down_grad, *row_added))
    row_sum.hop(down_grad)
    out_sum.hop(down_grad)
    gate_wgrad, gate_share = in_grad(
        hidden_units, local_experts, copies, core, False, ordered_rows, gate_grad, *row_added
    )
    row_added = add_rings([row_sum, out_sum])
    gate_total = over_wide(after(gate_wgrad, *row_added))
    row_last = row_sum.hop(gate_wgrad)
    out_last = out_sum.hop(gate_wgrad)
    up_kept, up_sent, up_share = in_grad(
        hidden_units, local_experts, copies, core, True, ordered_rows, up_grad, *row_added
    )

    hidden_grad, branch_grad, out_grads, spare_out_grad, gain_terms = back(
        row_sum.last(), after(hidden, up_kept), cotangent, ffn_gain_row, output_weight, group, out_last[0], out_sum.backward
    )
    up_got = wide_first(after(up_sent, out_grads))
    own_out_grad = lax.all_to_all(out_grads, "narrow", split_axis=0, concat_axis=0, tiled=True)
    other = (1 - (lax.axis_index("wide") // 2) % 2).astype(jnp.int32).reshape(1)
    spare_back, spare_query_grad, dense_grad, up_sent_half = spare_attention_back(
        own_place,
        packed_heads,
        spare_q,
        spare_out,
        spare_level,
        spare_out_grad,
        cosine,
        sine,
        (attended, branch_grad, gain_terms, gate_share, up_share),
        share,
        (up_kept, up_got),
        other,
    )
    _, up_cross, up_terms = wide_rest(up_kept, up_got, sent=up_sent_half)

    head_grad, *attn_part, dense_grad = attention_back(
        slot_block, packed_heads, own_out, level, own_out_grad, cosine, sine, spare_back, packed_weight, [dense_grad]
    )
    dense_total = over_wide(dense_grad.reshape(copies, width // copies, dense_grad.shape[1]))

    def exchange(part):
        return lax.all_to_all(
            part.reshape(group, part.shape[0] // group, part.shape[1]),
            "narrow",
            split_axis=0,
            concat_axis=0,
            tiled=True,
        )

    spot = jnp.arange(group * gap, dtype=jnp.int32)
    spot_column = spot % gap
    spot_unit = jnp.where(
        spot_column % spacing < share,
        ((spot_column // spacing) * group + spot // gap) * share + spot_column % spacing,
        -1,
    )
    to_units = (spot_unit[:, None] == jnp.arange(hidden_units, dtype=jnp.int32)[None, :]).astype(HALF)
    to_units = to_units.reshape(group, gap, hidden_units)

    attn_sum = RingSum(attn_part)
    attn_sum.hop()
    attn_kept, attn_sent = attn_wgrad(
        slot_block, core, copies, attn_slots, after(head_grad, *attn_part), spare_query_grad
    )
    attn_added = attn_sum.add()
    attn_got = wide_first(after(attn_sent, *attn_added))
    attn_sum.hop()
    attn_sent_half, attn_cross, attn_terms = wide_rest(attn_kept, attn_got, *attn_added)
    attn_added = attn_sum.add(attn_sent_half)
    attn_sum.hop()
    expert_down_grad, shared_down_grad = widen_out(
        down_total, local_experts, hidden_units // copies, share, *attn_added
    )
    gate_total = widen(gate_total, *attn_added)
    attn_added = attn_sum.add(attn_cross, expert_down_grad, gate_total)
    attn_last = attn_sum.hop()
    up_total = sum_halves(*up_terms, FLOAT, attn_last[0])[0]
    first = exchange(after(dense_total, *attn_added))
    output_weight_grad, ffn_gain_columns, shared_gate_grad, shared_up_grad = finish_dense(
        first, to_units, width
    )
    second = exchange(
        sum_halves(
            *attn_terms, HALF, attn_last[0], attn_sum.backward, up_cross, first
        )[0]
    )
    tokens_grad = input_grad(
        attn_sum.last(), spare_query_grad, spare_query_weight, tokens, attn_gain_row, hidden_grad
    )
    mixed = (hidden + sum(part.astype(FLOAT) for part in out_sum.last())).astype(HALF)
    expert_gate_grad, expert_up_grad = gate_total, up_total

    ffn_gain_grad = ffn_gain_columns[:, share]
    own_rows = width // (copies * group)
    first_row = (lax.axis_index("wide") * group + place) * own_rows

    def own_part(array):
        return lax.dynamic_slice_in_dim(array, first_row, own_rows, axis=0)

    query_weight_grad, key_weight_grad, value_weight_grad, attn_gain_columns = finish_attn(
        spare_heads, second, [own_part(query_weight), own_part(key_weight), own_part(value_weight)]
    )
    attn_gain_grad = attn_gain_columns[:, 0] / own_part(attn_gain).astype(FLOAT)
    return (
        mixed,
        tokens_grad,
        attn_gain_grad,
        query_weight_grad,
        key_weight_grad,
        value_weight_grad,
        output_weight_grad,
        ffn_gain_grad,
        shared_gate_grad,
        shared_up_grad,
        shared_down_grad,
        expert_gate_grad,
        expert_up_grad,
        expert_down_grad,
    )


def solution(mesh):
    rows = P(("wide", "narrow"), None)
    vector = P(("wide", "narrow"))
    held = P("narrow", None, None)
    in_specs = (rows, rows, rows) + (P(),) * 9 + (held, held, held, rows)
    out_specs = (rows, rows, vector) + (rows,) * 4 + (vector,) + (rows,) * 3 + (P("narrow", "wide", None),) * 3
    return jax.shard_map(
        on_device, mesh=mesh, in_specs=in_specs, out_specs=out_specs, check_vma=False
    )
```
